32 devices in a mesh: seq: 8 (over y, x, core), head: 4 (over z).
Axes of the slice: x: 2, y: 2, z: 4, core: 2. Of those that a mesh axis runs over, the one named last changes fastest.
Arguments:
- tokens: bfloat16 [32768, 768], P(('seq', 'head')), may hold values from -6 to 6
- lengths: int32 [8, 32], P('seq'), may hold values from 1 to 512, 4096 in all within a row
- cotangent: bfloat16 [32768, 768], P(('seq', 'head')), may hold values from -12 to 12
- w_query: bfloat16 [768, 768], replicated, may hold values from -0.21875 to 0.21875
- w_key: bfloat16 [768, 768], replicated, may hold values from -0.21875 to 0.21875
- w_value: bfloat16 [768, 768], replicated, may hold values from -0.21875 to 0.21875
- w_output: bfloat16 [768, 768], replicated, may hold values from -1.25 to 1.25
- vera_down: bfloat16 [768, 1024], replicated, may hold values from -0.21875 to 0.21875
- vera_up: bfloat16 [1024, 768], replicated, may hold values from -0.1875 to 0.1875
- query_scale: float32 [1024], replicated, may hold values from 0.5 to 1.5
- query_bias: float32 [768], replicated, may hold values from -4 to 4
- value_scale: float32 [1024], replicated, may hold values from 0.5 to 1.5
- value_bias: float32 [768], replicated, may hold values from -4 to 4
- hidden_in: bfloat16 [768, 3072], P(None, ('seq', 'head')), may hold values from -0.21875 to 0.21875
- hidden_out: bfloat16 [768, 3072], P(None, ('seq', 'head')), may hold values from -0.109375 to 0.109375
Outputs:
- layer_output: bfloat16 [32768, 768], P(('seq', 'head'))
- token_grad: bfloat16 [32768, 768], P(('seq', 'head'))
- query_scale_grad: float32 [1024], replicated
- query_bias_grad: float32 [768], replicated
- value_scale_grad: float32 [1024], replicated
- value_bias_grad: float32 [768], replicated
The draws below stay inside these ranges and needn't reach their ends.
Inputs may be any that keep to these rules, and one draw needn't show every extreme that they name: `lengths`: each row sums to 4096, and its longest sequence has exactly 512 tokens.
All inputs are finite; a program needn't handle non-finite values.
Results may differ from the reference program's by a relative error of at most 0.015.
Values may be sent and summed in bfloat16 or wider, within the bound.
A program may use at most 192 MiB of HBM per device.

```python
import math
import jax
import jax.numpy as jnp
import numpy as np
from jax import lax

D = 768
HEAD_DIM = 64
FF = 3072
R = 1024
TOK_DEV = 1024
SEQ_MOST = 512
SEQS = 32
TOKENS = 32768
N_SEQ = 8
N_HEAD = 4


def draw_cotangent(key, part):
    key = jax.random.fold_in(key, 7)
    positions = jnp.arange(TOKENS, dtype=jnp.float32)[:, None] / (TOKENS - 1)
    ramp = 1.0 + 2.0 * positions
    base = jax.random.truncated_normal(key, -4.0, 4.0, (TOKENS, D), jnp.float32)
    values = base * ramp
    return values.astype(jnp.bfloat16)


def block_levels(key, extent, pieces, least, high):
    level, own = 1.0, jax.random.fold_in(key, 6)
    for position, shards_of in pieces:
        draws = jnp.exp(jax.random.uniform(jax.random.fold_in(own, position), (shards_of,), jnp.float32, least / len(pieces), high / len(pieces)))
        level = level * jnp.repeat(draws, extent[position] // shards_of).reshape([-1 if axis == position else 1 for axis in range(len(extent))])
    return level


def length_profile(amount, total, reach, slope):
    portions = [(1 << 20) // math.isqrt(standing ** slope) + 1 for standing in range(2, amount + 1)]
    surplus, counts = total - reach - (amount - 1), [1] * (amount - 1)
    while surplus > 0:
        free = [i for i in range(amount - 1) if counts[i] < reach]
        pool, left = sum([portions[i] for i in free]), surplus
        for i in free:
            addition = min(reach - counts[i], max(1, left * portions[i] // pool), surplus)
            counts[i] = counts[i] + addition
            surplus = surplus - addition
    return np.array([reach] + counts)


def ragged(rng, number_of, total, limit, slope):
    if number_of == 2:
        one = jax.random.randint(rng, (), max(1, total - limit), min(limit, total - 1) + 1)
        return jnp.stack([one, total - one])
    tallies = jnp.asarray(length_profile(number_of, total, limit, slope), jnp.int32)
    pairs = (number_of - 1) // 2
    source_of, sink = tallies[1:1 + 2 * pairs:2], tallies[2:2 + 2 * pairs:2]
    margin = jnp.minimum(source_of - 1, limit - sink)
    passed = jax.random.randint(jax.random.fold_in(rng, 1), (pairs,), 0, 1 << 20) % (margin + 1)
    tallies = tallies.at[1:1 + 2 * pairs:2].set(source_of - passed).at[2:2 + 2 * pairs:2].set(sink + passed)
    return tallies[jax.random.permutation(jax.random.fold_in(rng, 2), number_of)]


def centred(own_key, extent, deviation, most, pieces=(), kind=jnp.bfloat16):
    values = deviation * jax.random.normal(own_key, extent, jnp.float32)
    if pieces:
        values = values * block_levels(own_key, extent, pieces, -0.22, 0.18)
    return jnp.clip(values, -most, most).astype(kind)


def setup_inputs(seed: int = 0) -> dict:
    seeds = jax.random.split(jax.random.key(seed), 16)
    tokens = centred(seeds[0], (TOKENS, D), 1.0, 6.0, ((0, 32),))
    lengths = jax.vmap(lambda own: ragged(own, SEQS, N_HEAD * TOK_DEV, SEQ_MOST, 2))(jax.random.split(seeds[1], N_SEQ)).reshape((N_SEQ, SEQS)).astype(jnp.int32)
    cotangent = draw_cotangent(jax.random.fold_in(seeds[15], 71), 0)
    w_query = centred(seeds[3], (D, D), D ** -0.5, 0.21875)
    w_key = centred(seeds[4], (D, D), D ** -0.5, 0.21875)
    w_value = centred(seeds[5], (D, D), D ** -0.5, 0.21875)
    w_output = centred(seeds[6], (D, D), (D // 32) ** -0.5, 1.25)
    vera_down = centred(seeds[7], (D, R), D ** -0.5, 0.21875)
    vera_up = centred(seeds[8], (R, D), R ** -0.5, 0.1875)
    query_scale = jnp.clip(jax.random.uniform(seeds[9], (R,), jnp.float32, 0.5, 1.5), 0.5, 1.5)
    query_bias = centred(seeds[10], (D,), 0.7, 4.0, (), jnp.float32)
    value_scale = jnp.clip(jax.random.uniform(seeds[11], (R,), jnp.float32, 0.5, 1.5), 0.5, 1.5)
    value_bias = centred(seeds[12], (D,), 0.7, 4.0, (), jnp.float32)
    hidden_in = centred(seeds[13], (D, FF), D ** -0.5, 0.21875, ((1, 32),))
    hidden_out = centred(seeds[14], (D, FF), FF ** -0.5, 0.109375, ((1, 32),))
    return {"tokens": tokens, "lengths": lengths, "cotangent": cotangent, "w_query": w_query, "w_key": w_key, "w_value": w_value, "w_output": w_output, "vera_down": vera_down, "vera_up": vera_up, "query_scale": query_scale, "query_bias": query_bias, "value_scale": value_scale, "value_bias": value_bias, "hidden_in": hidden_in, "hidden_out": hidden_out}


HIGHEST = lax.Precision.HIGHEST
EPSILON = 1e-05
MASKED = -1000000000.0

@jax.custom_vjp
def low(v):
    return lax.optimization_barrier(v.astype(jnp.bfloat16)).astype(jnp.float32)

@jax.custom_vjp
def low_back(v):
    return v

def low_keep(v):
    return (low(v), None)

def low_pass(kept, grad):
    return (grad,)

def back_keep(v):
    return (v, None)

def back_low(kept, grad):
    return (low(grad),)
low.defvjp(low_keep, low_pass)
low_back.defvjp(back_keep, back_low)

def matmul(left_side, right_side):
    return jnp.dot(left_side, right_side, precision=HIGHEST, preferred_element_type=jnp.float32)

def layer_norm(values):
    center = values - lax.optimization_barrier(jnp.mean(values, axis=-1, keepdims=True))
    variance = lax.optimization_barrier(jnp.mean(center * center, axis=-1, keepdims=True))
    return center * lax.rsqrt(variance + EPSILON)

def segment_ids(lengths, group_rows):
    seq_ends = jnp.cumsum(lengths)
    positions = jnp.arange(group_rows, dtype=jnp.int32)
    return lax.optimization_barrier(jnp.sum((positions[:, None] >= seq_ends[None, :]).astype(jnp.int32), axis=1))

def attend(queries, key_rows, value_rows, segment):
    group_rows = queries.shape[0]
    head_count = queries.shape[1] // HEAD_DIM
    score_scale = HEAD_DIM ** (-0.5)
    query_heads = queries.reshape(group_rows, head_count, HEAD_DIM)
    padding = ((SEQ_MOST, SEQ_MOST), (0, 0), (0, 0))
    key_pad = jnp.pad(key_rows.reshape(group_rows, head_count, HEAD_DIM), padding)
    value_pad = jnp.pad(value_rows.reshape(group_rows, head_count, HEAD_DIM), padding)
    segment_pad = jnp.pad(segment, (SEQ_MOST, SEQ_MOST), constant_values=-1)

    def one_block(block_index):
        offset = (block_index * SEQ_MOST).astype(jnp.int32)
        query_block = lax.dynamic_slice_in_dim(query_heads, offset, SEQ_MOST, 0)
        key_block = lax.dynamic_slice_in_dim(key_pad, offset, 3 * SEQ_MOST, 0)
        value_block = lax.dynamic_slice_in_dim(value_pad, offset, 3 * SEQ_MOST, 0)
        own_segment = lax.dynamic_slice_in_dim(segment, offset, SEQ_MOST, 0)
        key_segment = lax.dynamic_slice_in_dim(segment_pad, offset, 3 * SEQ_MOST, 0)
        scores = low_back(jnp.einsum('qhd,khd->hqk', query_block, key_block, precision=HIGHEST) * score_scale)
        allowed = own_segment[:, None] == key_segment[None, :]
        scores = jnp.where(allowed[None], scores, MASKED)
        weights = low(jax.nn.softmax(scores, axis=-1))
        context = jnp.einsum('hqk,khd->qhd', weights, value_block, precision=HIGHEST)
        return context.reshape(SEQ_MOST, head_count * HEAD_DIM)
    blocks = lax.map(jax.checkpoint(one_block), jnp.arange(group_rows // SEQ_MOST, dtype=jnp.int32))
    return blocks.reshape(group_rows, head_count * HEAD_DIM)

def group_forward(trained, tokens, segment, frozen):
    query_scale, query_bias, value_scale, value_bias = trained
    w_query, w_key, w_value, w_output, vera_down, vera_up, hidden_in, hidden_out = frozen
    shared_code = low_back(matmul(tokens, vera_down))
    code_query = low(shared_code * query_scale)
    code_value = low(shared_code * value_scale)
    side_query = low_back(matmul(code_query, vera_up))
    side_value = low_back(matmul(code_value, vera_up))
    queries = low(low_back(matmul(tokens, w_query) + side_query * query_bias))
    key_rows = low(low_back(matmul(tokens, w_key)))
    value_rows = low(low_back(matmul(tokens, w_value) + side_value * value_bias))
    context = low(low_back(attend(queries, key_rows, value_rows, segment)))
    attended = low_back(matmul(context, w_output))
    normed = layer_norm(tokens + attended)
    preact = low_back(matmul(low(normed), hidden_in))
    activated = low(jax.nn.gelu(preact, approximate=False))
    forward_out = low_back(lax.dot_general(activated, hidden_out, (((1,), (1,)), ((), ())), precision=HIGHEST, preferred_element_type=jnp.float32))
    return layer_norm(normed + forward_out)

def reference(tokens, lengths, cotangent, w_query, w_key, w_value, w_output, vera_down, vera_up, query_scale, query_bias, value_scale, value_bias, hidden_in, hidden_out):
    frozen = tuple((weight.astype(jnp.float32) for weight in (w_query, w_key, w_value, w_output, vera_down, vera_up, hidden_in, hidden_out)))
    trained = (query_scale, query_bias, value_scale, value_bias)
    group_rows = N_HEAD * TOK_DEV
    token_groups = tokens.reshape(N_SEQ, group_rows, D)
    tangent_groups = cotangent.reshape(N_SEQ, group_rows, D)

    def one_group(running, inputs):
        token_block, length_row, tangent_block = inputs
        segment = segment_ids(length_row, group_rows)

        def forward(train_params, token_values):
            return group_forward(train_params, token_values, segment, frozen)
        output, pullback = jax.vjp(forward, trained, token_block.astype(jnp.float32))
        train_grads, token_grads = pullback(tangent_block.astype(jnp.float32))
        running = jax.tree.map(lambda earlier, adding: earlier + adding, running, train_grads)
        return (running, (output.astype(jnp.bfloat16), token_grads.astype(jnp.bfloat16)))
    initial = tuple((jnp.zeros_like(parameter) for parameter in trained))
    totals, (outputs, grad_rows) = lax.scan(one_group, initial, (token_groups, lengths, tangent_groups))
    return (outputs.reshape(TOKENS, D), grad_rows.reshape(TOKENS, D), totals[0], totals[1], totals[2], totals[3])
```

```python
import functools
import math

import jax
import jax.numpy as jnp
from jax import lax
from jax.experimental import pallas as pl
from jax.experimental.pallas import tpu as pltpu
from jax.sharding import PartitionSpec as P

HEAD_DIM = 64
SEQ_MOST = 512
EPSILON = 1e-05
HIDDEN = -1e30
LN2 = math.log(2.0)
QUERY_FOLD = HEAD_DIM ** (-0.5) / LN2
TILE_Q = 256
TILE_K = 256
LANES = 128
NN = (((1,), (0,)), ((), ()))
NT = (((1,), (1,)), ((), ()))
TN = (((0,), (0,)), ((), ()))
F32 = jnp.float32
BF16 = jnp.bfloat16
VMEM = pl.BlockSpec(memory_space=pltpu.VMEM)
SMEM = pl.BlockSpec(memory_space=pltpu.SMEM)
PARAMS = pltpu.CompilerParams(vmem_limit_bytes=58 << 20)


def dot(left, right, form):
    return lax.dot_general(left, right, form, preferred_element_type=F32)


def sds(shape, dtype):
    return jax.ShapeDtypeStruct(shape, dtype)


def span(index, size):
    return pl.ds(pl.multiple_of(index * size, size), size)


def project_kernel(
    x_ref, wq_ref, wk_ref, wv_ref, down_ref, up_ref, qs_ref, qb_ref, vs_ref, vb_ref,
    qt_ref, kt_ref, vt_ref, xt_ref, wqe_ref, wve_ref,
):
    rows, width = x_ref.shape

    def fold(index, carry):
        part = span(index, 256)
        down = down_ref[part, :].astype(F32)
        side_q = dot((down * qs_ref[...]).astype(BF16), up_ref[...], NN) * qb_ref[...]
        wqe_ref[part, :] = ((wq_ref[part, :].astype(F32) + side_q) * QUERY_FOLD).astype(BF16)
        side_v = dot((down * vs_ref[...]).astype(BF16), up_ref[...], NN) * vb_ref[...]
        wve_ref[part, :] = (wv_ref[part, :].astype(F32) + side_v).astype(BF16)
        return carry

    lax.fori_loop(0, width // 256, fold, 0)

    def flip(index, carry):
        part = span(index, 256)
        xt_ref[:, part] = x_ref[part, :].T
        return carry

    lax.fori_loop(0, rows // 256, flip, 0)

    def apply(index, carry):
        part = span(index, 256)
        qt_ref[part, :] = dot(wqe_ref[:, part], xt_ref[...], TN).astype(BF16)
        kt_ref[part, :] = dot(wk_ref[:, part], xt_ref[...], TN).astype(BF16)
        vt_ref[part, :] = dot(wve_ref[:, part], xt_ref[...], TN).astype(BF16)
        return carry

    lax.fori_loop(0, width // 256, apply, 0)


def bounds(len_ref, first, count):
    row = first + lax.broadcasted_iota(jnp.int32, (1, count), 1)
    last = first + count - 1
    low = jnp.zeros((1, count), jnp.int32)
    high = jnp.full((1, count), 1 << 30, jnp.int32)
    end, least, most = 0, 0, 1 << 30
    for i in range(len_ref.shape[1]):
        end = end + len_ref[0, i]
        low = jnp.where(row >= end, end, low)
        high = jnp.where(row < end, jnp.minimum(high, end), high)
        least = jnp.where(first >= end, end, least)
        most = jnp.where(last < end, jnp.minimum(most, end), most)
    return low, high, least, most


def key_range(least, most, shift, extent):
    start = (least - shift) // LANES
    tiles = (most - shift - start * LANES + TILE_K - 1) // TILE_K
    start = jnp.minimum(start, (extent - tiles * TILE_K) // LANES)
    return start, tiles


def attend_kernel(
    shift_ref, len_ref, qt_ref, kt_ref, vt_ref, xl_ref, xr_ref, wk_ref, wve_ref,
    ct_ref, ls_ref, ke_ref, ve_ref,
    flip_ref, acc_ref, high_ref, total_ref, bias_ref,
):
    width, rows = qt_ref.shape
    extent = ke_ref.shape[1]
    heads = width // HEAD_DIM
    shift = shift_ref[0]

    ke_ref[:, SEQ_MOST : SEQ_MOST + rows] = kt_ref[...]
    ve_ref[:, SEQ_MOST : SEQ_MOST + rows] = vt_ref[...]
    for side_ref, base in ((xl_ref, 0), (xr_ref, SEQ_MOST + rows)):
        flip_ref[...] = side_ref[...].T

        def edge(index, carry):
            part = span(index, 256)
            ke_ref[part, base : base + SEQ_MOST] = dot(
                wk_ref[:, part], flip_ref[...], TN
            ).astype(BF16)
            ve_ref[part, base : base + SEQ_MOST] = dot(
                wve_ref[:, part], flip_ref[...], TN
            ).astype(BF16)
            return carry

        lax.fori_loop(0, width // 256, edge, 0)

    def query_tile(tile, carry):
        first = shift + SEQ_MOST + tile * TILE_Q
        low, high, least, most = bounds(len_ref, first, TILE_Q)
        start, tiles = key_range(least, most, shift, extent)
        q_part = span(tile, TILE_Q)
        acc_ref[...] = jnp.zeros_like(acc_ref)
        high_ref[...] = jnp.full_like(high_ref, HIDDEN)
        total_ref[...] = jnp.zeros_like(total_ref)

        def key_tile(step, inner):
            base = pl.multiple_of((start + step * (TILE_K // LANES)) * LANES, LANES)
            k_part = pl.ds(base, TILE_K)
            key = shift + base + lax.broadcasted_iota(jnp.int32, (TILE_K, TILE_Q), 0)
            bias_ref[...] = jnp.where((key >= low) & (key < high), 0.0, HIDDEN)

            def group(index, deep):
                for sub in range(4):
                    head = index * 4 + sub
                    part = span(head, HEAD_DIM)
                    scores = dot(ke_ref[part, k_part], qt_ref[part, q_part], TN) + bias_ref[...]
                    before = high_ref[head]
                    best = jnp.maximum(before, jnp.max(scores, axis=0, keepdims=True))
                    fade = jnp.exp2(before - best)
                    probs = jnp.exp2(scores - best)
                    high_ref[head] = best
                    total_ref[head] = total_ref[head] * fade + jnp.sum(
                        probs, axis=0, keepdims=True
                    )
                    acc_ref[part, :] = acc_ref[part, :] * fade + dot(
                        ve_ref[part, k_part], probs.astype(BF16), NN
                    )
                return deep

            lax.fori_loop(0, heads // 4, group, 0)
            return inner

        lax.fori_loop(0, tiles, key_tile, 0)
        for head in range(heads):
            part = pl.ds(head * HEAD_DIM, HEAD_DIM)
            total = total_ref[head]
            ct_ref[part, q_part] = (acc_ref[part, :] / total).astype(BF16)
            ls_ref[head, :, q_part] = high_ref[head] + jnp.log2(total)
        return carry

    lax.fori_loop(0, rows // TILE_Q, query_tile, 0)


def attend_back_kernel(
    shift_ref, len_ref, qt_ref, ke_ref, ve_ref, ls_ref, gt_ref, dl_ref,
    dq_ref, dk_ref, dv_ref,
    dq_acc, dk_acc, dv_acc, bias_ref,
):
    width, rows = qt_ref.shape
    extent = ke_ref.shape[1]
    heads = width // HEAD_DIM
    shift = shift_ref[0]
    dk_acc[...] = jnp.zeros_like(dk_acc)
    dv_acc[...] = jnp.zeros_like(dv_acc)

    def query_tile(tile, carry):
        first = shift + SEQ_MOST + tile * TILE_Q
        low, high, least, most = bounds(len_ref, first, TILE_Q)
        start, tiles = key_range(least, most, shift, extent)
        q_part = span(tile, TILE_Q)
        dq_acc[...] = jnp.zeros_like(dq_acc)

        def key_tile(step, inner):
            base = pl.multiple_of((start + step * (TILE_K // LANES)) * LANES, LANES)
            k_part = pl.ds(base, TILE_K)
            key = shift + base + lax.broadcasted_iota(jnp.int32, (TILE_K, TILE_Q), 0)
            bias_ref[...] = jnp.where((key >= low) & (key < high), 0.0, HIDDEN)

            def group(index, deep):
                for sub in range(4):
                    head = index * 4 + sub
                    part = span(head, HEAD_DIM)
                    keys = ke_ref[part, k_part]
                    queries = qt_ref[part, q_part]
                    grads = gt_ref[part, q_part]
                    scores = dot(keys, queries, TN) + bias_ref[...]
                    probs = jnp.exp2(scores - ls_ref[head, :, q_part])
                    grad_probs = dot(ve_ref[part, k_part], grads, TN)
                    slopes = (probs * (grad_probs - dl_ref[head, :, q_part])).astype(BF16)
                    dv_acc[part, k_part] += dot(grads, probs.astype(BF16), NT)
                    dk_acc[part, k_part] += dot(queries, slopes, NT)
                    dq_acc[part, :] += dot(keys, slopes, NN)
                return deep

            lax.fori_loop(0, heads // 4, group, 0)
            return inner

        lax.fori_loop(0, tiles, key_tile, 0)
        dq_ref[:, q_part] = (dq_acc[...] * LN2).astype(BF16)
        return carry

    lax.fori_loop(0, rows // TILE_Q, query_tile, 0)
    dk_ref[...] = (dk_acc[...] * LN2).astype(BF16)
    dv_ref[...] = dv_acc[...].astype(BF16)


def norm(values):
    center = values - jnp.mean(values, axis=0, keepdims=True)
    inverse = lax.rsqrt(jnp.mean(center * center, axis=0, keepdims=True) + EPSILON)
    return center * inverse, inverse


def norm_back(gradient, normed, inverse):
    centered = gradient - jnp.mean(gradient, axis=0, keepdims=True)
    return inverse * (centered - normed * jnp.mean(gradient * normed, axis=0, keepdims=True))


def gelu_parts(x):
    bell = jnp.exp(-0.5 * (x * x))
    t = 1.0 / (1.0 + (0.3275911 * math.sqrt(0.5)) * jnp.abs(x))
    poly = t * (0.127414796 + t * (-0.142248368 + t * (0.710706870 + t * (-0.726576013 + t * 0.530702714))))
    tail = poly * bell
    normal = jnp.where(x >= 0, 1.0 - tail, tail)
    return x * normal, normal + x * (bell * (1.0 / math.sqrt(2.0 * math.pi)))


def feed_kernel(
    xt_ref, ct_ref, cot_ref, wo_ref, hi_ref, ho_ref,
    out_ref, gf_ref, gc_ref, dl_ref,
    normed_ref, low_ref, slope_ref, sum_ref,
):
    width = xt_ref.shape[0]
    hidden = hi_ref.shape[0]
    step = 768
    heads = width // HEAD_DIM
    attended = dot(wo_ref[...], ct_ref[...], TN)
    normed, inverse_first = norm(xt_ref[...].astype(F32) + attended)
    normed_ref[...] = normed
    low_ref[...] = normed.astype(BF16)
    sum_ref[...] = normed

    def forward(index, carry):
        part = span(index, step)
        act, slope = gelu_parts(dot(hi_ref[part, :], low_ref[...], NN))
        slope_ref[part, :] = slope
        sum_ref[...] += dot(ho_ref[part, :], act.astype(BF16), TN)
        return carry

    lax.fori_loop(0, hidden // step, forward, 0)
    layer_out, inverse_second = norm(sum_ref[...])
    out_ref[...] = layer_out.T.astype(BF16)
    grad = norm_back(cot_ref[...].astype(F32).T, layer_out, inverse_second)
    sum_ref[...] = grad
    low_ref[...] = grad.astype(BF16)

    def backward(index, carry):
        part = span(index, step)
        upstream = dot(ho_ref[part, :], low_ref[...], NN)
        grad_pre = (slope_ref[part, :] * upstream).astype(BF16)
        sum_ref[...] += dot(hi_ref[part, :], grad_pre, TN)
        return carry

    lax.fori_loop(0, hidden // step, backward, 0)
    grad_first = norm_back(sum_ref[...], normed_ref[...], inverse_first)
    gf_ref[...] = grad_first
    grad_context = dot(wo_ref[...], grad_first.astype(BF16), NN).astype(BF16)
    gc_ref[...] = grad_context
    product = grad_context.astype(F32) * ct_ref[...].astype(F32)
    for head in range(heads):
        dl_ref[head] = jnp.sum(
            product[head * HEAD_DIM : (head + 1) * HEAD_DIM], axis=0, keepdims=True
        )


def edge_kernel(dk_ref, dv_ref, wk_ref, wve_ref, left_ref, right_ref):
    extent = dk_ref.shape[1]
    width = wk_ref.shape[0]

    def part_of(index, carry):
        part = span(index, 256)
        for out_ref, base in ((left_ref, 0), (right_ref, extent - SEQ_MOST)):
            side = slice(base, base + SEQ_MOST)
            out_ref[part, :] = (
                dot(wk_ref[part, :], dk_ref[:, side], NN)
                + dot(wve_ref[part, :], dv_ref[:, side], NN)
            ).astype(BF16)
        return carry

    lax.fori_loop(0, width // 256, part_of, 0)


def grads_kernel(
    dq_ref, dk_ref, dv_ref, xt_ref, xl_ref, xr_ref, gf_ref, wqe_ref, wk_ref, wve_ref,
    down_ref, up_ref, qs_ref, qb_ref, vs_ref, vb_ref,
    own_ref, gqs_ref, gqb_ref, gvs_ref, gvb_ref,
    sum_ref,
):
    width, rows = dq_ref.shape
    rank = up_ref.shape[0]
    own = slice(SEQ_MOST, SEQ_MOST + rows)

    def tokens_part(index, carry):
        part = span(index, 256)
        own_ref[part, :] = (
            gf_ref[part, :]
            + dot(wqe_ref[part, :], dq_ref[...], NN)
            + dot(wk_ref[part, :], dk_ref[:, own], NN)
            + dot(wve_ref[part, :], dv_ref[:, own], NN)
        )
        return carry

    lax.fori_loop(0, width // 256, tokens_part, 0)

    for value in (False, True):
        scale_ref, bias_ref = (vs_ref, vb_ref) if value else (qs_ref, qb_ref)
        out_scale, out_bias = (gvs_ref, gvb_ref) if value else (gqs_ref, gqb_ref)
        factor = 1.0 if value else QUERY_FOLD

        def outer(index, carry):
            part = span(index, 256)
            if value:
                total = dot(xt_ref[part, :], dv_ref[:, own], NT)
                total += dot(xl_ref[:, part], dv_ref[:, :SEQ_MOST], (((0,), (1,)), ((), ())))
                total += dot(xr_ref[:, part], dv_ref[:, SEQ_MOST + rows :], (((0,), (1,)), ((), ())))
            else:
                total = dot(xt_ref[part, :], dq_ref[...], NT)
            sum_ref[part, :] = total.astype(BF16)
            return carry

        lax.fori_loop(0, width // 256, outer, 0)
        out_bias[...] = jnp.zeros_like(out_bias)

        def inner(index, carry):
            part = span(index, 256)
            mixed = dot(down_ref[:, part], sum_ref[...], TN) * up_ref[part, :].astype(F32) * factor
            out_bias[...] += dot_rows(scale_ref[:, part], mixed)
            weighted = mixed * bias_ref[...]
            folded = weighted[:, :LANES]
            for at in range(LANES, width, LANES):
                folded = folded + weighted[:, at : at + LANES]
            out_scale[:, part] = jnp.sum(folded.T, axis=0, keepdims=True)
            return carry

        lax.fori_loop(0, rank // 256, inner, 0)


def dot_rows(scale, mixed):
    return jnp.sum(mixed * jnp.broadcast_to(scale, (LANES, scale.shape[1])).T[:, :1], axis=0, keepdims=True)


def finish_kernel(own_ref, left_ref, right_ref, out_ref):
    rows = own_ref.shape[1]
    total = own_ref[...]
    out_ref[:SEQ_MOST, :] = (total[:, :SEQ_MOST] + left_ref[...].astype(F32)).T.astype(BF16)
    out_ref[rows - SEQ_MOST :, :] = (
        total[:, rows - SEQ_MOST :] + right_ref[...].astype(F32)
    ).T.astype(BF16)


def call(kernel, outs, count, scratch=(), **kw):
    return pl.pallas_call(
        kernel,
        out_shape=outs,
        in_specs=[VMEM] * count,
        out_specs=[VMEM] * len(outs),
        scratch_shapes=list(scratch),
        compiler_params=PARAMS,
        **kw,
    )


def body(n_head, *arrays):
    (
        tokens, lengths, cotangent, w_query, w_key, w_value, w_output, vera_down, vera_up,
        query_scale, query_bias, value_scale, value_bias, hidden_in, hidden_out,
    ) = arrays
    rows, width = tokens.shape
    rank = vera_up.shape[0]
    heads = width // HEAD_DIM
    extent = rows + 2 * SEQ_MOST
    up_z = [(i, i + 1) for i in range(n_head - 1)]
    down_z = [(i + 1, i) for i in range(n_head - 1)]
    from_left = lax.ppermute(tokens[rows - SEQ_MOST :], "head", up_z)
    from_right = lax.ppermute(tokens[:SEQ_MOST], "head", down_z)
    hidden_in_t = lax.all_gather(hidden_in.T, ("seq", "head"), axis=0, tiled=True)
    hidden_out_t = lax.all_gather(hidden_out.T, ("seq", "head"), axis=0, tiled=True)
    hidden = hidden_in_t.shape[0]
    shift = (lax.axis_index("head") * rows - SEQ_MOST).astype(jnp.int32).reshape(1)
    qs, qb = query_scale[None], query_bias[None]
    vs, vb = value_scale[None], value_bias[None]
    tall = sds((width, rows), BF16)
    wide = sds((width, extent), BF16)
    square = sds((width, width), BF16)

    qt, kt, vt, xt, wqe, wve = call(
        project_kernel, [tall, tall, tall, tall, square, square], 10
    )(tokens, w_query, w_key, w_value, vera_down, vera_up, qs, qb, vs, vb)

    stats = sds((heads, 1, rows), F32)
    ct, ls, ke, ve = pl.pallas_call(
        attend_kernel,
        out_shape=[tall, stats, wide, wide],
        in_specs=[SMEM, SMEM] + [VMEM] * 7,
        out_specs=[VMEM] * 4,
        scratch_shapes=[
            pltpu.VMEM((width, SEQ_MOST), BF16),
            pltpu.VMEM((width, TILE_Q), F32),
            pltpu.VMEM((heads, 1, TILE_Q), F32),
            pltpu.VMEM((heads, 1, TILE_Q), F32),
            pltpu.VMEM((TILE_K, TILE_Q), F32),
        ],
        compiler_params=PARAMS,
    )(shift, lengths, qt, kt, vt, from_left, from_right, w_key, wve)

    tile = 256
    column = pl.BlockSpec((width, tile), lambda i: (0, i))
    row = pl.BlockSpec((tile, width), lambda i: (i, 0))
    layer_out, gf, gc, dl = pl.pallas_call(
        feed_kernel,
        grid=(rows // tile,),
        out_shape=[sds((rows, width), BF16), sds((width, rows), F32), tall, stats],
        in_specs=[column, column, row, VMEM, VMEM, VMEM],
        out_specs=[row, column, column, pl.BlockSpec((heads, 1, tile), lambda i: (0, 0, i))],
        scratch_shapes=[
            pltpu.VMEM((width, tile), F32),
            pltpu.VMEM((width, tile), BF16),
            pltpu.VMEM((hidden, tile), F32),
            pltpu.VMEM((width, tile), F32),
        ],
        compiler_params=PARAMS,
    )(xt, ct, cotangent, w_output, hidden_in_t, hidden_out_t)

    dq, dk, dv = pl.pallas_call(
        attend_back_kernel,
        out_shape=[tall, wide, wide],
        in_specs=[SMEM, SMEM] + [VMEM] * 6,
        out_specs=[VMEM] * 3,
        scratch_shapes=[
            pltpu.VMEM((width, TILE_Q), F32),
            pltpu.VMEM((width, extent), F32),
            pltpu.VMEM((width, extent), F32),
            pltpu.VMEM((TILE_K, TILE_Q), F32),
        ],
        compiler_params=PARAMS,
    )(shift, lengths, qt, ke, ve, ls, gc, dl)

    half = sds((width, SEQ_MOST), BF16)
    to_left, to_right = call(edge_kernel, [half, half], 4)(dk, dv, w_key, wve)
    right_part = lax.ppermute(to_left, "head", down_z)
    left_part = lax.ppermute(to_right, "head", up_z)
    own, gqs, gqb, gvs, gvb = call(
        grads_kernel,
        [
            sds((width, rows), F32), sds((1, rank), F32), sds((1, width), F32),
            sds((1, rank), F32), sds((1, width), F32),
        ],
        16,
        [pltpu.VMEM((width, width), BF16)],
    )(dq, dk, dv, xt, from_left, from_right, gf, wqe, w_key, wve, vera_down, vera_up, qs, qb, vs, vb)
    totals = lax.psum((gqs[0], gqb[0], gvs[0], gvb[0]), ("seq", "head"))
    (token_grad,) = call(finish_kernel, [sds((rows, width), BF16)], 3)(own, left_part, right_part)
    return (layer_out, token_grad, *totals)


def solution(mesh):
    return jax.shard_map(
        functools.partial(body, mesh.shape["head"]),
        mesh=mesh,
        in_specs=(
            P(("seq", "head"), None),
            P("seq", None),
            P(("seq", "head"), None),
            P(), P(), P(), P(), P(), P(), P(), P(), P(), P(),
            P(None, ("seq", "head")),
            P(None, ("seq", "head")),
        ),
        out_specs=(P(("seq", "head"), None), P(("seq", "head"), None), P(), P(), P(), P()),
        check_vma=False,
    )
```

```python
import functools
import math

import jax
import jax.numpy as jnp
from jax import lax
from jax.experimental import pallas as pl
from jax.experimental.pallas import tpu as pltpu
from jax.sharding import PartitionSpec as P

HEAD_DIM = 64
SEQ_MOST = 512
EPSILON = 1e-05
HIDDEN = -1e30
LN2 = math.log(2.0)
QUERY_FOLD = HEAD_DIM ** (-0.5) / LN2
TILE_Q = 256
TILE_K = 256
LANES = 128
NN = (((1,), (0,)), ((), ()))
NT = (((1,), (1,)), ((), ()))
TN = (((0,), (0,)), ((), ()))
F32 = jnp.float32
BF16 = jnp.bfloat16
VMEM = pl.BlockSpec(memory_space=pltpu.VMEM)
SMEM = pl.BlockSpec(memory_space=pltpu.SMEM)
MESH = pl.DeviceIdType.MESH
ANY = pl.BlockSpec(memory_space=pl.ANY)
PARAMS = pltpu.CompilerParams(vmem_limit_bytes=58 << 20)


def dot(left, right, form):
    return lax.dot_general(left, right, form, preferred_element_type=F32)


def sds(shape, dtype):
    return jax.ShapeDtypeStruct(shape, dtype)


def span(index, size):
    if isinstance(index, int):
        return pl.ds(index * size, size)
    return pl.ds(pl.multiple_of(index * size, size), size)


def bounds(len_ref, first, count):
    row = first + lax.broadcasted_iota(jnp.int32, (1, count), 1)
    low = jnp.zeros((1, count), jnp.int32)
    high = jnp.full((1, count), 1 << 30, jnp.int32)
    end = 0
    for i in range(len_ref.shape[1]):
        end = end + len_ref[0, i]
        low = jnp.where(row >= end, end, low)
        high = jnp.where(row < end, jnp.minimum(high, end), high)
    return low, high


def reach(len_ref, first, count):
    last = first + count - 1
    end, least, most = 0, 0, 1 << 30
    for i in range(len_ref.shape[1]):
        end = end + len_ref[0, i]
        least = jnp.where(first >= end, end, least)
        most = jnp.where(last < end, jnp.minimum(most, end), most)
    return least, most


def key_range(least, most, shift, extent):
    start = (least - shift) // LANES
    tiles = (most - shift - start * LANES + TILE_K - 1) // TILE_K
    start = jnp.minimum(start, (extent - tiles * TILE_K) // LANES)
    return start, tiles


def other(index, bit):
    return index + bit - 2 * bit * ((index // bit) % 2)


def remote(src, dst, send, recv, seq, head):
    return pltpu.make_async_remote_copy(
        src_ref=src, dst_ref=dst, send_sem=send, recv_sem=recv, device_id=(seq, head), device_id_type=MESH
    )


class Gather:
    def __init__(self, own, full, sems, seq, head, n_head):
        self.own, self.full, self.sems = own, full, sems
        self.seq, self.head, self.n = seq, head, n_head
        self.shard = own.shape[1]
        self.near_x, self.near_y = other(seq, 2), other(seq, 4)
        self.far = other(self.near_x, 4)

    def rows(self, seq, k):
        origin = (self.head + self.n - k) % self.n
        return self.full.at[:, span(seq * self.n + origin, self.shard), :]

    def column(self, seq):
        return self.full.at[:, span(seq, self.n * self.shard), :]

    def pair(self, kind, k):
        return self.sems.at[2 * (4 * kind + k)], self.sems.at[2 * (4 * kind + k) + 1]

    def local(self):
        return pltpu.make_async_copy(self.own, self.rows(self.seq, 0), self.sems.at[0])

    def over_z(self, k):
        return remote(self.own, self.rows(self.seq, 0), *self.pair(0, k), self.seq, (self.head + k) % self.n)

    def over_x(self, k):
        src = self.own if k == 0 else self.rows(self.seq, k)
        return remote(src, self.rows(self.seq, k), *self.pair(1, k), self.near_x, self.head)

    def over_y(self, k):
        src = self.own if k == 0 else self.rows(self.seq, k)
        return remote(src, self.rows(self.seq, k), *self.pair(2, k), self.near_y, self.head)

    def onward(self, k):
        src, to = (self.near_x, self.near_y) if k < 2 else (self.near_y, self.near_x)
        return remote(self.rows(src, k), self.rows(src, k), *self.pair(3, k), to, self.head)

    def across(self, group):
        seq = (self.seq, self.near_x, self.near_y, self.far)[group]
        return remote(
            self.column(seq), self.column(seq), *self.pair(4, group), other(self.seq, 1), self.head
        )


def front_kernel(n_head, n_seq, gather, *refs):
    (
        len_ref, x_ref, wq_ref, wk_ref, wv_ref, down_ref, up_ref, qs_ref, qb_ref, vs_ref, vb_ref,
    ) = refs[:11]
    refs = refs[11:]
    if gather:
        (hi_ref, ho_ref), refs = refs[:2], refs[2:]
    (ct_ref, ls_ref, qt_ref, ke_ref, ve_ref, xt_ref, lt_ref, rt_ref, wqe_ref, wve_ref), refs = refs[:10], refs[10:]
    if gather:
        full_ref, refs = refs[0], refs[1:]
    (
        xl_ref, xr_ref, acc_ref, high_ref, total_ref, low_row, high_row, bias_ref, halo_sem,
    ), refs = refs[:9], refs[9:]
    rows, width = x_ref.shape
    heads = width // HEAD_DIM
    seq, head_at = lax.axis_index("seq"), lax.axis_index("head")
    shift = head_at * rows - SEQ_MOST
    first_z, last_z = head_at == 0, head_at == n_head - 1

    barrier = pltpu.get_barrier_semaphore()
    partners = [(seq, (head_at + k) % n_head) for k in range(1, n_head)]
    if gather:
        partners += [(other(seq, bit), head_at) for bit in (1, 2, 4)]
        own_ref, gather_sem = refs
        own_ref[0] = hi_ref[...].T
        own_ref[1] = ho_ref[...].T
    for partner in partners:
        pl.semaphore_signal(barrier, inc=1, device_id=partner, device_id_type=MESH)
    pl.semaphore_wait(barrier, len(partners))

    to_right = remote(
        x_ref.at[rows - SEQ_MOST :], xl_ref, halo_sem.at[0], halo_sem.at[1], seq, (head_at + 1) % n_head
    )
    to_left = remote(
        x_ref.at[:SEQ_MOST], xr_ref, halo_sem.at[2], halo_sem.at[3], seq, (head_at + n_head - 1) % n_head
    )
    if gather:
        g = Gather(own_ref, full_ref, gather_sem, seq, head_at, n_head)
        for k in (1, 3, 2):
            g.over_z(k).start()
        g.over_x(0).start()
        g.over_y(0).start()
        g.local().start()

    @pl.when(head_at < n_head - 1)
    def _():
        to_right.start()

    @pl.when(head_at > 0)
    def _():
        to_left.start()

    def fold(index, carry):
        part = span(index, 256)
        down = down_ref[part, :].astype(F32)
        side_q = dot((down * qs_ref[...]).astype(BF16), up_ref[...], NN) * qb_ref[...]
        wqe_ref[part, :] = ((wq_ref[part, :].astype(F32) + side_q) * QUERY_FOLD).astype(BF16)
        side_v = dot((down * vs_ref[...]).astype(BF16), up_ref[...], NN) * vb_ref[...]
        wve_ref[part, :] = (wv_ref[part, :].astype(F32) + side_v).astype(BF16)
        return carry

    lax.fori_loop(0, width // 256, fold, 0)

    def flip(index, carry):
        part = span(index, 256)
        xt_ref[:, part] = x_ref[part, :].T
        return carry

    lax.fori_loop(0, rows // 256, flip, 0)
    own = slice(SEQ_MOST, SEQ_MOST + rows)

    def apply(index, carry):
        part = span(index, 256)
        qt_ref[part, :] = dot(wqe_ref[:, part], xt_ref[...], TN).astype(BF16)
        ke_ref[part, own] = dot(wk_ref[:, part], xt_ref[...], TN).astype(BF16)
        ve_ref[part, own] = dot(wve_ref[:, part], xt_ref[...], TN).astype(BF16)
        return carry

    lax.fori_loop(0, width // 256, apply, 0)

    low, high = bounds(len_ref, shift + SEQ_MOST, rows)
    low_row[...] = low
    high_row[...] = high
    acc_ref[...] = jnp.zeros_like(acc_ref)
    high_ref[...] = jnp.full_like(high_ref, HIDDEN)
    total_ref[...] = jnp.zeros_like(total_ref)

    def block(tile, key_tile):
        q_part, k_part = span(tile, TILE_Q), span(key_tile, TILE_K)
        key = shift + key_tile * TILE_K + lax.broadcasted_iota(jnp.int32, (TILE_K, TILE_Q), 0)
        bias_ref[...] = jnp.where((key >= low_row[:, q_part]) & (key < high_row[:, q_part]), 0.0, HIDDEN)
        bias = bias_ref[...]
        parts = [span(head, HEAD_DIM) for head in range(heads)]
        before = [high_ref[head, :, q_part] for head in range(heads)]
        totals = [total_ref[head, :, q_part] for head in range(heads)]
        sums = [acc_ref[part, q_part] for part in parts]
        scores = [dot(ke_ref[part, k_part], qt_ref[part, q_part], TN) + bias for part in parts]
        best = [jnp.maximum(b, jnp.max(v, axis=0, keepdims=True)) for b, v in zip(before, scores)]
        probs = [jnp.exp2(v - b) for v, b in zip(scores, best)]
        fade = [jnp.exp2(a - b) for a, b in zip(before, best)]
        totals = [t * f + jnp.sum(p, axis=0, keepdims=True) for t, f, p in zip(totals, fade, probs)]
        sums = [
            a * f + dot(ve_ref[part, k_part], p.astype(BF16), NN)
            for a, f, p, part in zip(sums, fade, probs, parts)
        ]
        for head, part, b, t, a in zip(range(heads), parts, best, totals, sums):
            high_ref[head, :, q_part] = b
            total_ref[head, :, q_part] = t
            acc_ref[part, q_part] = a

    def own_block(index, carry):
        tile, at = (index + 1) // 4, (index + 1) % 4
        block(tile, at + 1 + (tile + 1) // 2)
        return carry

    def left_block(index, carry):
        block(index // 2, (index + 1) // 2)
        return carry

    def right_block(index, carry):
        block(2 + (index + 1) // 2, 6 + index // 2)
        return carry

    if gather:
        g.over_x(0).wait_recv()
        g.onward(0).start()
    lax.fori_loop(0, 3, own_block, 0)
    if gather:
        g.over_z(1).wait_recv()
        g.over_x(1).start()
        g.over_y(1).start()
    lax.fori_loop(3, 7, own_block, 0)
    if gather:
        g.over_z(3).wait_recv()
        g.over_x(3).start()
        g.over_y(3).start()
        g.over_x(1).wait_recv()
        g.onward(1).start()
    lax.fori_loop(7, 11, own_block, 0)
    if gather:
        g.over_z(2).wait_recv()
        g.over_x(2).start()
        g.over_y(2).start()
        g.local().wait()
        g.across(0).start()
    lax.fori_loop(11, 14, own_block, 0)

    for absent, copy, side_ref, flat_ref, base in (
        (first_z, to_right, xl_ref, lt_ref, 0),
        (last_z, to_left, xr_ref, rt_ref, SEQ_MOST + rows),
    ):

        @pl.when(absent)
        def _():
            side_ref[...] = jnp.zeros_like(side_ref)

        @pl.when(jnp.logical_not(absent))
        def _():
            copy.wait_recv()

        def edge_flip(index, carry):
            part = span(index, 256)
            flat_ref[:, part] = side_ref[part, :].T
            return carry

        lax.fori_loop(0, SEQ_MOST // 256, edge_flip, 0)

        def edge(index, carry):
            part = span(index, 256)
            ke_ref[part, base : base + SEQ_MOST] = dot(wk_ref[:, part], flat_ref[...], TN).astype(BF16)
            ve_ref[part, base : base + SEQ_MOST] = dot(wve_ref[:, part], flat_ref[...], TN).astype(BF16)
            return carry

        lax.fori_loop(0, width // 256, edge, 0)

    if gather:
        g.over_y(3).wait_recv()
        g.onward(3).start()
    lax.fori_loop(0, 3, left_block, 0)
    if gather:
        g.over_y(2).wait_recv()
        g.onward(2).start()
        for k in (2, 3):
            g.over_x(k).wait_recv()
        g.across(1).start()
        for k in (0, 1):
            g.over_y(k).wait_recv()
        g.across(2).start()
    lax.fori_loop(0, 3, right_block, 0)

    for head in range(heads):
        part = pl.ds(head * HEAD_DIM, HEAD_DIM)
        total = total_ref[head]
        ct_ref[part, :] = (acc_ref[part, :] / total).astype(BF16)
        ls_ref[head] = high_ref[head] + jnp.log2(total)

    @pl.when(head_at < n_head - 1)
    def _():
        to_right.wait_send()

    @pl.when(head_at > 0)
    def _():
        to_left.wait_send()

    if gather:
        for k in range(4):
            g.onward(k).wait_recv()
        g.across(3).start()
        for k in (1, 2, 3):
            g.over_z(k).wait_send()
        for k in range(4):
            g.over_x(k).wait_send()
            g.over_y(k).wait_send()
            g.onward(k).wait_send()
        for k, seq_at in enumerate((seq, g.near_x, g.near_y, g.far)):
            g.across(k).wait_send()
            came = g.column(other(seq_at, 1))
            remote(came, came, *g.pair(4, k), other(seq, 1), head_at).wait_recv()


def attend_back_kernel(
    shift_ref, len_ref, qt_ref, ke_ref, ve_ref, ls_ref, gt_ref, dl_ref,
    dq_ref, dk_ref, dv_ref,
    dq_acc, dk_acc, dv_acc, bias_ref,
):
    width, rows = qt_ref.shape
    extent = ke_ref.shape[1]
    heads = width // HEAD_DIM
    shift = shift_ref[0]
    dk_acc[...] = jnp.zeros_like(dk_acc)
    dv_acc[...] = jnp.zeros_like(dv_acc)

    def query_tile(tile, carry):
        first = shift + SEQ_MOST + tile * TILE_Q
        low, high = bounds(len_ref, first, TILE_Q)
        least, most = reach(len_ref, first, TILE_Q)
        start, tiles = key_range(least, most, shift, extent)
        q_part = span(tile, TILE_Q)
        dq_acc[...] = jnp.zeros_like(dq_acc)

        def key_tile(step, inner):
            base = pl.multiple_of((start + step * (TILE_K // LANES)) * LANES, LANES)
            k_part = pl.ds(base, TILE_K)
            key = shift + base + lax.broadcasted_iota(jnp.int32, (TILE_K, TILE_Q), 0)
            bias_ref[...] = jnp.where((key >= low) & (key < high), 0.0, HIDDEN)

            def group(index):
                heads_of = [index * 6 + sub for sub in range(6)]
                parts = [span(head, HEAD_DIM) for head in heads_of]
                bias = bias_ref[...]
                scores = [dot(ke_ref[part, k_part], qt_ref[part, q_part], TN) + bias for part in parts]
                grad_probs = [dot(ve_ref[part, k_part], gt_ref[part, q_part], TN) for part in parts]
                probs = [jnp.exp2(v - ls_ref[head, :, q_part]) for head, v in zip(heads_of, scores)]
                slopes = [
                    (p * (g - dl_ref[head, :, q_part])).astype(BF16)
                    for head, p, g in zip(heads_of, probs, grad_probs)
                ]
                for part, p, d in zip(parts, probs, slopes):
                    dv_acc[part, k_part] += dot(gt_ref[part, q_part], p.astype(BF16), NT)
                    dk_acc[part, k_part] += dot(qt_ref[part, q_part], d, NT)
                    dq_acc[part, :] += dot(ke_ref[part, k_part], d, NN)

            for index in range(heads // 6):
                group(index)
            return inner

        lax.fori_loop(0, tiles, key_tile, 0)
        dq_ref[:, q_part] = (dq_acc[...] * LN2).astype(BF16)
        return carry

    lax.fori_loop(0, rows // TILE_Q, query_tile, 0)
    dk_ref[...] = (dk_acc[...] * LN2).astype(BF16)
    dv_ref[...] = dv_acc[...].astype(BF16)


def norm(values):
    center = values - jnp.mean(values, axis=0, keepdims=True)
    inverse = lax.rsqrt(jnp.mean(center * center, axis=0, keepdims=True) + EPSILON)
    return center * inverse, inverse


def norm_back(gradient, normed, inverse):
    centered = gradient - jnp.mean(gradient, axis=0, keepdims=True)
    return inverse * (centered - normed * jnp.mean(gradient * normed, axis=0, keepdims=True))


def gelu_parts(x):
    bell = jnp.exp2((-0.5 / LN2) * (x * x))
    t = 1.0 / (1.0 + (0.3275911 * math.sqrt(0.5)) * jnp.abs(x))
    poly = t * (0.127414796 + t * (-0.142248368 + t * (0.710706870 + t * (-0.726576013 + t * 0.530702714))))
    tail = poly * bell
    normal = jnp.where(x >= 0, 1.0 - tail, tail)
    return x * normal, normal + x * (bell * (1.0 / math.sqrt(2.0 * math.pi)))


def feed_kernel(
    xt_ref, ct_ref, cot_ref, wo_ref, w_ref,
    out_ref, gf_ref, gc_ref, dl_ref,
    normed_ref, low_ref, slope_ref, sum_ref, act_ref, pre_ref,
):
    width = xt_ref.shape[0]
    hidden = w_ref.shape[1]
    step = act_ref.shape[1]
    heads = width // HEAD_DIM
    pieces = [pl.ds(at, step) for at in range(0, hidden, step)]

    def sweep(first, second, change):
        count = len(pieces)
        pre_ref[0] = dot(w_ref[first, pieces[0], :], low_ref[...], NN)
        for at in range(count):
            if at + 1 < count:
                pre_ref[(at + 1) % 2] = dot(w_ref[first, pieces[at + 1], :], low_ref[...], NN)
            act_ref[at % 2] = change(pieces[at], pre_ref[at % 2]).astype(BF16)
            if at > 0:
                sum_ref[...] += dot(w_ref[second, pieces[at - 1], :], act_ref[(at - 1) % 2], TN)
        sum_ref[...] += dot(w_ref[second, pieces[-1], :], act_ref[(count - 1) % 2], TN)

    def forward(piece, pre):
        act, slope = gelu_parts(pre)
        slope_ref[piece, :] = slope
        return act

    attended = dot(wo_ref[...], ct_ref[...], TN)
    normed, inverse_first = norm(xt_ref[...].astype(F32) + attended)
    normed_ref[...] = normed
    low_ref[...] = normed.astype(BF16)
    sum_ref[...] = normed
    sweep(0, 1, forward)
    layer_out, inverse_second = norm(sum_ref[...])
    out_ref[...] = layer_out.T.astype(BF16)
    grad = norm_back(cot_ref[...].astype(F32).T, layer_out, inverse_second)
    sum_ref[...] = grad
    low_ref[...] = grad.astype(BF16)
    sweep(1, 0, lambda piece, upstream: slope_ref[piece, :] * upstream)
    grad_first = norm_back(sum_ref[...], normed_ref[...], inverse_first)
    gf_ref[...] = grad_first
    grad_context = dot(wo_ref[...], grad_first.astype(BF16), NN).astype(BF16)
    gc_ref[...] = grad_context
    product = grad_context.astype(F32) * ct_ref[...].astype(F32)
    for head in range(heads):
        dl_ref[head] = jnp.sum(
            product[head * HEAD_DIM : (head + 1) * HEAD_DIM], axis=0, keepdims=True
        )


def edge_kernel(dk_ref, dv_ref, wk_ref, wve_ref, left_ref, right_ref):
    extent = dk_ref.shape[1]
    width = wk_ref.shape[0]

    def part_of(index, carry):
        part = span(index, 256)
        for out_ref, base in ((left_ref, 0), (right_ref, extent - SEQ_MOST)):
            side = slice(base, base + SEQ_MOST)
            out_ref[part, :] = (
                dot(wk_ref[part, :], dk_ref[:, side], NN)
                + dot(wve_ref[part, :], dv_ref[:, side], NN)
            ).astype(BF16)
        return carry

    lax.fori_loop(0, width // 256, part_of, 0)


def grads_kernel(
    dq_ref, dk_ref, dv_ref, xt_ref, xl_ref, xr_ref, gf_ref, wqe_ref, wk_ref, wve_ref,
    down_ref, up_ref, qs_ref, qb_ref, vs_ref, vb_ref,
    own_ref, gqs_ref, gqb_ref, gvs_ref, gvb_ref,
    sum_ref,
):
    width, rows = dq_ref.shape
    rank = up_ref.shape[0]
    own = slice(SEQ_MOST, SEQ_MOST + rows)

    def tokens_part(index, carry):
        part = span(index, 256)
        own_ref[part, :] = (
            gf_ref[part, :]
            + dot(wqe_ref[part, :], dq_ref[...], NN)
            + dot(wk_ref[part, :], dk_ref[:, own], NN)
            + dot(wve_ref[part, :], dv_ref[:, own], NN)
        )
        return carry

    lax.fori_loop(0, width // 256, tokens_part, 0)

    for value in (False, True):
        scale_ref, bias_ref = (vs_ref, vb_ref) if value else (qs_ref, qb_ref)
        out_scale, out_bias = (gvs_ref, gvb_ref) if value else (gqs_ref, gqb_ref)
        factor = 1.0 if value else QUERY_FOLD

        def outer(index, carry):
            part = span(index, 256)
            if value:
                total = dot(xt_ref[part, :], dv_ref[:, own], NT)
                total += dot(xl_ref[part, :], dv_ref[:, :SEQ_MOST], NT)
                total += dot(xr_ref[part, :], dv_ref[:, SEQ_MOST + rows :], NT)
            else:
                total = dot(xt_ref[part, :], dq_ref[...], NT)
            sum_ref[part, :] = total.astype(BF16)
            return carry

        lax.fori_loop(0, width // 256, outer, 0)
        out_bias[...] = jnp.zeros_like(out_bias)

        def inner(index, carry):
            part = span(index, 256)
            mixed = dot(down_ref[:, part], sum_ref[...], TN) * up_ref[part, :].astype(F32) * factor
            out_bias[...] += dot_rows(scale_ref[:, part], mixed)
            weighted = mixed * bias_ref[...]
            folded = weighted[:, :LANES]
            for at in range(LANES, width, LANES):
                folded = folded + weighted[:, at : at + LANES]
            out_scale[:, part] = jnp.sum(folded.T, axis=0, keepdims=True)
            return carry

        lax.fori_loop(0, rank // 256, inner, 0)


def dot_rows(scale, mixed):
    return jnp.sum(mixed * jnp.broadcast_to(scale, (LANES, scale.shape[1])).T[:, :1], axis=0, keepdims=True)


def finish_kernel(own_ref, left_ref, right_ref, out_ref):
    rows = own_ref.shape[1]
    total = own_ref[...]
    out_ref[:SEQ_MOST, :] = (total[:, :SEQ_MOST] + left_ref[...].astype(F32)).T.astype(BF16)
    out_ref[rows - SEQ_MOST :, :] = (
        total[:, rows - SEQ_MOST :] + right_ref[...].astype(F32)
    ).T.astype(BF16)


def call(kernel, outs, count, scratch=(), scalars=0):
    return pl.pallas_call(
        kernel,
        out_shape=outs,
        in_specs=[SMEM] * scalars + [VMEM] * count,
        out_specs=[VMEM] * len(outs),
        scratch_shapes=list(scratch),
        compiler_params=PARAMS,
    )


def front(n_head, n_seq, lengths, tokens, w_query, w_key, w_value, vera, shards):
    rows, width = tokens.shape
    heads = width // HEAD_DIM
    extent = rows + 2 * SEQ_MOST
    tall, wide = sds((width, rows), BF16), sds((width, extent), BF16)
    square, half = sds((width, width), BF16), sds((width, SEQ_MOST), BF16)
    outs = [tall, sds((heads, 1, rows), F32), tall, wide, wide, tall, half, half, square, square]
    scratch = [
        pltpu.VMEM((SEQ_MOST, width), BF16),
        pltpu.VMEM((SEQ_MOST, width), BF16),
        pltpu.VMEM((width, rows), F32),
        pltpu.VMEM((heads, 1, rows), F32),
        pltpu.VMEM((heads, 1, rows), F32),
        pltpu.VMEM((1, rows), jnp.int32),
        pltpu.VMEM((1, rows), jnp.int32),
        pltpu.VMEM((TILE_K, TILE_Q), F32),
        pltpu.SemaphoreType.DMA((4,)),
    ]
    gather = len(shards) > 0
    specs = [VMEM] * len(outs)
    if gather:
        shard = shards[0].shape[1]
        outs.append(sds((2, n_head * n_seq * shard, width), BF16))
        specs.append(ANY)
        scratch += [pltpu.VMEM((2, shard, width), BF16), pltpu.SemaphoreType.DMA((40,))]
    return pl.pallas_call(
        functools.partial(front_kernel, n_head, n_seq, gather),
        out_shape=outs,
        in_specs=[SMEM] + [VMEM] * (10 + len(shards)),
        out_specs=specs,
        scratch_shapes=scratch,
        compiler_params=pltpu.CompilerParams(
            vmem_limit_bytes=58 << 20, collective_id=0, has_side_effects=True
        ),
    )(lengths, tokens, w_query, w_key, w_value, *vera, *shards)


def feed(xt, ct, cotangent, w_output, weights):
    width, rows = xt.shape
    hidden = weights.shape[1]
    heads = width // HEAD_DIM
    tile, step = 512, 768
    column = pl.BlockSpec((width, tile), lambda i: (0, i))
    row = pl.BlockSpec((tile, width), lambda i: (i, 0))
    return pl.pallas_call(
        feed_kernel,
        grid=(rows // tile,),
        out_shape=[
            sds((rows, width), BF16), sds((width, rows), F32), sds((width, rows), BF16),
            sds((heads, 1, rows), F32),
        ],
        in_specs=[column, column, row, VMEM, VMEM],
        out_specs=[row, column, column, pl.BlockSpec((heads, 1, tile), lambda i: (0, 0, i))],
        scratch_shapes=[
            pltpu.VMEM((width, tile), F32),
            pltpu.VMEM((width, tile), BF16),
            pltpu.VMEM((hidden, tile), F32),
            pltpu.VMEM((width, tile), F32),
            pltpu.VMEM((2, step, tile), BF16),
            pltpu.VMEM((2, step, tile), F32),
        ],
        compiler_params=PARAMS,
    )(xt, ct, cotangent, w_output, weights)


def attend_back(shift, lengths, qt, ke, ve, ls, gc, dl):
    width, rows = qt.shape
    extent = ke.shape[1]
    wide = sds((width, extent), BF16)
    return call(
        attend_back_kernel,
        [sds((width, rows), BF16), wide, wide],
        6,
        [
            pltpu.VMEM((width, TILE_Q), F32),
            pltpu.VMEM((width, extent), F32),
            pltpu.VMEM((width, extent), F32),
            pltpu.VMEM((TILE_K, TILE_Q), F32),
        ],
        2,
    )(shift, lengths, qt, ke, ve, ls, gc, dl)


def edges(dk, dv, w_key, wve):
    half = sds((dk.shape[0], SEQ_MOST), BF16)
    return call(edge_kernel, [half, half], 4)(dk, dv, w_key, wve)


def grads(dq, *rest):
    width, rows = dq.shape
    rank = rest[-5].shape[0]
    return call(
        grads_kernel,
        [
            sds((width, rows), F32), sds((1, rank), F32), sds((1, width), F32),
            sds((1, rank), F32), sds((1, width), F32),
        ],
        16,
        [pltpu.VMEM((width, width), BF16)],
    )(dq, *rest)


def body(n_seq, n_head, *arrays):
    (
        tokens, lengths, cotangent, w_query, w_key, w_value, w_output, vera_down, vera_up,
        query_scale, query_bias, value_scale, value_bias, hidden_in, hidden_out,
    ) = arrays
    rows, width = tokens.shape
    up_z = [(i, i + 1) for i in range(n_head - 1)]
    down_z = [(i + 1, i) for i in range(n_head - 1)]
    shift = (lax.axis_index("head") * rows - SEQ_MOST).astype(jnp.int32).reshape(1)
    vera = (vera_down, vera_up, query_scale[None], query_bias[None], value_scale[None], value_bias[None])
    fused = (n_seq, n_head) == (8, 4)
    shards = (hidden_in, hidden_out) if fused else ()
    ct, ls, qt, ke, ve, xt, lt, rt, wqe, wve, *full = front(
        n_head, n_seq, lengths, tokens, w_query, w_key, w_value, vera, shards
    )
    if fused:
        (weights,) = full
    else:
        weights = lax.all_gather(
            jnp.stack([hidden_in.T, hidden_out.T]), ("seq", "head"), axis=1, tiled=True
        )
    layer_out, gf, gc, dl = feed(xt, ct, cotangent, w_output, weights)
    dq, dk, dv = attend_back(shift, lengths, qt, ke, ve, ls, gc, dl)
    to_left, to_right = edges(dk, dv, w_key, wve)
    right_part = lax.ppermute(to_left, "head", down_z)
    left_part = lax.ppermute(to_right, "head", up_z)
    own, gqs, gqb, gvs, gvb = grads(dq, dk, dv, xt, lt, rt, gf, wqe, w_key, wve, *vera)
    totals = lax.psum((gqs[0], gqb[0], gvs[0], gvb[0]), ("seq", "head"))
    (token_grad,) = call(finish_kernel, [sds((rows, width), BF16)], 3)(own, left_part, right_part)
    return (layer_out, token_grad, *totals)


def solution(mesh):
    return jax.shard_map(
        functools.partial(body, mesh.shape["seq"], mesh.shape["head"]),
        mesh=mesh,
        in_specs=(
            P(("seq", "head"), None),
            P("seq", None),
            P(("seq", "head"), None),
            P(), P(), P(), P(), P(), P(), P(), P(), P(), P(),
            P(None, ("seq", "head")),
            P(None, ("seq", "head")),
        ),
        out_specs=(P(("seq", "head"), None), P(("seq", "head"), None), P(), P(), P(), P()),
        check_vma=False,
    )
```

```python
import functools
import math

import jax
import jax.numpy as jnp
from jax import lax
from jax.experimental import pallas as pl
from jax.experimental.pallas import tpu as pltpu
from jax.sharding import PartitionSpec as P

HEAD_DIM = 64
SEQ_MOST = 512
EPSILON = 1e-05
HIDDEN = -1e30
LN2 = math.log(2.0)
QUERY_FOLD = HEAD_DIM ** (-0.5) / LN2
TILE_Q = 256
TILE_K = 256
LANES = 128
PACK = 512
NN = (((1,), (0,)), ((), ()))
NT = (((1,), (1,)), ((), ()))
TN = (((0,), (0,)), ((), ()))
F32 = jnp.float32
BF16 = jnp.bfloat16
VMEM = pl.BlockSpec(memory_space=pltpu.VMEM)
SMEM = pl.BlockSpec(memory_space=pltpu.SMEM)
MESH = pl.DeviceIdType.MESH
ANY = pl.BlockSpec(memory_space=pl.ANY)
PARAMS = pltpu.CompilerParams(vmem_limit_bytes=58 << 20)


def dot(left, right, form):
    return lax.dot_general(left, right, form, preferred_element_type=F32)


def sds(shape, dtype):
    return jax.ShapeDtypeStruct(shape, dtype)


def span(index, size):
    if isinstance(index, int):
        return pl.ds(index * size, size)
    return pl.ds(pl.multiple_of(index * size, size), size)


def bounds(len_ref, first, count):
    row = first + lax.broadcasted_iota(jnp.int32, (1, count), 1)
    low = jnp.zeros((1, count), jnp.int32)
    high = jnp.full((1, count), 1 << 30, jnp.int32)
    end = 0
    for i in range(len_ref.shape[1]):
        end = end + len_ref[0, i]
        low = jnp.where(row >= end, end, low)
        high = jnp.where(row < end, jnp.minimum(high, end), high)
    return low, high


def reach(len_ref, first, count):
    last = first + count - 1
    end, least, most = 0, 0, 1 << 30
    for i in range(len_ref.shape[1]):
        end = end + len_ref[0, i]
        least = jnp.where(first >= end, end, least)
        most = jnp.where(last < end, jnp.minimum(most, end), most)
    return least, most


def key_range(least, most, shift, extent):
    start = (least - shift) // LANES
    tiles = (most - shift - start * LANES + TILE_K - 1) // TILE_K
    start = jnp.minimum(start, (extent - tiles * TILE_K) // LANES)
    return start, tiles


def other(index, bit):
    return index + bit - 2 * bit * ((index // bit) % 2)


def remote(src, dst, send, recv, seq, head):
    return pltpu.make_async_remote_copy(
        src_ref=src, dst_ref=dst, send_sem=send, recv_sem=recv, device_id=(seq, head), device_id_type=MESH
    )


class Gather:
    def __init__(self, own, full, sems, seq, head, n_head):
        self.own, self.full, self.sems = own, full, sems
        self.seq, self.head, self.n = seq, head, n_head
        self.shard = own.shape[1]
        self.near_x, self.near_y = other(seq, 2), other(seq, 4)
        self.groups = (seq, self.near_x, self.near_y, other(self.near_x, 4))

    def origin(self, way):
        return self.head - way if way < 4 else self.head + way - 3

    def there(self, way):
        return self.head >= way if way < 4 else self.head + way - 3 < self.n

    def rows(self, seq, origin):
        return self.full.at[:, span(seq * self.n + origin, self.shard), :]

    def source(self, way):
        return self.own if way == 0 else self.rows(self.seq, self.origin(way))

    def pair(self, kind, way):
        return self.sems.at[2 * (7 * kind + way)], self.sems.at[2 * (7 * kind + way) + 1]

    def local(self):
        return pltpu.make_async_copy(self.own, self.rows(self.seq, self.head), self.sems.at[0])

    def up(self, far):
        dst = self.rows(self.seq, self.head - far)
        return remote(self.source(far), dst, self.pair(8, far)[0], self.pair(0, far + 1)[1], self.seq, self.head + 1)

    def down(self, far):
        way = far + 3 if far else 0
        dst = self.rows(self.seq, self.head + far)
        return remote(self.source(way), dst, self.pair(8, far)[1], self.pair(0, far + 4)[1], self.seq, self.head - 1)

    def came_z(self, way):
        dst = self.rows(self.seq, self.origin(way))
        return remote(dst, dst, *self.pair(0, way), self.seq, self.head)

    def over_x(self, way):
        dst = self.rows(self.seq, self.origin(way))
        return remote(self.source(way), dst, *self.pair(1, way), self.near_x, self.head)

    def over_y(self, way):
        dst = self.rows(self.seq, self.origin(way))
        return remote(self.source(way), dst, *self.pair(2, way), self.near_y, self.head)

    def onward(self, way, half):
        src, to = ((self.near_x, self.near_y), (self.near_y, self.near_x))[half]
        part = self.rows(src, self.origin(way)).at[half]
        return remote(part, part, *self.pair(3 + half, way), to, self.head)

    def across(self, group, way):
        dst = self.rows(self.groups[group], self.origin(way))
        src = self.own if group == 0 and way == 0 else dst
        sems = self.sems.at[126 + 2 * (7 * group + way)], self.sems.at[127 + 2 * (7 * group + way)]
        return remote(src, dst, *sems, other(self.seq, 1), self.head)

    def when(self, way, action):
        if way == 0:
            action()
        else:
            pl.when(self.there(way))(action)

    def spread(self, way):
        self.over_x(way).start()
        self.over_y(way).start()
        self.across(0, way).start()

    def begin(self):
        pl.when(self.head < self.n - 1)(lambda: self.up(0).start())
        pl.when(self.head > 0)(lambda: self.down(0).start())
        self.spread(0)
        self.local().start()

    def take_z(self, *ways):
        for way in ways:

            def action():
                self.came_z(way).wait_recv()
                if way in (1, 2):
                    pl.when(self.head < self.n - 1)(lambda: self.up(way).start())
                if way in (4, 5):
                    pl.when(self.head > 0)(lambda: self.down(way - 3).start())
                self.spread(way)

            self.when(way, action)

    def take_xy(self, *ways):
        for way in ways:

            def action():
                self.over_x(way).wait_recv()
                self.onward(way, 0).start()
                self.across(1, way).start()
                self.over_y(way).wait_recv()
                self.onward(way, 1).start()
                self.across(2, way).start()

            self.when(way, action)

    def take_far(self, *ways):
        for way in ways:

            def action():
                self.onward(way, 0).wait_recv()
                self.onward(way, 1).wait_recv()
                self.across(3, way).start()

            self.when(way, action)

    def end(self):
        self.local().wait()
        for far in range(3):
            pl.when((self.head < self.n - 1) & (self.head >= far))(lambda: self.up(far).wait_send())
            pl.when((self.head > 0) & (self.head + far < self.n))(lambda: self.down(far).wait_send())
        for way in range(7):

            def action():
                self.over_x(way).wait_send()
                self.over_y(way).wait_send()
                self.onward(way, 0).wait_send()
                self.onward(way, 1).wait_send()
                for group in range(4):
                    copy = self.across(group, way)
                    copy.wait_send()
                    copy.wait_recv()

            self.when(way, action)


def front_kernel(n_head, n_seq, gather, *refs):
    big, refs = refs[:6], refs[6:]
    len_ref, vectors, refs = refs[0], refs[1:5], refs[5:]
    if gather:
        (hi_ref, ho_ref), refs = refs[:2], refs[2:]
    (ct_ref, ls_ref), refs = refs[:2], refs[2:]
    stored, refs = refs[:8], refs[8:]
    if gather:
        full_ref, refs = refs[0], refs[1:]
    held, refs = refs[:6], refs[6:]
    kept, refs = refs[:8], refs[8:]
    (
        xl_ref, xr_ref, acc_ref, high_ref, total_ref, low_row, high_row, bias_ref,
        load_sem, store_sem, halo_sem,
    ), refs = refs[:11], refs[11:]
    x_hbm = big[0]
    loads = [pltpu.make_async_copy(src, dst, load_sem.at[n]) for n, (src, dst) in enumerate(zip(big, held))]
    stores = [pltpu.make_async_copy(src, dst, store_sem.at[n]) for n, (src, dst) in enumerate(zip(kept, stored))]
    for n in (1, 2, 3, 4, 0, 5):
        loads[n].start()
    x_ref, down_ref, up_ref, wq_ref, wv_ref, wk_ref = held
    qt_ref, ke_ref, ve_ref, xt_ref, lt_ref, rt_ref, wqe_ref, wve_ref = kept
    rows, width = x_ref.shape
    heads = width // HEAD_DIM
    seq, head_at = lax.axis_index("seq"), lax.axis_index("head")
    shift = head_at * rows - SEQ_MOST
    first_z, last_z = head_at == 0, head_at == n_head - 1

    barrier = pltpu.get_barrier_semaphore()
    partners = [(seq, (head_at + k) % n_head) for k in range(1, n_head)]
    if gather:
        partners += [(other(seq, bit), head_at) for bit in (1, 2, 4)]
        own_ref, gather_sem = refs
        own_ref[0] = hi_ref[...]
        own_ref[1] = ho_ref[...]
    for partner in partners:
        pl.semaphore_signal(barrier, inc=1, device_id=partner, device_id_type=MESH)
    pl.semaphore_wait(barrier, len(partners))

    to_right = remote(
        x_hbm.at[rows - SEQ_MOST :], xl_ref, halo_sem.at[0], halo_sem.at[1], seq, (head_at + 1) % n_head
    )
    to_left = remote(
        x_hbm.at[:SEQ_MOST], xr_ref, halo_sem.at[2], halo_sem.at[3], seq, (head_at + n_head - 1) % n_head
    )

    def send_halo():
        pl.when(head_at < n_head - 1)(lambda: to_right.start())
        pl.when(head_at > 0)(lambda: to_left.start())

    if gather:
        g = Gather(own_ref, full_ref, gather_sem, seq, head_at, n_head)
        g.begin()
    else:
        send_halo()
    query_scale, query_bias, value_scale, value_bias = [ref[...].reshape(1, -1) for ref in vectors]
    for n in (1, 2, 3, 4):
        loads[n].wait()

    def fold(index, carry):
        part = span(index, 256)
        down = down_ref[part, :].astype(F32)
        side_q = dot((down * query_scale).astype(BF16), up_ref[...], NN) * query_bias
        wqe_ref[part, :] = ((wq_ref[part, :].astype(F32) + side_q) * QUERY_FOLD).astype(BF16)
        side_v = dot((down * value_scale).astype(BF16), up_ref[...], NN) * value_bias
        wve_ref[part, :] = (wv_ref[part, :].astype(F32) + side_v).astype(BF16)
        return carry

    lax.fori_loop(0, width // 256, fold, 0)
    stores[6].start()
    stores[7].start()
    loads[0].wait()

    def flip(index, carry):
        part = span(index, 256)
        xt_ref[:, part] = x_ref[part, :].T
        return carry

    lax.fori_loop(0, rows // 256, flip, 0)
    stores[3].start()
    own = slice(SEQ_MOST, SEQ_MOST + rows)

    def apply(weight_ref, out_ref, at):
        def piece(index, carry):
            part = span(index, 256)
            out_ref[part, at] = dot(weight_ref[:, part], xt_ref[...], TN).astype(BF16)
            return carry

        lax.fori_loop(0, width // 256, piece, 0)

    apply(wqe_ref, qt_ref, slice(0, rows))
    if gather:
        g.take_z(1, 4)
    loads[5].wait()
    stores[0].start()
    apply(wk_ref, ke_ref, own)
    apply(wve_ref, ve_ref, own)

    low, high = bounds(len_ref, shift + SEQ_MOST, rows)
    low_row[...] = low
    high_row[...] = high
    acc_ref[...] = jnp.zeros_like(acc_ref)
    high_ref[...] = jnp.full_like(high_ref, HIDDEN)
    total_ref[...] = jnp.zeros_like(total_ref)

    def block(tile, key_tile):
        q_part, k_part = span(tile, TILE_Q), span(key_tile, TILE_K)
        key = shift + key_tile * TILE_K + lax.broadcasted_iota(jnp.int32, (TILE_K, TILE_Q), 0)
        bias_ref[...] = jnp.where((key >= low_row[:, q_part]) & (key < high_row[:, q_part]), 0.0, HIDDEN)
        bias = bias_ref[...]
        parts = [span(head, HEAD_DIM) for head in range(heads)]
        before = [high_ref[head, :, q_part] for head in range(heads)]
        totals = [total_ref[head, :, q_part] for head in range(heads)]
        sums = [acc_ref[part, q_part] for part in parts]
        scores = [dot(ke_ref[part, k_part], qt_ref[part, q_part], TN) + bias for part in parts]
        best = [jnp.maximum(b, jnp.max(v, axis=0, keepdims=True)) for b, v in zip(before, scores)]
        probs = [jnp.exp2(v - b) for v, b in zip(scores, best)]
        fade = [jnp.exp2(a - b) for a, b in zip(before, best)]
        totals = [t * f + jnp.sum(p, axis=0, keepdims=True) for t, f, p in zip(totals, fade, probs)]
        sums = [
            a * f + dot(ve_ref[part, k_part], p.astype(BF16), NN)
            for a, f, p, part in zip(sums, fade, probs, parts)
        ]
        for head, part, b, t, a in zip(range(heads), parts, best, totals, sums):
            high_ref[head, :, q_part] = b
            total_ref[head, :, q_part] = t
            acc_ref[part, q_part] = a

    def own_block(index, carry):
        if gather:
            for at, step in (
                (1, lambda: g.take_xy(0)),
                (2, lambda: (g.take_z(2, 5), send_halo())),
                (3, lambda: g.take_xy(1, 4)),
                (5, lambda: g.take_z(3, 6)),
                (6, lambda: g.take_far(0)),
                (8, lambda: g.take_xy(2, 5)),
                (10, lambda: g.take_far(1, 4)),
                (13, lambda: g.take_xy(3, 6)),
            ):

                @pl.when(index == at)
                def _():
                    step()

        tile, at = (index + 1) // 4, (index + 1) % 4
        block(tile, at + 1 + (tile + 1) // 2)
        return carry

    def left_block(index, carry):
        block(index // 2, (index + 1) // 2)
        return carry

    def right_block(index, carry):
        if gather:
            pl.when(index == 0)(lambda: g.take_far(3, 6))
        block(2 + (index + 1) // 2, 6 + index // 2)
        return carry

    lax.fori_loop(0, 14, own_block, 0)

    for absent, copy, side_ref, flat_ref, base in (
        (first_z, to_right, xl_ref, lt_ref, 0),
        (last_z, to_left, xr_ref, rt_ref, SEQ_MOST + rows),
    ):

        @pl.when(absent)
        def _():
            side_ref[...] = jnp.zeros_like(side_ref)

        @pl.when(jnp.logical_not(absent))
        def _():
            copy.wait_recv()

        def edge_flip(index, carry):
            part = span(index, 256)
            flat_ref[:, part] = side_ref[part, :].T
            return carry

        lax.fori_loop(0, SEQ_MOST // 256, edge_flip, 0)

        def edge(index, carry):
            part = span(index, 256)
            ke_ref[part, base : base + SEQ_MOST] = dot(wk_ref[:, part], flat_ref[...], TN).astype(BF16)
            ve_ref[part, base : base + SEQ_MOST] = dot(wve_ref[:, part], flat_ref[...], TN).astype(BF16)
            return carry

        lax.fori_loop(0, width // 256, edge, 0)

    for n in (1, 2, 4, 5):
        stores[n].start()
    if gather:
        g.take_far(2, 5)
    lax.fori_loop(0, 3, left_block, 0)
    lax.fori_loop(0, 3, right_block, 0)

    for head in range(heads):
        part = pl.ds(head * HEAD_DIM, HEAD_DIM)
        total = total_ref[head]
        ct_ref[part, :] = (acc_ref[part, :] / total).astype(BF16)
        ls_ref[head] = high_ref[head] + jnp.log2(total)

    pl.when(head_at < n_head - 1)(lambda: to_right.wait_send())
    pl.when(head_at > 0)(lambda: to_left.wait_send())
    for store in stores:
        store.wait()
    if gather:
        g.end()


def attend_back_kernel(
    shift_ref, len_ref, qt_ref, ke_ref, ve_ref, ls_ref, gt_ref, dl_ref,
    dq_ref, dk_ref, dv_ref,
    dq_acc, dk_acc, dv_acc, bias_ref,
):
    width, rows = qt_ref.shape
    extent = ke_ref.shape[1]
    heads = width // HEAD_DIM
    shift = shift_ref[0]
    dk_acc[...] = jnp.zeros_like(dk_acc)
    dv_acc[...] = jnp.zeros_like(dv_acc)

    def query_tile(tile, carry):
        first = shift + SEQ_MOST + tile * TILE_Q
        low, high = bounds(len_ref, first, TILE_Q)
        least, most = reach(len_ref, first, TILE_Q)
        start, tiles = key_range(least, most, shift, extent)
        q_part = span(tile, TILE_Q)
        dq_acc[...] = jnp.zeros_like(dq_acc)

        def key_tile(step, inner):
            base = pl.multiple_of((start + step * (TILE_K // LANES)) * LANES, LANES)
            k_part = pl.ds(base, TILE_K)
            key = shift + base + lax.broadcasted_iota(jnp.int32, (TILE_K, TILE_Q), 0)
            bias_ref[...] = jnp.where((key >= low) & (key < high), 0.0, HIDDEN)

            def group(index):
                heads_of = [index * 6 + sub for sub in range(6)]
                parts = [span(head, HEAD_DIM) for head in heads_of]
                bias = bias_ref[...]
                scores = [dot(ke_ref[part, k_part], qt_ref[part, q_part], TN) + bias for part in parts]
                grad_probs = [dot(ve_ref[part, k_part], gt_ref[part, q_part], TN) for part in parts]
                probs = [jnp.exp2(v - ls_ref[head, :, q_part]) for head, v in zip(heads_of, scores)]
                slopes = [
                    (p * (g - dl_ref[head, :, q_part])).astype(BF16)
                    for head, p, g in zip(heads_of, probs, grad_probs)
                ]
                for part, p, d in zip(parts, probs, slopes):
                    dv_acc[part, k_part] += dot(gt_ref[part, q_part], p.astype(BF16), NT)
                    dk_acc[part, k_part] += dot(qt_ref[part, q_part], d, NT)
                    dq_acc[part, :] += dot(ke_ref[part, k_part], d, NN)

            for index in range(heads // 6):
                group(index)
            return inner

        lax.fori_loop(0, tiles, key_tile, 0)
        dq_ref[:, q_part] = (dq_acc[...] * LN2).astype(BF16)
        return carry

    lax.fori_loop(0, rows // TILE_Q, query_tile, 0)
    dk_ref[...] = (dk_acc[...] * LN2).astype(BF16)
    dv_ref[...] = dv_acc[...].astype(BF16)


def norm(values):
    center = values - jnp.mean(values, axis=0, keepdims=True)
    inverse = lax.rsqrt(jnp.mean(center * center, axis=0, keepdims=True) + EPSILON)
    return center * inverse, inverse


def norm_back(gradient, normed, inverse):
    centered = gradient - jnp.mean(gradient, axis=0, keepdims=True)
    return inverse * (centered - normed * jnp.mean(gradient * normed, axis=0, keepdims=True))


def gelu_parts(x):
    bell = jnp.exp2((-0.5 / LN2) * (x * x))
    t = 1.0 / (1.0 + (0.3275911 * math.sqrt(0.5)) * jnp.abs(x))
    poly = t * (0.127414796 + t * (-0.142248368 + t * (0.710706870 + t * (-0.726576013 + t * 0.530702714))))
    tail = poly * bell
    normal = jnp.where(x >= 0, 1.0 - tail, tail)
    return x * normal, normal + x * (bell * (1.0 / math.sqrt(2.0 * math.pi)))


def feed_kernel(
    xt_ref, ct_ref, cot_ref, wo_ref, w_ref,
    out_ref, gf_ref, gc_ref, dl_ref,
    normed_ref, low_ref, slope_ref, sum_ref, act_ref, pre_ref,
):
    width = xt_ref.shape[0]
    hidden = w_ref.shape[1]
    step = act_ref.shape[1]
    heads = width // HEAD_DIM
    pieces = [pl.ds(at, step) for at in range(0, hidden, step)]

    def sweep(first, second, change):
        count = len(pieces)
        pre_ref[0] = dot(w_ref[first, pieces[0], :], low_ref[...], NN)
        for at in range(count):
            if at + 1 < count:
                pre_ref[(at + 1) % 2] = dot(w_ref[first, pieces[at + 1], :], low_ref[...], NN)
            act_ref[at % 2] = change(pieces[at], pre_ref[at % 2]).astype(BF16)
            if at > 0:
                sum_ref[...] += dot(w_ref[second, pieces[at - 1], :], act_ref[(at - 1) % 2], TN)
        sum_ref[...] += dot(w_ref[second, pieces[-1], :], act_ref[(count - 1) % 2], TN)

    def forward(piece, pre):
        act, slope = gelu_parts(pre)
        slope_ref[piece, :] = slope
        return act

    attended = dot(wo_ref[...], ct_ref[...], TN)
    normed, inverse_first = norm(xt_ref[...].astype(F32) + attended)
    normed_ref[...] = normed
    low_ref[...] = normed.astype(BF16)
    sum_ref[...] = normed
    sweep(0, 1, forward)
    layer_out, inverse_second = norm(sum_ref[...])
    out_ref[...] = layer_out.T.astype(BF16)
    grad = norm_back(cot_ref[...].astype(F32).T, layer_out, inverse_second)
    sum_ref[...] = grad
    low_ref[...] = grad.astype(BF16)
    sweep(1, 0, lambda piece, upstream: slope_ref[piece, :] * upstream)
    grad_first = norm_back(sum_ref[...], normed_ref[...], inverse_first)
    gf_ref[...] = grad_first
    grad_context = dot(wo_ref[...], grad_first.astype(BF16), NN).astype(BF16)
    gc_ref[...] = grad_context
    product = grad_context.astype(F32) * ct_ref[...].astype(F32)
    for head in range(heads):
        dl_ref[head] = jnp.sum(
            product[head * HEAD_DIM : (head + 1) * HEAD_DIM], axis=0, keepdims=True
        )


def pack(rows):
    places, at = [], 0
    for size in rows:
        places.append([(at + n, n * PACK, min(PACK, size - n * PACK)) for n in range(-(-size // PACK))])
        at += len(places[-1])
    return places, at


def tail_kernel(n_head, n_seq, *refs):
    big, refs = refs[:12], refs[12:]
    vectors, refs = refs[:4], refs[4:]
    query_scale, query_bias, value_scale, value_bias = [ref[...].reshape(1, -1) for ref in vectors]
    (out_ref, gqs_ref, gqb_ref, gvs_ref, gvb_ref), refs = refs[:5], refs[5:]
    held, refs = refs[:12], refs[12:]
    (
        load_sem, own_ref, mix_ref, send_left, send_right, from_left, from_right, halo_sem,
        z_slots, s_slots, z_sem, s_sem,
    ) = refs
    loads = [pltpu.make_async_copy(src, dst, load_sem.at[n]) for n, (src, dst) in enumerate(zip(big, held))]
    for load in loads:
        load.start()
    dk_ref, dv_ref, wk_ref, wve_ref, xt_ref, dq_ref, lt_ref, rt_ref, down_ref, up_ref, wqe_ref, gf_ref = held
    width, rows = dq_ref.shape
    rank = up_ref.shape[0]
    own = slice(SEQ_MOST, SEQ_MOST + rows)
    seq, head_at = lax.axis_index("seq"), lax.axis_index("head")

    barrier = pltpu.get_barrier_semaphore()
    partners = [(seq, (head_at + k) % n_head) for k in range(1, n_head)]
    partners += [((seq + k) % n_seq, head_at) for k in range(1, n_seq)]
    for partner in partners:
        pl.semaphore_signal(barrier, inc=1, device_id=partner, device_id_type=MESH)
    pl.semaphore_wait(barrier, len(partners))

    for load in loads[:4]:
        load.wait()

    def edge(index, carry):
        part = span(index, 256)
        for side_ref, base in ((send_left, 0), (send_right, SEQ_MOST + rows)):
            side = slice(base, base + SEQ_MOST)
            side_ref[part, :] = (
                dot(wk_ref[part, :], dk_ref[:, side], NN) + dot(wve_ref[part, :], dv_ref[:, side], NN)
            ).astype(BF16)
        return carry

    lax.fori_loop(0, width // 256, edge, 0)
    to_left = remote(
        send_left, from_right, halo_sem.at[0], halo_sem.at[1], seq, (head_at + n_head - 1) % n_head
    )
    to_right = remote(send_right, from_left, halo_sem.at[2], halo_sem.at[3], seq, (head_at + 1) % n_head)
    first_z, last_z = head_at == 0, head_at == n_head - 1

    @pl.when(jnp.logical_not(first_z))
    def _():
        to_left.start()

    @pl.when(jnp.logical_not(last_z))
    def _():
        to_right.start()

    places, depth = pack((rank, width, rank, width))
    z_slots[head_at] = jnp.zeros_like(z_slots[0])
    for load in loads[4:10]:
        load.wait()

    for value in (False, True):
        scale_row, bias = (value_scale, value_bias) if value else (query_scale, query_bias)
        factor = 1.0 if value else QUERY_FOLD
        scale_at, bias_at = places[2 * value], places[2 * value + 1]

        def outer(index, carry):
            part = span(index, 256)
            if value:
                total = dot(xt_ref[part, :], dv_ref[:, own], NT)
                total += dot(lt_ref[part, :], dv_ref[:, :SEQ_MOST], NT)
                total += dot(rt_ref[part, :], dv_ref[:, SEQ_MOST + rows :], NT)
            else:
                total = dot(xt_ref[part, :], dq_ref[...], NT)
            mix_ref[part, :] = total.astype(BF16)
            return carry

        lax.fori_loop(0, width // 256, outer, 0)
        bias_sum = jnp.zeros((1, width), F32)
        for at in range(0, rank, 256):
            part = slice(at, at + 256)
            mixed = dot(down_ref[:, part], mix_ref[...], TN) * up_ref[part, :].astype(F32) * factor
            scale = jnp.broadcast_to(scale_row[:, part], (LANES, 256)).T[:, :1]
            bias_sum += jnp.sum(mixed * scale, axis=0, keepdims=True)
            weighted = mixed * bias
            folded = weighted[:, :LANES]
            for lane in range(LANES, width, LANES):
                folded = folded + weighted[:, lane : lane + LANES]
            row, column = at // PACK, at % PACK
            z_slots[head_at, pl.ds(scale_at[row][0], 1), pl.ds(column, 256)] = jnp.sum(
                folded.T, axis=0, keepdims=True
            )
        for row, start, size in bias_at:
            z_slots[head_at, pl.ds(row, 1), pl.ds(0, size)] = bias_sum[:, start : start + size]

    def over_z(k):
        return remote(
            z_slots.at[head_at], z_slots.at[head_at], z_sem.at[2 * k], z_sem.at[2 * k + 1],
            seq, (head_at + k) % n_head,
        )

    def over_seq(k):
        return remote(
            s_slots.at[seq], s_slots.at[seq], s_sem.at[2 * k], s_sem.at[2 * k + 1],
            (seq + k) % n_seq, head_at,
        )

    for k in range(1, n_head):
        over_z(k).start()
    for load in loads[10:]:
        load.wait()

    def tokens_part(index, carry):
        part = span(index, 256)
        own_ref[part, :] = (
            gf_ref[part, :]
            + dot(wqe_ref[part, :], dq_ref[...], NN)
            + dot(wk_ref[part, :], dk_ref[:, own], NN)
            + dot(wve_ref[part, :], dv_ref[:, own], NN)
        )
        return carry

    lax.fori_loop(0, width // 256, tokens_part, 0)
    for k in range(1, n_head):
        over_z(k).wait_recv()
    total = z_slots[0]
    for k in range(1, n_head):
        total = total + z_slots[k]
    s_slots[seq] = total
    for k in range(1, n_seq):
        over_seq(k).start()

    for absent, copy, side_ref, base in (
        (first_z, to_right, from_left, 0),
        (last_z, to_left, from_right, rows - SEQ_MOST),
    ):

        @pl.when(absent)
        def _():
            side_ref[...] = jnp.zeros_like(side_ref)

        @pl.when(jnp.logical_not(absent))
        def _():
            copy.wait_recv()

        def finish(index, carry):
            part = span(index, 256)
            at = pl.ds(pl.multiple_of(base + index * 256, 256), 256)
            out_ref[at, :] = (own_ref[:, at] + side_ref[:, part].astype(F32)).T.astype(BF16)
            return carry

        lax.fori_loop(0, SEQ_MOST // 256, finish, 0)

    for k in range(1, n_seq):
        over_seq(k).wait_recv()
    total = s_slots[0]
    for k in range(1, n_seq):
        total = total + s_slots[k]
    for vector_ref, place in zip((gqs_ref, gqb_ref, gvs_ref, gvb_ref), places):
        for row, start, size in place:
            vector_ref[start : start + size] = total[row, :size]

    @pl.when(jnp.logical_not(first_z))
    def _():
        to_left.wait_send()

    @pl.when(jnp.logical_not(last_z))
    def _():
        to_right.wait_send()

    for k in range(1, n_head):
        over_z(k).wait_send()
    for k in range(1, n_seq):
        over_seq(k).wait_send()


def call(kernel, outs, count, scratch=(), scalars=0):
    return pl.pallas_call(
        kernel,
        out_shape=outs,
        in_specs=[SMEM] * scalars + [VMEM] * count,
        out_specs=[VMEM] * len(outs),
        scratch_shapes=list(scratch),
        compiler_params=PARAMS,
    )


def front(n_head, n_seq, lengths, tokens, w_query, w_key, w_value, vera, shards):
    rows, width = tokens.shape
    heads = width // HEAD_DIM
    extent = rows + 2 * SEQ_MOST
    tall, wide = sds((width, rows), BF16), sds((width, extent), BF16)
    square, half = sds((width, width), BF16), sds((width, SEQ_MOST), BF16)
    kept = [tall, wide, wide, tall, half, half, square, square]
    outs = [tall, sds((heads, 1, rows), F32)] + kept
    big = (tokens, vera[0], vera[1], w_query, w_value, w_key)
    scratch = [pltpu.VMEM(a.shape, a.dtype) for a in (*big, *kept)] + [
        pltpu.VMEM((SEQ_MOST, width), BF16),
        pltpu.VMEM((SEQ_MOST, width), BF16),
        pltpu.VMEM((width, rows), F32),
        pltpu.VMEM((heads, 1, rows), F32),
        pltpu.VMEM((heads, 1, rows), F32),
        pltpu.VMEM((1, rows), jnp.int32),
        pltpu.VMEM((1, rows), jnp.int32),
        pltpu.VMEM((TILE_K, TILE_Q), F32),
        pltpu.SemaphoreType.DMA((len(big),)),
        pltpu.SemaphoreType.DMA((len(kept),)),
        pltpu.SemaphoreType.DMA((4,)),
    ]
    gather = len(shards) > 0
    specs = [VMEM] * 2 + [ANY] * len(kept)
    if gather:
        shard = shards[0].shape[0]
        outs.append(sds((2, n_head * n_seq * shard, width), BF16))
        specs.append(ANY)
        scratch += [pltpu.VMEM((2, shard, width), BF16), pltpu.SemaphoreType.DMA((182,))]
    return pl.pallas_call(
        functools.partial(front_kernel, n_head, n_seq, gather),
        out_shape=outs,
        in_specs=[ANY] * len(big) + [SMEM] + [VMEM] * (4 + len(shards)),
        out_specs=specs,
        scratch_shapes=scratch,
        compiler_params=pltpu.CompilerParams(
            vmem_limit_bytes=58 << 20, collective_id=0, has_side_effects=True
        ),
    )(*big, lengths, *vera[2:], *shards)


def feed(xt, ct, cotangent, w_output, weights):
    width, rows = xt.shape
    hidden = weights.shape[1]
    heads = width // HEAD_DIM
    tile, step = 512, 768
    column = pl.BlockSpec((width, tile), lambda i: (0, i))
    row = pl.BlockSpec((tile, width), lambda i: (i, 0))
    return pl.pallas_call(
        feed_kernel,
        grid=(rows // tile,),
        out_shape=[
            sds((rows, width), BF16), sds((width, rows), F32), sds((width, rows), BF16),
            sds((heads, 1, rows), F32),
        ],
        in_specs=[column, column, row, VMEM, VMEM],
        out_specs=[row, column, column, pl.BlockSpec((heads, 1, tile), lambda i: (0, 0, i))],
        scratch_shapes=[
            pltpu.VMEM((width, tile), F32),
            pltpu.VMEM((width, tile), BF16),
            pltpu.VMEM((hidden, tile), F32),
            pltpu.VMEM((width, tile), F32),
            pltpu.VMEM((2, step, tile), BF16),
            pltpu.VMEM((2, step, tile), F32),
        ],
        compiler_params=PARAMS,
    )(xt, ct, cotangent, w_output, weights)


def attend_back(shift, lengths, qt, ke, ve, ls, gc, dl):
    width, rows = qt.shape
    extent = ke.shape[1]
    wide = sds((width, extent), BF16)
    return call(
        attend_back_kernel,
        [sds((width, rows), BF16), wide, wide],
        6,
        [
            pltpu.VMEM((width, TILE_Q), F32),
            pltpu.VMEM((width, extent), F32),
            pltpu.VMEM((width, extent), F32),
            pltpu.VMEM((TILE_K, TILE_Q), F32),
        ],
        2,
    )(shift, lengths, qt, ke, ve, ls, gc, dl)


def tail(n_head, n_seq, big, small):
    dq, up = big[5], big[9]
    width, rows = dq.shape
    rank = up.shape[0]
    depth = -(-pack((rank, width, rank, width))[1] // 8) * 8
    half = pltpu.VMEM((width, SEQ_MOST), BF16)
    outs = [sds((rows, width), BF16)] + [sds((size,), F32) for size in (rank, width, rank, width)]
    return pl.pallas_call(
        functools.partial(tail_kernel, n_head, n_seq),
        out_shape=outs,
        in_specs=[ANY] * len(big) + [VMEM] * len(small),
        out_specs=[VMEM] * len(outs),
        scratch_shapes=[pltpu.VMEM(a.shape, a.dtype) for a in big]
        + [
            pltpu.SemaphoreType.DMA((len(big),)),
            pltpu.VMEM((width, rows), F32),
            pltpu.VMEM((width, width), BF16),
            half, half, half, half,
            pltpu.SemaphoreType.DMA((4,)),
            pltpu.VMEM((n_head, depth, PACK), F32),
            pltpu.VMEM((n_seq, depth, PACK), F32),
            pltpu.SemaphoreType.DMA((2 * n_head,)),
            pltpu.SemaphoreType.DMA((2 * n_seq,)),
        ],
        compiler_params=pltpu.CompilerParams(
            vmem_limit_bytes=58 << 20, collective_id=1, has_side_effects=True
        ),
    )(*big, *small)


def body(n_seq, n_head, *arrays):
    (
        tokens, lengths, cotangent, w_query, w_key, w_value, w_output, vera_down, vera_up,
        query_scale, query_bias, value_scale, value_bias, hidden_in, hidden_out,
    ) = arrays
    rows, width = tokens.shape
    shift = (lax.axis_index("head") * rows - SEQ_MOST).astype(jnp.int32).reshape(1)
    vera = (vera_down, vera_up, query_scale, query_bias, value_scale, value_bias)
    fused = (n_seq, n_head) == (8, 4)
    shards = (hidden_in.T, hidden_out.T) if fused else ()
    ct, ls, qt, ke, ve, xt, lt, rt, wqe, wve, *full = front(
        n_head, n_seq, lengths, tokens, w_query, w_key, w_value, vera, shards
    )
    if fused:
        (weights,) = full
    else:
        weights = lax.all_gather(
            jnp.stack([hidden_in.T, hidden_out.T]), ("seq", "head"), axis=1, tiled=True
        )
    layer_out, gf, gc, dl = feed(xt, ct, cotangent, w_output, weights)
    dq, dk, dv = attend_back(shift, lengths, qt, ke, ve, ls, gc, dl)
    token_grad, *totals = tail(
        n_head, n_seq, (dk, dv, w_key, wve, xt, dq, lt, rt, vera_down, vera_up, wqe, gf), vera[2:]
    )
    return (layer_out, token_grad, *totals)


def solution(mesh):
    return jax.shard_map(
        functools.partial(body, mesh.shape["seq"], mesh.shape["head"]),
        mesh=mesh,
        in_specs=(
            P(("seq", "head"), None),
            P("seq", None),
            P(("seq", "head"), None),
            P(), P(), P(), P(), P(), P(), P(), P(), P(), P(),
            P(None, ("seq", "head")),
            P(None, ("seq", "head")),
        ),
        out_specs=(P(("seq", "head"), None), P(("seq", "head"), None), P(), P(), P(), P()),
        check_vma=False,
    )
```

```python
import functools
import math

import jax
import jax.numpy as jnp
from jax import lax
from jax.experimental import pallas as pl
from jax.experimental.pallas import tpu as pltpu
from jax.sharding import PartitionSpec as P

HEAD_DIM = 64
SEQ_MOST = 512
EPSILON = 1e-05
HIDDEN = -1e30
LN2 = math.log(2.0)
QUERY_FOLD = HEAD_DIM ** (-0.5) / LN2
TILE_Q = 256
TILE_K = 256
LANES = 128
PACK = 512
NN = (((1,), (0,)), ((), ()))
NT = (((1,), (1,)), ((), ()))
TN = (((0,), (0,)), ((), ()))
F32 = jnp.float32
BF16 = jnp.bfloat16
VMEM = pl.BlockSpec(memory_space=pltpu.VMEM)
SMEM = pl.BlockSpec(memory_space=pltpu.SMEM)
MESH = pl.DeviceIdType.MESH
ANY = pl.BlockSpec(memory_space=pl.ANY)
PARAMS = pltpu.CompilerParams(vmem_limit_bytes=58 << 20)


def dot(left, right, form):
    return lax.dot_general(left, right, form, preferred_element_type=F32)


def sds(shape, dtype):
    return jax.ShapeDtypeStruct(shape, dtype)


def span(index, size):
    if isinstance(index, int):
        return pl.ds(index * size, size)
    return pl.ds(pl.multiple_of(index * size, size), size)


def bounds(len_ref, first, count):
    row = first + lax.broadcasted_iota(jnp.int32, (1, count), 1)
    low = jnp.zeros((1, count), jnp.int32)
    high = jnp.full((1, count), 1 << 30, jnp.int32)
    end = 0
    for i in range(len_ref.shape[1]):
        end = end + len_ref[0, i]
        low = jnp.where(row >= end, end, low)
        high = jnp.where(row < end, jnp.minimum(high, end), high)
    return low, high


def reach(len_ref, first, count):
    last = first + count - 1
    end, least, most = 0, 0, 1 << 30
    for i in range(len_ref.shape[1]):
        end = end + len_ref[0, i]
        least = jnp.where(first >= end, end, least)
        most = jnp.where(last < end, jnp.minimum(most, end), most)
    return least, most


def key_range(least, most, shift, extent):
    start = (least - shift) // LANES
    tiles = (most - shift - start * LANES + TILE_K - 1) // TILE_K
    start = jnp.minimum(start, (extent - tiles * TILE_K) // LANES)
    return start, tiles


def other(index, bit):
    return index + bit - 2 * bit * ((index // bit) % 2)


def remote(src, dst, send, recv, seq, head):
    return pltpu.make_async_remote_copy(
        src_ref=src, dst_ref=dst, send_sem=send, recv_sem=recv, device_id=(seq, head), device_id_type=MESH
    )


class Gather:
    def __init__(self, own, full, sems, seq, head, n_head):
        self.own, self.full, self.sems = own, full, sems
        self.seq, self.head, self.n = seq, head, n_head
        self.shard = own.shape[1]
        self.near_x, self.near_y = other(seq, 2), other(seq, 4)
        self.groups = (seq, self.near_x, self.near_y, other(self.near_x, 4))

    def origin(self, way):
        return self.head - way if way < 4 else self.head + way - 3

    def there(self, way):
        return self.head >= way if way < 4 else self.head + way - 3 < self.n

    def rows(self, seq, origin):
        return self.full.at[:, span(seq * self.n + origin, self.shard), :]

    def source(self, way):
        return self.own if way == 0 else self.rows(self.seq, self.origin(way))

    def pair(self, kind, way):
        return self.sems.at[2 * (7 * kind + way)], self.sems.at[2 * (7 * kind + way) + 1]

    def local(self):
        return pltpu.make_async_copy(self.own, self.rows(self.seq, self.head), self.sems.at[0])

    def up(self, far):
        dst = self.rows(self.seq, self.head - far)
        return remote(self.source(far), dst, self.pair(8, far)[0], self.pair(0, far + 1)[1], self.seq, self.head + 1)

    def down(self, far):
        way = far + 3 if far else 0
        dst = self.rows(self.seq, self.head + far)
        return remote(self.source(way), dst, self.pair(8, far)[1], self.pair(0, far + 4)[1], self.seq, self.head - 1)

    def came_z(self, way):
        dst = self.rows(self.seq, self.origin(way))
        return remote(dst, dst, *self.pair(0, way), self.seq, self.head)

    def over_x(self, way):
        dst = self.rows(self.seq, self.origin(way))
        return remote(self.source(way), dst, *self.pair(1, way), self.near_x, self.head)

    def over_y(self, way):
        dst = self.rows(self.seq, self.origin(way))
        return remote(self.source(way), dst, *self.pair(2, way), self.near_y, self.head)

    def onward(self, way, half):
        src, to = ((self.near_x, self.near_y), (self.near_y, self.near_x))[half]
        part = self.rows(src, self.origin(way)).at[half]
        return remote(part, part, *self.pair(3 + half, way), to, self.head)

    def across(self, group, way):
        dst = self.rows(self.groups[group], self.origin(way))
        src = self.own if group == 0 and way == 0 else dst
        sems = self.sems.at[126 + 2 * (7 * group + way)], self.sems.at[127 + 2 * (7 * group + way)]
        return remote(src, dst, *sems, other(self.seq, 1), self.head)

    def slots(self, index):
        z = self.head
        return (
            ((0, None),),
            ((1, z > 0), (4, z == 0)),
            ((4, (z == 1) | (z == 2)), (5, z == 0), (2, z == 3)),
            ((6, z == 0), (5, z == 1), (2, z == 2), (3, z == 3)),
        )[index]

    def each(self, index, action):
        for way, chosen in self.slots(index):
            if chosen is None:
                action(way)
            else:
                pl.when(chosen)(functools.partial(action, way))

    def begin(self):
        pl.when(self.head < self.n - 1)(lambda: self.up(0).start())
        pl.when(self.head > 0)(lambda: self.down(0).start())
        self.local().start()
        self.spread(0)

    def take_z(self, far):
        def below():
            self.came_z(far).wait_recv()
            if far < self.n - 1:
                pl.when(self.head < self.n - 1)(lambda: self.up(far).start())

        def above():
            self.came_z(far + 3).wait_recv()
            if far < self.n - 1:
                pl.when(self.head > 0)(lambda: self.down(far).start())

        pl.when(self.there(far))(below)
        pl.when(self.there(far + 3))(above)

    def spread(self, index):
        def action(way):
            self.over_x(way).start()
            self.over_y(way).start()
            self.across(0, way).start()

        self.each(index, action)

    def take_xy(self, index):
        def action(way):
            self.over_x(way).wait_recv()
            self.onward(way, 0).start()
            self.over_y(way).wait_recv()
            self.onward(way, 1).start()
            self.across(1, way).start()
            self.across(2, way).start()

        self.each(index, action)

    def take_far(self, index):
        def action(way):
            self.onward(way, 0).wait_recv()
            self.onward(way, 1).wait_recv()
            self.across(3, way).start()

        self.each(index, action)

    def end(self):
        self.local().wait()
        for far in range(3):
            pl.when((self.head < self.n - 1) & (self.head >= far))(lambda: self.up(far).wait_send())
            pl.when((self.head > 0) & (self.head + far < self.n))(lambda: self.down(far).wait_send())
        for way in range(7):

            def action():
                self.over_x(way).wait_send()
                self.over_y(way).wait_send()
                self.onward(way, 0).wait_send()
                self.onward(way, 1).wait_send()
                for group in range(4):
                    copy = self.across(group, way)
                    copy.wait_send()
                    copy.wait_recv()

            if way == 0:
                action()
            else:
                pl.when(self.there(way))(action)


def front_kernel(n_head, n_seq, gather, *refs):
    big, refs = refs[:6], refs[6:]
    len_ref, vectors, refs = refs[0], refs[1:5], refs[5:]
    if gather:
        (hi_ref, ho_ref), refs = refs[:2], refs[2:]
    (ct_ref, ls_ref), refs = refs[:2], refs[2:]
    stored, refs = refs[:8], refs[8:]
    if gather:
        full_ref, refs = refs[0], refs[1:]
    held, refs = refs[:6], refs[6:]
    kept, refs = refs[:8], refs[8:]
    (
        xl_ref, xr_ref, acc_ref, high_ref, total_ref, low_row, high_row, bias_ref,
        load_sem, store_sem, halo_sem,
    ), refs = refs[:11], refs[11:]
    x_hbm = big[0]
    loads = [pltpu.make_async_copy(src, dst, load_sem.at[n]) for n, (src, dst) in enumerate(zip(big, held))]
    stores = [pltpu.make_async_copy(src, dst, store_sem.at[n]) for n, (src, dst) in enumerate(zip(kept, stored))]
    for n in (1, 2, 3, 4, 0, 5):
        loads[n].start()
    x_ref, down_ref, up_ref, wq_ref, wv_ref, wk_ref = held
    qt_ref, ke_ref, ve_ref, xt_ref, lt_ref, rt_ref, wqe_ref, wve_ref = kept
    rows, width = x_ref.shape
    heads = width // HEAD_DIM
    seq, head_at = lax.axis_index("seq"), lax.axis_index("head")
    shift = head_at * rows - SEQ_MOST
    first_z, last_z = head_at == 0, head_at == n_head - 1

    barrier = pltpu.get_barrier_semaphore()
    partners = [(seq, (head_at + k) % n_head) for k in range(1, n_head)]
    if gather:
        partners += [(other(seq, bit), head_at) for bit in (1, 2, 4)]
        own_ref, gather_sem = refs
        own_ref[0] = hi_ref[...]
        own_ref[1] = ho_ref[...]
    for partner in partners:
        pl.semaphore_signal(barrier, inc=1, device_id=partner, device_id_type=MESH)
    pl.semaphore_wait(barrier, len(partners))

    to_right = remote(
        x_hbm.at[rows - SEQ_MOST :], xl_ref, halo_sem.at[0], halo_sem.at[1], seq, (head_at + 1) % n_head
    )
    to_left = remote(
        x_hbm.at[:SEQ_MOST], xr_ref, halo_sem.at[2], halo_sem.at[3], seq, (head_at + n_head - 1) % n_head
    )

    def send_halo():
        pl.when(head_at < n_head - 1)(lambda: to_right.start())
        pl.when(head_at > 0)(lambda: to_left.start())

    if gather:
        g = Gather(own_ref, full_ref, gather_sem, seq, head_at, n_head)
        g.begin()
    else:
        send_halo()
    query_scale, query_bias, value_scale, value_bias = [ref[...].reshape(1, -1) for ref in vectors]
    for n in (1, 2, 3, 4):
        loads[n].wait()

    def fold(index, carry):
        part = span(index, 256)
        down = down_ref[part, :].astype(F32)
        side_q = dot((down * query_scale).astype(BF16), up_ref[...], NN) * query_bias
        wqe_ref[part, :] = ((wq_ref[part, :].astype(F32) + side_q) * QUERY_FOLD).astype(BF16)
        side_v = dot((down * value_scale).astype(BF16), up_ref[...], NN) * value_bias
        wve_ref[part, :] = (wv_ref[part, :].astype(F32) + side_v).astype(BF16)
        return carry

    lax.fori_loop(0, width // 256, fold, 0)
    stores[6].start()
    stores[7].start()
    loads[0].wait()

    def flip(index, carry):
        part = span(index, 256)
        xt_ref[:, part] = x_ref[part, :].T
        return carry

    lax.fori_loop(0, rows // 256, flip, 0)
    stores[3].start()
    own = slice(SEQ_MOST, SEQ_MOST + rows)

    def apply(weight_ref, out_ref, at):
        def piece(index, carry):
            part = span(index, 256)
            out_ref[part, at] = dot(weight_ref[:, part], xt_ref[...], TN).astype(BF16)
            return carry

        lax.fori_loop(0, width // 256, piece, 0)

    apply(wqe_ref, qt_ref, slice(0, rows))
    if gather:
        g.take_z(1)
        g.spread(1)
    loads[5].wait()
    stores[0].start()
    apply(wk_ref, ke_ref, own)
    apply(wve_ref, ve_ref, own)

    low, high = bounds(len_ref, shift + SEQ_MOST, rows)
    low_row[...] = low
    high_row[...] = high
    acc_ref[...] = jnp.zeros_like(acc_ref)
    high_ref[...] = jnp.full_like(high_ref, HIDDEN)
    total_ref[...] = jnp.zeros_like(total_ref)

    def block(tile, key_tile):
        q_part, k_part = span(tile, TILE_Q), span(key_tile, TILE_K)
        key = shift + key_tile * TILE_K + lax.broadcasted_iota(jnp.int32, (TILE_K, TILE_Q), 0)
        bias_ref[...] = jnp.where((key >= low_row[:, q_part]) & (key < high_row[:, q_part]), 0.0, HIDDEN)
        bias = bias_ref[...]
        parts = [span(head, HEAD_DIM) for head in range(heads)]
        before = [high_ref[head, :, q_part] for head in range(heads)]
        totals = [total_ref[head, :, q_part] for head in range(heads)]
        sums = [acc_ref[part, q_part] for part in parts]
        scores = [dot(ke_ref[part, k_part], qt_ref[part, q_part], TN) + bias for part in parts]
        best = [jnp.maximum(b, jnp.max(v, axis=0, keepdims=True)) for b, v in zip(before, scores)]
        probs = [jnp.exp2(v - b) for v, b in zip(scores, best)]
        fade = [jnp.exp2(a - b) for a, b in zip(before, best)]
        totals = [t * f + jnp.sum(p, axis=0, keepdims=True) for t, f, p in zip(totals, fade, probs)]
        sums = [
            a * f + dot(ve_ref[part, k_part], p.astype(BF16), NN)
            for a, f, p, part in zip(sums, fade, probs, parts)
        ]
        for head, part, b, t, a in zip(range(heads), parts, best, totals, sums):
            high_ref[head, :, q_part] = b
            total_ref[head, :, q_part] = t
            acc_ref[part, q_part] = a

    steps = {}
    if gather:
        steps = {
            0: lambda: (g.take_xy(0),),
            2: lambda: (g.take_z(2), g.spread(2),),
            4: lambda: (send_halo(), g.take_xy(1),),
            7: lambda: (g.take_z(3), g.spread(3), g.take_far(0),),
            10: lambda: (g.take_xy(2),),
            12: lambda: (g.take_far(1),),
            14: lambda: (g.take_xy(3),),
            16: lambda: (g.take_far(2),),
            18: lambda: (g.take_far(3),),
        }

    def blocks(first, last, place):
        def one(index, carry):
            for at in steps:
                if first <= at < last:

                    @pl.when(index == at)
                    def _():
                        steps[at]()

            block(*place(index))
            return carry

        lax.fori_loop(first, last, one, 0)

    def own_place(index):
        tile = (index + 1) // 4
        return tile, (index + 1) % 4 + 1 + (tile + 1) // 2

    blocks(0, 14, own_place)

    for absent, copy, side_ref, flat_ref, base in (
        (first_z, to_right, xl_ref, lt_ref, 0),
        (last_z, to_left, xr_ref, rt_ref, SEQ_MOST + rows),
    ):

        @pl.when(absent)
        def _():
            side_ref[...] = jnp.zeros_like(side_ref)

        @pl.when(jnp.logical_not(absent))
        def _():
            copy.wait_recv()

        def edge_flip(index, carry):
            part = span(index, 256)
            flat_ref[:, part] = side_ref[part, :].T
            return carry

        lax.fori_loop(0, SEQ_MOST // 256, edge_flip, 0)

        def edge(index, carry):
            part = span(index, 256)
            ke_ref[part, base : base + SEQ_MOST] = dot(wk_ref[:, part], flat_ref[...], TN).astype(BF16)
            ve_ref[part, base : base + SEQ_MOST] = dot(wve_ref[:, part], flat_ref[...], TN).astype(BF16)
            return carry

        lax.fori_loop(0, width // 256, edge, 0)

    for n in (1, 2, 4, 5):
        stores[n].start()
    blocks(14, 17, lambda index: ((index - 14) // 2, (index - 13) // 2))
    blocks(17, 20, lambda index: (2 + (index - 16) // 2, 6 + (index - 17) // 2))

    for head in range(heads):
        part = pl.ds(head * HEAD_DIM, HEAD_DIM)
        total = total_ref[head]
        ct_ref[part, :] = (acc_ref[part, :] / total).astype(BF16)
        ls_ref[head] = high_ref[head] + jnp.log2(total)

    pl.when(head_at < n_head - 1)(lambda: to_right.wait_send())
    pl.when(head_at > 0)(lambda: to_left.wait_send())
    for store in stores:
        store.wait()
    if gather:
        g.end()


def attend_back_kernel(
    len_ref, qt_ref, ke_ref, ve_ref, ls_ref, gt_ref, dl_ref,
    dq_ref, dk_ref, dv_ref,
    dq_acc, dk_acc, dv_acc, bias_ref,
):
    width, rows = qt_ref.shape
    extent = ke_ref.shape[1]
    heads = width // HEAD_DIM
    shift = lax.axis_index("head") * rows - SEQ_MOST
    dk_acc[...] = jnp.zeros_like(dk_acc)
    dv_acc[...] = jnp.zeros_like(dv_acc)

    def query_tile(tile, carry):
        first = shift + SEQ_MOST + tile * TILE_Q
        low, high = bounds(len_ref, first, TILE_Q)
        least, most = reach(len_ref, first, TILE_Q)
        start, tiles = key_range(least, most, shift, extent)
        q_part = span(tile, TILE_Q)
        dq_acc[...] = jnp.zeros_like(dq_acc)

        def key_tile(step, inner):
            base = pl.multiple_of((start + step * (TILE_K // LANES)) * LANES, LANES)
            k_part = pl.ds(base, TILE_K)
            key = shift + base + lax.broadcasted_iota(jnp.int32, (TILE_K, TILE_Q), 0)
            bias_ref[...] = jnp.where((key >= low) & (key < high), 0.0, HIDDEN)

            def group(index):
                heads_of = [index * 6 + sub for sub in range(6)]
                parts = [span(head, HEAD_DIM) for head in heads_of]
                bias = bias_ref[...]
                scores = [dot(ke_ref[part, k_part], qt_ref[part, q_part], TN) + bias for part in parts]
                grad_probs = [dot(ve_ref[part, k_part], gt_ref[part, q_part], TN) for part in parts]
                probs = [jnp.exp2(v - ls_ref[head, :, q_part]) for head, v in zip(heads_of, scores)]
                slopes = [
                    (p * (g - dl_ref[head, :, q_part])).astype(BF16)
                    for head, p, g in zip(heads_of, probs, grad_probs)
                ]
                for part, p, d in zip(parts, probs, slopes):
                    dv_acc[part, k_part] += dot(gt_ref[part, q_part], p.astype(BF16), NT)
                    dk_acc[part, k_part] += dot(qt_ref[part, q_part], d, NT)
                    dq_acc[part, :] += dot(ke_ref[part, k_part], d, NN)

            for index in range(heads // 6):
                group(index)
            return inner

        lax.fori_loop(0, tiles, key_tile, 0)
        dq_ref[:, q_part] = (dq_acc[...] * LN2).astype(BF16)
        return carry

    lax.fori_loop(0, rows // TILE_Q, query_tile, 0)
    dk_ref[...] = (dk_acc[...] * LN2).astype(BF16)
    dv_ref[...] = dv_acc[...].astype(BF16)


def norm(values):
    center = values - jnp.mean(values, axis=0, keepdims=True)
    inverse = lax.rsqrt(jnp.mean(center * center, axis=0, keepdims=True) + EPSILON)
    return center * inverse, inverse


def norm_back(gradient, normed, inverse):
    centered = gradient - jnp.mean(gradient, axis=0, keepdims=True)
    return inverse * (centered - normed * jnp.mean(gradient * normed, axis=0, keepdims=True))


def gelu_parts(x):
    bell = jnp.exp2((-0.5 / LN2) * (x * x))
    t = 1.0 / (1.0 + (0.3275911 * math.sqrt(0.5)) * jnp.abs(x))
    poly = t * (0.127414796 + t * (-0.142248368 + t * (0.710706870 + t * (-0.726576013 + t * 0.530702714))))
    tail = poly * bell
    normal = jnp.where(x >= 0, 1.0 - tail, tail)
    return x * normal, normal + x * (bell * (1.0 / math.sqrt(2.0 * math.pi)))


def feed_kernel(
    xt_ref, ct_ref, cot_ref, wo_ref, w_ref,
    out_ref, gf_ref, gc_ref, dl_ref,
    normed_ref, low_ref, slope_ref, sum_ref, act_ref, pre_ref,
):
    width = xt_ref.shape[0]
    hidden = w_ref.shape[1]
    step = act_ref.shape[1]
    heads = width // HEAD_DIM
    pieces = [pl.ds(at, step) for at in range(0, hidden, step)]

    def sweep(first, second, change):
        count = len(pieces)
        pre_ref[0] = dot(w_ref[first, pieces[0], :], low_ref[...], NN)
        for at in range(count):
            if at + 1 < count:
                pre_ref[(at + 1) % 2] = dot(w_ref[first, pieces[at + 1], :], low_ref[...], NN)
            act_ref[at % 2] = change(pieces[at], pre_ref[at % 2]).astype(BF16)
            if at > 0:
                sum_ref[...] += dot(w_ref[second, pieces[at - 1], :], act_ref[(at - 1) % 2], TN)
        sum_ref[...] += dot(w_ref[second, pieces[-1], :], act_ref[(count - 1) % 2], TN)

    def forward(piece, pre):
        act, slope = gelu_parts(pre)
        slope_ref[piece, :] = slope
        return act

    attended = dot(wo_ref[...], ct_ref[...], TN)
    normed, inverse_first = norm(xt_ref[...].astype(F32) + attended)
    normed_ref[...] = normed
    low_ref[...] = normed.astype(BF16)
    sum_ref[...] = normed
    sweep(0, 1, forward)
    layer_out, inverse_second = norm(sum_ref[...])
    out_ref[...] = layer_out.T.astype(BF16)
    grad = norm_back(cot_ref[...].astype(F32).T, layer_out, inverse_second)
    sum_ref[...] = grad
    low_ref[...] = grad.astype(BF16)
    sweep(1, 0, lambda piece, upstream: slope_ref[piece, :] * upstream)
    grad_first = norm_back(sum_ref[...], normed_ref[...], inverse_first)
    gf_ref[...] = grad_first
    grad_context = dot(wo_ref[...], grad_first.astype(BF16), NN).astype(BF16)
    gc_ref[...] = grad_context
    product = grad_context.astype(F32) * ct_ref[...].astype(F32)
    for head in range(heads):
        dl_ref[head] = jnp.sum(
            product[head * HEAD_DIM : (head + 1) * HEAD_DIM], axis=0, keepdims=True
        )


def pack(rows):
    places, at = [], 0
    for size in rows:
        places.append([(at + n, n * PACK, min(PACK, size - n * PACK)) for n in range(-(-size // PACK))])
        at += len(places[-1])
    return places, at


def tail_kernel(n_head, n_seq, *refs):
    big, refs = refs[:12], refs[12:]
    vectors, refs = refs[:4], refs[4:]
    query_scale, query_bias, value_scale, value_bias = [ref[...].reshape(1, -1) for ref in vectors]
    (own_hbm, from_left, from_right, sum_ref), refs = refs[:4], refs[4:]
    held, refs = refs[:12], refs[12:]
    (
        load_sem, own_ref, mix_ref, send_left, send_right, halo_sem, z_slots, s_slots, z_sem, s_sem,
    ) = refs
    dk_ref, dv_ref, wk_ref, wve_ref, xt_ref, dq_ref, lt_ref, rt_ref, down_ref, up_ref, wqe_ref, gf_ref = held
    width, rows = dq_ref.shape
    rank = up_ref.shape[0]
    own = slice(SEQ_MOST, SEQ_MOST + rows)
    sides = (slice(0, SEQ_MOST), slice(SEQ_MOST + rows, 2 * SEQ_MOST + rows))
    pieces = [(wk_ref, big[2]), (wve_ref, big[3])]
    pieces += [(ref.at[:, side], hbm.at[:, side]) for side in sides for ref, hbm in zip(held[:2], big[:2])]
    pieces += [(dq_ref, big[5]), (xt_ref, big[4]), (down_ref, big[8]), (up_ref, big[9])]
    pieces += [(lt_ref, big[6]), (rt_ref, big[7]), (dv_ref.at[:, own], big[1].at[:, own])]
    pieces += [(dk_ref.at[:, own], big[0].at[:, own]), (wqe_ref, big[10]), (gf_ref, big[11])]
    loads = [pltpu.make_async_copy(src, dst, load_sem.at[n]) for n, (dst, src) in enumerate(pieces)]
    for load in loads:
        load.start()
    seq, head_at = lax.axis_index("seq"), lax.axis_index("head")

    barrier = pltpu.get_barrier_semaphore()
    partners = [(seq, (head_at + k) % n_head) for k in range(1, n_head)]
    partners += [((seq + k) % n_seq, head_at) for k in range(1, n_seq)]
    for partner in partners:
        pl.semaphore_signal(barrier, inc=1, device_id=partner, device_id_type=MESH)
    pl.semaphore_wait(barrier, len(partners))
    first_z, last_z = head_at == 0, head_at == n_head - 1
    to_left = remote(
        send_left, from_right, halo_sem.at[0], halo_sem.at[1], seq, (head_at + n_head - 1) % n_head
    )
    to_right = remote(send_right, from_left, halo_sem.at[2], halo_sem.at[3], seq, (head_at + 1) % n_head)

    for side_ref, side, absent, copy, waits in (
        (send_left, sides[0], first_z, to_left, loads[:4]),
        (send_right, sides[1], last_z, to_right, loads[4:6]),
    ):
        for load in waits:
            load.wait()

        def edge(index, carry):
            part = span(index, 256)
            side_ref[part, :] = (
                dot(wk_ref[part, :], dk_ref[:, side], NN) + dot(wve_ref[part, :], dv_ref[:, side], NN)
            ).astype(BF16)
            return carry

        lax.fori_loop(0, width // 256, edge, 0)
        pl.when(jnp.logical_not(absent))(copy.start)

    places, depth = pack((rank, width, rank, width))
    z_slots[head_at] = jnp.zeros_like(z_slots[0])
    for load in loads[6:10]:
        load.wait()

    for value in (False, True):
        scale_row, bias = (value_scale, value_bias) if value else (query_scale, query_bias)
        factor = 1.0 if value else QUERY_FOLD
        scale_at, bias_at = places[2 * value], places[2 * value + 1]

        if value:
            for load in loads[10:13]:
                load.wait()

        def outer(index, carry):
            part = span(index, 256)
            if value:
                total = dot(xt_ref[part, :], dv_ref[:, own], NT)
                total += dot(lt_ref[part, :], dv_ref[:, :SEQ_MOST], NT)
                total += dot(rt_ref[part, :], dv_ref[:, SEQ_MOST + rows :], NT)
            else:
                total = dot(xt_ref[part, :], dq_ref[...], NT)
            mix_ref[part, :] = total.astype(BF16)
            return carry

        lax.fori_loop(0, width // 256, outer, 0)
        bias_sum = jnp.zeros((1, width), F32)
        for at in range(0, rank, 256):
            part = slice(at, at + 256)
            mixed = dot(down_ref[:, part], mix_ref[...], TN) * up_ref[part, :].astype(F32) * factor
            scale = jnp.broadcast_to(scale_row[:, part], (LANES, 256)).T[:, :1]
            bias_sum += jnp.sum(mixed * scale, axis=0, keepdims=True)
            weighted = mixed * bias
            folded = weighted[:, :LANES]
            for lane in range(LANES, width, LANES):
                folded = folded + weighted[:, lane : lane + LANES]
            row, column = at // PACK, at % PACK
            z_slots[head_at, pl.ds(scale_at[row][0], 1), pl.ds(column, 256)] = jnp.sum(
                folded.T, axis=0, keepdims=True
            )
        for row, start, size in bias_at:
            z_slots[head_at, pl.ds(row, 1), pl.ds(0, size)] = bias_sum[:, start : start + size]

    def over_z(k):
        return remote(
            z_slots.at[head_at], z_slots.at[head_at], z_sem.at[2 * k], z_sem.at[2 * k + 1],
            seq, (head_at + k) % n_head,
        )

    def over_seq(k):
        return remote(
            s_slots.at[seq], s_slots.at[seq], s_sem.at[2 * k], s_sem.at[2 * k + 1],
            (seq + k) % n_seq, head_at,
        )

    for k in range(1, n_head):
        over_z(k).start()
    for load in loads[13:]:
        load.wait()

    def tokens_part(index, carry):
        part = span(index, 256)
        own_ref[part, :] = (
            gf_ref[part, :]
            + dot(wqe_ref[part, :], dq_ref[...], NN)
            + dot(wk_ref[part, :], dk_ref[:, own], NN)
            + dot(wve_ref[part, :], dv_ref[:, own], NN)
        )
        return carry

    lax.fori_loop(0, width // 256, tokens_part, 0)
    for k in range(1, n_head):
        over_z(k).wait_recv()
    total = z_slots[0]
    for k in range(1, n_head):
        total = total + z_slots[k]
    s_slots[seq] = total
    for k in range(1, n_seq):
        over_seq(k).start()

    out = pltpu.make_async_copy(own_ref, own_hbm, load_sem.at[len(pieces)])
    out.start()
    for k in range(1, n_seq):
        over_seq(k).wait_recv()
    total = s_slots[0]
    for k in range(1, n_seq):
        total = total + s_slots[k]
    sum_ref[...] = total
    for absent, back, copy in ((first_z, to_right, to_left), (last_z, to_left, to_right)):

        @pl.when(jnp.logical_not(absent))
        def _():
            back.wait_recv()
            copy.wait_send()

    out.wait()
    for k in range(1, n_head):
        over_z(k).wait_send()
    for k in range(1, n_seq):
        over_seq(k).wait_send()


def finish_kernel(n_head, own_ref, left_ref, right_ref, sum_ref, out_ref, *vector_refs):
    tile, half = pl.program_id(0), pl.num_programs(0) // 2
    first_z = lax.axis_index("head") == 0
    last_z = lax.axis_index("head") == n_head - 1
    left = jnp.where(first_z, 0.0, left_ref[...].astype(F32))
    right = jnp.where(last_z, 0.0, right_ref[...].astype(F32))
    total = own_ref[...] + jnp.where(tile < half, left, right)
    out_ref[...] = total.T.astype(BF16)

    @pl.when(tile == 0)
    def _():
        places, _ = pack([ref.shape[0] for ref in vector_refs])
        for vector_ref, place in zip(vector_refs, places):
            for row, start, size in place:
                vector_ref[start : start + size] = sum_ref[row, :size]


def call(kernel, outs, count, scratch=(), scalars=0):
    return pl.pallas_call(
        kernel,
        out_shape=outs,
        in_specs=[SMEM] * scalars + [VMEM] * count,
        out_specs=[VMEM] * len(outs),
        scratch_shapes=list(scratch),
        compiler_params=PARAMS,
    )


def front(n_head, n_seq, lengths, tokens, w_query, w_key, w_value, vera, shards):
    rows, width = tokens.shape
    heads = width // HEAD_DIM
    extent = rows + 2 * SEQ_MOST
    tall, wide = sds((width, rows), BF16), sds((width, extent), BF16)
    square, half = sds((width, width), BF16), sds((width, SEQ_MOST), BF16)
    kept = [tall, wide, wide, tall, half, half, square, square]
    outs = [tall, sds((heads, 1, rows), F32)] + kept
    big = (tokens, vera[0], vera[1], w_query, w_value, w_key)
    scratch = [pltpu.VMEM(a.shape, a.dtype) for a in (*big, *kept)] + [
        pltpu.VMEM((SEQ_MOST, width), BF16),
        pltpu.VMEM((SEQ_MOST, width), BF16),
        pltpu.VMEM((width, rows), F32),
        pltpu.VMEM((heads, 1, rows), F32),
        pltpu.VMEM((heads, 1, rows), F32),
        pltpu.VMEM((1, rows), jnp.int32),
        pltpu.VMEM((1, rows), jnp.int32),
        pltpu.VMEM((TILE_K, TILE_Q), F32),
        pltpu.SemaphoreType.DMA((len(big),)),
        pltpu.SemaphoreType.DMA((len(kept),)),
        pltpu.SemaphoreType.DMA((4,)),
    ]
    gather = len(shards) > 0
    specs = [VMEM] * 2 + [ANY] * len(kept)
    if gather:
        shard = shards[0].shape[0]
        outs.append(sds((2, n_head * n_seq * shard, width), BF16))
        specs.append(ANY)
        scratch += [pltpu.VMEM((2, shard, width), BF16), pltpu.SemaphoreType.DMA((182,))]
    return pl.pallas_call(
        functools.partial(front_kernel, n_head, n_seq, gather),
        out_shape=outs,
        in_specs=[ANY] * len(big) + [SMEM] + [VMEM] * (4 + len(shards)),
        out_specs=specs,
        scratch_shapes=scratch,
        compiler_params=pltpu.CompilerParams(
            vmem_limit_bytes=58 << 20, collective_id=0, has_side_effects=True
        ),
    )(*big, lengths, *vera[2:], *shards)


def feed(xt, ct, cotangent, w_output, weights):
    width, rows = xt.shape
    hidden = weights.shape[1]
    heads = width // HEAD_DIM
    tile, step = 512, 768
    column = pl.BlockSpec((width, tile), lambda i: (0, i))
    row = pl.BlockSpec((tile, width), lambda i: (i, 0))
    return pl.pallas_call(
        feed_kernel,
        grid=(rows // tile,),
        out_shape=[
            sds((rows, width), BF16), sds((width, rows), F32), sds((width, rows), BF16),
            sds((heads, 1, rows), F32),
        ],
        in_specs=[column, column, row, VMEM, VMEM],
        out_specs=[row, column, column, pl.BlockSpec((heads, 1, tile), lambda i: (0, 0, i))],
        scratch_shapes=[
            pltpu.VMEM((width, tile), F32),
            pltpu.VMEM((width, tile), BF16),
            pltpu.VMEM((hidden, tile), F32),
            pltpu.VMEM((width, tile), F32),
            pltpu.VMEM((2, step, tile), BF16),
            pltpu.VMEM((2, step, tile), F32),
        ],
        compiler_params=PARAMS,
    )(xt, ct, cotangent, w_output, weights)


def attend_back(lengths, qt, ke, ve, ls, gc, dl):
    width, rows = qt.shape
    extent = ke.shape[1]
    wide = sds((width, extent), BF16)
    return call(
        attend_back_kernel,
        [sds((width, rows), BF16), wide, wide],
        6,
        [
            pltpu.VMEM((width, TILE_Q), F32),
            pltpu.VMEM((width, extent), F32),
            pltpu.VMEM((width, extent), F32),
            pltpu.VMEM((TILE_K, TILE_Q), F32),
        ],
        1,
    )(lengths, qt, ke, ve, ls, gc, dl)


def tail(n_head, n_seq, big, small):
    dq, up = big[5], big[9]
    width, rows = dq.shape
    rank = up.shape[0]
    sizes = (rank, width, rank, width)
    depth = -(-pack(sizes)[1] // 8) * 8
    half = sds((width, SEQ_MOST), BF16)
    outs = [sds((width, rows), F32), half, half, sds((depth, PACK), F32)]
    own, left, right, total = pl.pallas_call(
        functools.partial(tail_kernel, n_head, n_seq),
        out_shape=outs,
        in_specs=[ANY] * len(big) + [VMEM] * len(small),
        out_specs=[ANY] * 3 + [VMEM],
        scratch_shapes=[pltpu.VMEM(a.shape, a.dtype) for a in big]
        + [
            pltpu.SemaphoreType.DMA((17,)),
            pltpu.VMEM((width, rows), F32),
            pltpu.VMEM((width, width), BF16),
            pltpu.VMEM(half.shape, BF16),
            pltpu.VMEM(half.shape, BF16),
            pltpu.SemaphoreType.DMA((4,)),
            pltpu.VMEM((n_head, depth, PACK), F32),
            pltpu.VMEM((n_seq, depth, PACK), F32),
            pltpu.SemaphoreType.DMA((2 * n_head,)),
            pltpu.SemaphoreType.DMA((2 * n_seq,)),
        ],
        compiler_params=pltpu.CompilerParams(
            vmem_limit_bytes=58 << 20, collective_id=1, has_side_effects=True
        ),
    )(*big, *small)
    tile = 256
    edge = SEQ_MOST // tile
    away = rows // tile - edge
    return pl.pallas_call(
        functools.partial(finish_kernel, n_head),
        grid=(rows // tile,),
        out_shape=[sds((rows, width), BF16)] + [sds((size,), F32) for size in sizes],
        in_specs=[
            pl.BlockSpec((width, tile), lambda i: (0, i)),
            pl.BlockSpec((width, tile), lambda i: (0, jnp.minimum(i, edge - 1))),
            pl.BlockSpec((width, tile), lambda i: (0, jnp.maximum(i - away, 0))),
            VMEM,
        ],
        out_specs=[pl.BlockSpec((tile, width), lambda i: (i, 0))] + [VMEM] * 4,
        compiler_params=PARAMS,
    )(own, left, right, total)


def body(n_seq, n_head, *arrays):
    (
        tokens, lengths, cotangent, w_query, w_key, w_value, w_output, vera_down, vera_up,
        query_scale, query_bias, value_scale, value_bias, hidden_in, hidden_out,
    ) = arrays
    rows, width = tokens.shape
    vera = (vera_down, vera_up, query_scale, query_bias, value_scale, value_bias)
    fused = (n_seq, n_head) == (8, 4)
    shards = (hidden_in.T, hidden_out.T) if fused else ()
    ct, ls, qt, ke, ve, xt, lt, rt, wqe, wve, *full = front(
        n_head, n_seq, lengths, tokens, w_query, w_key, w_value, vera, shards
    )
    if fused:
        (weights,) = full
    else:
        weights = lax.all_gather(
            jnp.stack([hidden_in.T, hidden_out.T]), ("seq", "head"), axis=1, tiled=True
        )
    layer_out, gf, gc, dl = feed(xt, ct, cotangent, w_output, weights)
    dq, dk, dv = attend_back(lengths, qt, ke, ve, ls, gc, dl)
    token_grad, *totals = tail(
        n_head, n_seq, (dk, dv, w_key, wve, xt, dq, lt, rt, vera_down, vera_up, wqe, gf), vera[2:]
    )
    return (layer_out, token_grad, *totals)


def solution(mesh):
    return jax.shard_map(
        functools.partial(body, mesh.shape["seq"], mesh.shape["head"]),
        mesh=mesh,
        in_specs=(
            P(("seq", "head"), None),
            P("seq", None),
            P(("seq", "head"), None),
            P(), P(), P(), P(), P(), P(), P(), P(), P(), P(),
            P(None, ("seq", "head")),
            P(None, ("seq", "head")),
        ),
        out_specs=(P(("seq", "head"), None), P(("seq", "head"), None), P(), P(), P(), P()),
        check_vma=False,
    )
```

```python
import functools
import math

import jax
import jax.numpy as jnp
from jax import lax
from jax.experimental import pallas as pl
from jax.experimental.pallas import tpu as pltpu
from jax.sharding import PartitionSpec as P

HEAD_DIM = 64
SEQ_MOST = 512
EPSILON = 1e-05
HIDDEN = -(2.0**100)
LN2 = math.log(2.0)
QUERY_FOLD = HEAD_DIM ** (-0.5) / LN2
TILE_Q = 256
TILE_K = 256
LANES = 128
PACK = 512
NN = (((1,), (0,)), ((), ()))
NT = (((1,), (1,)), ((), ()))
TN = (((0,), (0,)), ((), ()))
F32 = jnp.float32
BF16 = jnp.bfloat16
VMEM = pl.BlockSpec(memory_space=pltpu.VMEM)
SMEM = pl.BlockSpec(memory_space=pltpu.SMEM)
MESH = pl.DeviceIdType.MESH
ANY = pl.BlockSpec(memory_space=pl.ANY)
PARAMS = pltpu.CompilerParams(vmem_limit_bytes=58 << 20)


def dot(left, right, form):
    return lax.dot_general(left, right, form, preferred_element_type=F32)


def sds(shape, dtype):
    return jax.ShapeDtypeStruct(shape, dtype)


def span(index, size):
    if isinstance(index, int):
        return pl.ds(index * size, size)
    return pl.ds(pl.multiple_of(index * size, size), size)


def bounds(len_ref, first, count):
    row = first + lax.broadcasted_iota(jnp.int32, (1, count), 1)
    low = jnp.zeros((1, count), jnp.int32)
    high = jnp.full((1, count), 1 << 30, jnp.int32)
    end = 0
    for i in range(len_ref.shape[1]):
        end = end + len_ref[0, i]
        low = jnp.where(row >= end, end, low)
        high = jnp.where(row < end, jnp.minimum(high, end), high)
    return low, high


def fill_masks(len_ref, shift, query_mask, key_mask):
    for ref, first, within, outside in ((query_mask, shift + SEQ_MOST, HIDDEN, 0.0), (key_mask, shift, 0.0, 1.0)):
        row = first + lax.broadcasted_iota(jnp.int32, (1, ref.shape[1]), 1)
        end, pieces = 0, []
        for i in range(ref.shape[0]):
            start, end = end, end + len_ref[0, i]
            pieces.append(jnp.where((row >= start) & (row < end), within, outside))
        ref[...] = jnp.concatenate(pieces, axis=0).astype(BF16)


def reach(len_ref, first, count):
    last = first + count - 1
    end, least, most = 0, 0, 1 << 30
    for i in range(len_ref.shape[1]):
        end = end + len_ref[0, i]
        least = jnp.where(first >= end, end, least)
        most = jnp.where(last < end, jnp.minimum(most, end), most)
    return least, most


def key_range(least, most, shift, extent):
    start = (least - shift) // LANES
    tiles = (most - shift - start * LANES + TILE_K - 1) // TILE_K
    start = jnp.minimum(start, (extent - tiles * TILE_K) // LANES)
    return start, tiles


def other(index, bit):
    return index + bit - 2 * bit * ((index // bit) % 2)


def remote(src, dst, send, recv, seq, head):
    return pltpu.make_async_remote_copy(
        src_ref=src, dst_ref=dst, send_sem=send, recv_sem=recv, device_id=(seq, head), device_id_type=MESH
    )


class Gather:
    def __init__(self, own, full, sems, seq, head, n_head):
        self.own, self.full, self.sems = own, full, sems
        self.seq, self.head, self.n = seq, head, n_head
        self.shard = own.shape[1]
        self.near_x, self.near_y = other(seq, 2), other(seq, 4)
        self.groups = (seq, self.near_x, self.near_y, other(self.near_x, 4))

    def origin(self, way):
        return self.head - way if way < 4 else self.head + way - 3

    def there(self, way):
        return self.head >= way if way < 4 else self.head + way - 3 < self.n

    def rows(self, seq, origin):
        return self.full.at[:, span(seq * self.n + origin, self.shard), :]

    def source(self, way):
        return self.own if way == 0 else self.rows(self.seq, self.origin(way))

    def pair(self, kind, way):
        return self.sems.at[2 * (7 * kind + way)], self.sems.at[2 * (7 * kind + way) + 1]

    def local(self):
        return pltpu.make_async_copy(self.own, self.rows(self.seq, self.head), self.sems.at[0])

    def up(self, far):
        dst = self.rows(self.seq, self.head - far)
        return remote(self.source(far), dst, self.pair(8, far)[0], self.pair(0, far + 1)[1], self.seq, self.head + 1)

    def down(self, far):
        way = far + 3 if far else 0
        dst = self.rows(self.seq, self.head + far)
        return remote(self.source(way), dst, self.pair(8, far)[1], self.pair(0, far + 4)[1], self.seq, self.head - 1)

    def came_z(self, way):
        dst = self.rows(self.seq, self.origin(way))
        return remote(dst, dst, *self.pair(0, way), self.seq, self.head)

    def over_x(self, way):
        dst = self.rows(self.seq, self.origin(way))
        return remote(self.source(way), dst, *self.pair(1, way), self.near_x, self.head)

    def over_y(self, way):
        dst = self.rows(self.seq, self.origin(way))
        return remote(self.source(way), dst, *self.pair(2, way), self.near_y, self.head)

    def onward(self, way, half):
        src, to = ((self.near_x, self.near_y), (self.near_y, self.near_x))[half]
        part = self.rows(src, self.origin(way)).at[half]
        return remote(part, part, *self.pair(3 + half, way), to, self.head)

    def across(self, group, way):
        dst = self.rows(self.groups[group], self.origin(way))
        src = self.own if group == 0 and way == 0 else dst
        sems = self.sems.at[126 + 2 * (7 * group + way)], self.sems.at[127 + 2 * (7 * group + way)]
        return remote(src, dst, *sems, other(self.seq, 1), self.head)

    def slots(self, index):
        z = self.head
        return (
            ((0, None),),
            ((1, z > 0), (4, z == 0)),
            ((4, (z == 1) | (z == 2)), (5, z == 0), (2, z == 3)),
            ((6, z == 0), (5, z == 1), (2, z == 2), (3, z == 3)),
        )[index]

    def each(self, index, action):
        for way, chosen in self.slots(index):
            if chosen is None:
                action(way)
            else:
                pl.when(chosen)(functools.partial(action, way))

    def begin(self):
        pl.when(self.head < self.n - 1)(lambda: self.up(0).start())
        pl.when(self.head > 0)(lambda: self.down(0).start())
        self.local().start()
        self.spread(0)

    def take_z(self, far):
        def below():
            self.came_z(far).wait_recv()
            if far < self.n - 1:
                pl.when(self.head < self.n - 1)(lambda: self.up(far).start())

        def above():
            self.came_z(far + 3).wait_recv()
            if far < self.n - 1:
                pl.when(self.head > 0)(lambda: self.down(far).start())

        pl.when(self.there(far))(below)
        pl.when(self.there(far + 3))(above)

    def spread(self, index):
        def action(way):
            self.over_x(way).start()
            self.over_y(way).start()
            self.across(0, way).start()

        self.each(index, action)

    def take_xy(self, index):
        def action(way):
            self.over_x(way).wait_recv()
            self.onward(way, 0).start()
            self.over_y(way).wait_recv()
            self.onward(way, 1).start()
            self.across(1, way).start()
            self.across(2, way).start()

        self.each(index, action)

    def take_far(self, index):
        def action(way):
            self.onward(way, 0).wait_recv()
            self.onward(way, 1).wait_recv()
            self.across(3, way).start()

        self.each(index, action)

    def end(self):
        self.local().wait()
        for far in range(3):
            pl.when((self.head < self.n - 1) & (self.head >= far))(lambda: self.up(far).wait_send())
            pl.when((self.head > 0) & (self.head + far < self.n))(lambda: self.down(far).wait_send())
        for way in range(7):

            def action():
                self.over_x(way).wait_send()
                self.over_y(way).wait_send()
                self.onward(way, 0).wait_send()
                self.onward(way, 1).wait_send()
                for group in range(4):
                    copy = self.across(group, way)
                    copy.wait_send()
                    copy.wait_recv()

            if way == 0:
                action()
            else:
                pl.when(self.there(way))(action)


def front_kernel(n_head, n_seq, gather, *refs):
    big, refs = refs[:6], refs[6:]
    len_ref, vectors, refs = refs[0], refs[1:5], refs[5:]
    if gather:
        (hi_ref, ho_ref), refs = refs[:2], refs[2:]
    (ct_ref, ls_ref), refs = refs[:2], refs[2:]
    stored, refs = refs[:8], refs[8:]
    if gather:
        full_ref, refs = refs[0], refs[1:]
    held, refs = refs[:6], refs[6:]
    kept, refs = refs[:8], refs[8:]
    (
        xl_ref, xr_ref, acc_ref, high_ref, total_ref, query_mask, key_mask,
        load_sem, store_sem, halo_sem,
    ), refs = refs[:10], refs[10:]
    x_hbm = big[0]
    loads = [pltpu.make_async_copy(src, dst, load_sem.at[n]) for n, (src, dst) in enumerate(zip(big, held))]
    stores = [pltpu.make_async_copy(src, dst, store_sem.at[n]) for n, (src, dst) in enumerate(zip(kept, stored))]
    for n in (1, 2, 3, 4, 0, 5):
        loads[n].start()
    x_ref, down_ref, up_ref, wq_ref, wv_ref, wk_ref = held
    qt_ref, ke_ref, ve_ref, xt_ref, lt_ref, rt_ref, wqe_ref, wve_ref = kept
    rows, width = x_ref.shape
    heads = width // HEAD_DIM
    seq, head_at = lax.axis_index("seq"), lax.axis_index("head")
    shift = head_at * rows - SEQ_MOST
    first_z, last_z = head_at == 0, head_at == n_head - 1

    barrier = pltpu.get_barrier_semaphore()
    partners = [(seq, (head_at + k) % n_head) for k in range(1, n_head)]
    if gather:
        partners += [(other(seq, bit), head_at) for bit in (1, 2, 4)]
        own_ref, gather_sem = refs
        own_ref[0] = hi_ref[...]
        own_ref[1] = ho_ref[...]
    for partner in partners:
        pl.semaphore_signal(barrier, inc=1, device_id=partner, device_id_type=MESH)
    pl.semaphore_wait(barrier, len(partners))

    to_right = remote(
        x_hbm.at[rows - SEQ_MOST :], xl_ref, halo_sem.at[0], halo_sem.at[1], seq, (head_at + 1) % n_head
    )
    to_left = remote(
        x_hbm.at[:SEQ_MOST], xr_ref, halo_sem.at[2], halo_sem.at[3], seq, (head_at + n_head - 1) % n_head
    )

    def send_halo():
        pl.when(head_at < n_head - 1)(lambda: to_right.start())
        pl.when(head_at > 0)(lambda: to_left.start())

    if gather:
        g = Gather(own_ref, full_ref, gather_sem, seq, head_at, n_head)
        g.begin()
    else:
        send_halo()
    query_scale, query_bias, value_scale, value_bias = [ref[...].reshape(1, -1) for ref in vectors]
    for n in (1, 2, 3, 4):
        loads[n].wait()

    def fold(index, carry):
        part = span(index, 256)
        down = down_ref[part, :].astype(F32)
        side_q = dot((down * query_scale).astype(BF16), up_ref[...], NN) * query_bias
        wqe_ref[part, :] = ((wq_ref[part, :].astype(F32) + side_q) * QUERY_FOLD).astype(BF16)
        side_v = dot((down * value_scale).astype(BF16), up_ref[...], NN) * value_bias
        wve_ref[part, :] = (wv_ref[part, :].astype(F32) + side_v).astype(BF16)
        return carry

    lax.fori_loop(0, width // 256, fold, 0)
    stores[6].start()
    stores[7].start()
    loads[0].wait()

    def flip(index, carry):
        part = span(index, 256)
        xt_ref[:, part] = x_ref[part, :].T
        return carry

    lax.fori_loop(0, rows // 256, flip, 0)
    stores[3].start()
    own = slice(SEQ_MOST, SEQ_MOST + rows)

    def apply(weight_ref, out_ref, at):
        def piece(index, carry):
            part = span(index, 256)
            out_ref[part, at] = dot(weight_ref[:, part], xt_ref[...], TN).astype(BF16)
            return carry

        lax.fori_loop(0, width // 256, piece, 0)

    apply(wqe_ref, qt_ref, slice(0, rows))
    if gather:
        g.take_z(1)
        g.spread(1)
    loads[5].wait()
    stores[0].start()
    apply(wk_ref, ke_ref, own)
    apply(wve_ref, ve_ref, own)

    fill_masks(len_ref, shift, query_mask, key_mask)
    acc_ref[...] = jnp.zeros_like(acc_ref)
    high_ref[...] = jnp.full_like(high_ref, HIDDEN)
    total_ref[...] = jnp.zeros_like(total_ref)

    def block(tile, key_tile):
        q_part, k_part = span(tile, TILE_Q), span(key_tile, TILE_K)
        q_mask, k_mask = query_mask[:, q_part], key_mask[:, k_part]
        parts = [span(head, HEAD_DIM) for head in range(heads)]
        before = [high_ref[head, :, q_part] for head in range(heads)]
        totals = [total_ref[head, :, q_part] for head in range(heads)]
        sums = [acc_ref[part, q_part] for part in parts]
        scores = [
            dot(
                jnp.concatenate([ke_ref[part, k_part], k_mask]),
                jnp.concatenate([qt_ref[part, q_part], q_mask]),
                TN,
            )
            for part in parts
        ]
        best = [jnp.maximum(b, jnp.max(v, axis=0, keepdims=True)) for b, v in zip(before, scores)]
        probs = [jnp.exp2(v - b) for v, b in zip(scores, best)]
        fade = [jnp.exp2(a - b) for a, b in zip(before, best)]
        totals = [t * f + jnp.sum(p, axis=0, keepdims=True) for t, f, p in zip(totals, fade, probs)]
        sums = [
            a * f + dot(ve_ref[part, k_part], p.astype(BF16), NN)
            for a, f, p, part in zip(sums, fade, probs, parts)
        ]
        for head, part, b, t, a in zip(range(heads), parts, best, totals, sums):
            high_ref[head, :, q_part] = b
            total_ref[head, :, q_part] = t
            acc_ref[part, q_part] = a

    steps = {}
    if gather:
        steps = {
            0: lambda: (g.take_xy(0),),
            2: lambda: (g.take_z(2), g.spread(2),),
            4: lambda: (send_halo(), g.take_xy(1),),
            7: lambda: (g.take_z(3), g.spread(3), g.take_far(0),),
            10: lambda: (g.take_xy(2),),
            12: lambda: (g.take_far(1),),
            14: lambda: (g.take_xy(3),),
            16: lambda: (g.take_far(2),),
            18: lambda: (g.take_far(3),),
        }

    def blocks(first, last, place):
        def one(index, carry):
            for at in steps:
                if first <= at < last:

                    @pl.when(index == at)
                    def _():
                        steps[at]()

            block(*place(index))
            return carry

        lax.fori_loop(first, last, one, 0)

    def own_place(index):
        tile = (index + 1) // 4
        return tile, (index + 1) % 4 + 1 + (tile + 1) // 2

    blocks(0, 14, own_place)

    for absent, copy, side_ref, flat_ref, base in (
        (first_z, to_right, xl_ref, lt_ref, 0),
        (last_z, to_left, xr_ref, rt_ref, SEQ_MOST + rows),
    ):

        @pl.when(absent)
        def _():
            side_ref[...] = jnp.zeros_like(side_ref)

        @pl.when(jnp.logical_not(absent))
        def _():
            copy.wait_recv()

        def edge_flip(index, carry):
            part = span(index, 256)
            flat_ref[:, part] = side_ref[part, :].T
            return carry

        lax.fori_loop(0, SEQ_MOST // 256, edge_flip, 0)

        def edge(index, carry):
            part = span(index, 256)
            ke_ref[part, base : base + SEQ_MOST] = dot(wk_ref[:, part], flat_ref[...], TN).astype(BF16)
            ve_ref[part, base : base + SEQ_MOST] = dot(wve_ref[:, part], flat_ref[...], TN).astype(BF16)
            return carry

        lax.fori_loop(0, width // 256, edge, 0)

    for n in (1, 2, 4, 5):
        stores[n].start()
    blocks(14, 17, lambda index: ((index - 14) // 2, (index - 13) // 2))
    blocks(17, 20, lambda index: (2 + (index - 16) // 2, 6 + (index - 17) // 2))

    for head in range(heads):
        part = pl.ds(head * HEAD_DIM, HEAD_DIM)
        total = total_ref[head]
        ct_ref[part, :] = (acc_ref[part, :] / total).astype(BF16)
        ls_ref[head] = high_ref[head] + jnp.log2(total)

    pl.when(head_at < n_head - 1)(lambda: to_right.wait_send())
    pl.when(head_at > 0)(lambda: to_left.wait_send())
    for store in stores:
        store.wait()
    if gather:
        g.end()


def attend_back_kernel(
    len_ref, qt_hbm, ke_hbm, ve_hbm, ls_ref, gt_hbm, dl_ref,
    dq_hbm, dk_hbm, dv_hbm,
    qt_ref, ke_ref, ve_ref, gt_ref, dq_ref, dk_ref, dv_ref,
    dq_acc, dk_acc, dv_acc, bias_ref, load_sem, store_sem,
):
    width, rows = qt_ref.shape
    extent = ke_ref.shape[1]
    heads = width // HEAD_DIM
    shift = lax.axis_index("head") * rows - SEQ_MOST
    loads = [
        pltpu.make_async_copy(src, dst, load_sem.at[n])
        for n, (src, dst) in enumerate(((ke_hbm, ke_ref), (qt_hbm, qt_ref), (ve_hbm, ve_ref), (gt_hbm, gt_ref)))
    ]
    for load in loads:
        load.start()

    def store(kind, tile):
        src, dst = ((dq_ref, dq_hbm), (dk_ref, dk_hbm), (dv_ref, dv_hbm))[kind]
        part = span(tile, TILE_Q)
        return pltpu.make_async_copy(src.at[:, part], dst.at[:, part], store_sem.at[kind, tile])

    def settle(tile, carry):
        part = span(tile, TILE_Q)
        dk_ref[:, part] = (dk_acc[:, part] * LN2).astype(BF16)
        dv_ref[:, part] = dv_acc[:, part].astype(BF16)
        store(1, tile).start()
        store(2, tile).start()
        return carry

    dk_acc[...] = jnp.zeros_like(dk_acc)
    dv_acc[...] = jnp.zeros_like(dv_acc)
    for load in loads:
        load.wait()

    def query_tile(tile, carry):
        first = shift + SEQ_MOST + tile * TILE_Q
        low, high = bounds(len_ref, first, TILE_Q)
        least, most = reach(len_ref, first, TILE_Q)
        start, tiles = key_range(least, most, shift, extent)
        q_part = span(tile, TILE_Q)
        dq_acc[...] = jnp.zeros_like(dq_acc)

        def key_tile(step, inner):
            base = pl.multiple_of((start + step * (TILE_K // LANES)) * LANES, LANES)
            k_part = pl.ds(base, TILE_K)
            key = shift + base + lax.broadcasted_iota(jnp.int32, (TILE_K, TILE_Q), 0)
            bias_ref[...] = jnp.where((key >= low) & (key < high), 0.0, HIDDEN)

            def group(index):
                heads_of = [index * 6 + sub for sub in range(6)]
                parts = [span(head, HEAD_DIM) for head in heads_of]
                bias = bias_ref[...]
                scores = [dot(ke_ref[part, k_part], qt_ref[part, q_part], TN) + bias for part in parts]
                grad_probs = [dot(ve_ref[part, k_part], gt_ref[part, q_part], TN) for part in parts]
                probs = [jnp.exp2(v - ls_ref[head, :, q_part]) for head, v in zip(heads_of, scores)]
                slopes = [
                    (p * (g - dl_ref[head, :, q_part])).astype(BF16)
                    for head, p, g in zip(heads_of, probs, grad_probs)
                ]
                for part, p, d in zip(parts, probs, slopes):
                    dv_acc[part, k_part] += dot(gt_ref[part, q_part], p.astype(BF16), NT)
                    dk_acc[part, k_part] += dot(qt_ref[part, q_part], d, NT)
                    dq_acc[part, :] += dot(ke_ref[part, k_part], d, NN)

            for index in range(heads // 6):
                group(index)
            return inner

        lax.fori_loop(0, tiles, key_tile, 0)
        dq_ref[:, q_part] = (dq_acc[...] * LN2).astype(BF16)
        store(0, tile).start()
        settle(tile, 0)
        return carry

    def drain(tile, carry):
        store(1, tile).wait()
        store(2, tile).wait()
        return carry

    lax.fori_loop(0, rows // TILE_Q, query_tile, 0)
    lax.fori_loop(rows // TILE_Q, extent // TILE_Q, settle, 0)
    for tile in range(rows // TILE_Q):
        store(0, tile).wait()
    lax.fori_loop(0, extent // TILE_Q, drain, 0)


def norm(values):
    center = values - jnp.mean(values, axis=0, keepdims=True)
    inverse = lax.rsqrt(jnp.mean(center * center, axis=0, keepdims=True) + EPSILON)
    return center * inverse, inverse


def norm_back(gradient, normed, inverse):
    centered = gradient - jnp.mean(gradient, axis=0, keepdims=True)
    return inverse * (centered - normed * jnp.mean(gradient * normed, axis=0, keepdims=True))


def gelu_parts(x):
    bell = jnp.exp2((-0.5 / LN2) * (x * x))
    t = 1.0 / (1.0 + (0.3275911 * math.sqrt(0.5)) * jnp.abs(x))
    poly = t * (0.127414796 + t * (-0.142248368 + t * (0.710706870 + t * (-0.726576013 + t * 0.530702714))))
    tail = poly * bell
    normal = jnp.where(x >= 0, 1.0 - tail, tail)
    return x * normal, normal + x * (bell * (1.0 / math.sqrt(2.0 * math.pi)))


def feed_kernel(
    xt_ref, ct_ref, cot_ref, wo_ref, w_ref,
    out_ref, gf_ref, gc_ref, dl_ref,
    normed_ref, low_ref, slope_ref, sum_ref, act_ref, pre_ref,
):
    width = xt_ref.shape[0]
    hidden = w_ref.shape[1]
    step = act_ref.shape[1]
    heads = width // HEAD_DIM
    pieces = [pl.ds(at, step) for at in range(0, hidden, step)]

    def sweep(first, second, change):
        count = len(pieces)
        pre_ref[0] = dot(w_ref[first, pieces[0], :], low_ref[...], NN)
        for at in range(count):
            if at + 1 < count:
                pre_ref[(at + 1) % 2] = dot(w_ref[first, pieces[at + 1], :], low_ref[...], NN)
            act_ref[at % 2] = change(pieces[at], pre_ref[at % 2]).astype(BF16)
            if at > 0:
                sum_ref[...] += dot(w_ref[second, pieces[at - 1], :], act_ref[(at - 1) % 2], TN)
        sum_ref[...] += dot(w_ref[second, pieces[-1], :], act_ref[(count - 1) % 2], TN)

    def forward(piece, pre):
        act, slope = gelu_parts(pre)
        slope_ref[piece, :] = slope
        return act

    attended = dot(wo_ref[...], ct_ref[...], TN)
    normed, inverse_first = norm(xt_ref[...].astype(F32) + attended)
    normed_ref[...] = normed
    low_ref[...] = normed.astype(BF16)
    sum_ref[...] = normed
    sweep(0, 1, forward)
    layer_out, inverse_second = norm(sum_ref[...])
    out_ref[...] = layer_out.T.astype(BF16)
    grad = norm_back(cot_ref[...].astype(F32).T, layer_out, inverse_second)
    sum_ref[...] = grad
    low_ref[...] = grad.astype(BF16)
    sweep(1, 0, lambda piece, upstream: slope_ref[piece, :] * upstream)
    grad_first = norm_back(sum_ref[...], normed_ref[...], inverse_first)
    gf_ref[...] = grad_first
    grad_context = dot(wo_ref[...], grad_first.astype(BF16), NN).astype(BF16)
    gc_ref[...] = grad_context
    product = grad_context.astype(F32) * ct_ref[...].astype(F32)
    for head in range(heads):
        dl_ref[head] = jnp.sum(
            product[head * HEAD_DIM : (head + 1) * HEAD_DIM], axis=0, keepdims=True
        )


def pack(rows):
    places, at = [], 0
    for size in rows:
        places.append([(at + n, n * PACK, min(PACK, size - n * PACK)) for n in range(-(-size // PACK))])
        at += len(places[-1])
    return places, at


def tail_kernel(n_head, n_seq, *refs):
    big, refs = refs[:12], refs[12:]
    vectors, refs = refs[:4], refs[4:]
    query_scale, query_bias, value_scale, value_bias = [ref[...].reshape(1, -1) for ref in vectors]
    (own_hbm, from_left, from_right, sum_ref), refs = refs[:4], refs[4:]
    held, refs = refs[:12], refs[12:]
    (
        load_sem, own_ref, mix_ref, send_left, send_right, halo_sem, z_slots, s_slots, z_sem, s_sem,
    ) = refs
    dk_ref, dv_ref, wk_ref, wve_ref, xt_ref, dq_ref, lt_ref, rt_ref, down_ref, up_ref, wqe_ref, gf_ref = held
    width, rows = dq_ref.shape
    rank = up_ref.shape[0]
    own = slice(SEQ_MOST, SEQ_MOST + rows)
    sides = (slice(0, SEQ_MOST), slice(SEQ_MOST + rows, 2 * SEQ_MOST + rows))
    pieces = [(wk_ref, big[2]), (wve_ref, big[3])]
    pieces += [(ref.at[:, side], hbm.at[:, side]) for side in sides for ref, hbm in zip(held[:2], big[:2])]
    pieces += [(dq_ref, big[5]), (xt_ref, big[4]), (down_ref, big[8]), (up_ref, big[9])]
    pieces += [(lt_ref, big[6]), (rt_ref, big[7]), (dv_ref.at[:, own], big[1].at[:, own])]
    pieces += [(dk_ref.at[:, own], big[0].at[:, own]), (wqe_ref, big[10]), (gf_ref, big[11])]
    loads = [pltpu.make_async_copy(src, dst, load_sem.at[n]) for n, (dst, src) in enumerate(pieces)]
    for load in loads[:6]:
        load.start()
    seq, head_at = lax.axis_index("seq"), lax.axis_index("head")

    barrier = pltpu.get_barrier_semaphore()
    partners = [(seq, (head_at + k) % n_head) for k in range(1, n_head)]
    partners += [((seq + k) % n_seq, head_at) for k in range(1, n_seq)]
    for partner in partners:
        pl.semaphore_signal(barrier, inc=1, device_id=partner, device_id_type=MESH)
    pl.semaphore_wait(barrier, len(partners))
    first_z, last_z = head_at == 0, head_at == n_head - 1

    def to_left(piece):
        part = span(piece, 256)
        sems = halo_sem.at[2 * piece], halo_sem.at[2 * piece + 1]
        return remote(send_left.at[part], from_right.at[part], *sems, seq, (head_at + n_head - 1) % n_head)

    def to_right(piece):
        part = span(piece, 256)
        piece += width // 256
        sems = halo_sem.at[2 * piece], halo_sem.at[2 * piece + 1]
        return remote(send_right.at[part], from_left.at[part], *sems, seq, (head_at + 1) % n_head)

    for load in loads[:6]:
        load.wait()
    for load in loads[6:]:
        load.start()
    for piece in range(width // 256):
        part = span(piece, 256)
        for side_ref, side, absent, copy in (
            (send_left, sides[0], first_z, to_left(piece)),
            (send_right, sides[1], last_z, to_right(piece)),
        ):
            side_ref[part, :] = (
                dot(wk_ref[part, :], dk_ref[:, side], NN) + dot(wve_ref[part, :], dv_ref[:, side], NN)
            ).astype(BF16)
            pl.when(jnp.logical_not(absent))(copy.start)

    places, depth = pack((rank, width, rank, width))
    s_slots[seq] = jnp.zeros_like(s_slots[0])
    for load in loads[6:10]:
        load.wait()

    for value in (False, True):
        scale_row, bias = (value_scale, value_bias) if value else (query_scale, query_bias)
        factor = 1.0 if value else QUERY_FOLD
        scale_at, bias_at = places[2 * value], places[2 * value + 1]

        if value:
            for load in loads[10:13]:
                load.wait()

        def outer(index, carry):
            part = span(index, 256)
            if value:
                total = dot(xt_ref[part, :], dv_ref[:, own], NT)
                total += dot(lt_ref[part, :], dv_ref[:, :SEQ_MOST], NT)
                total += dot(rt_ref[part, :], dv_ref[:, SEQ_MOST + rows :], NT)
            else:
                total = dot(xt_ref[part, :], dq_ref[...], NT)
            mix_ref[part, :] = total.astype(BF16)
            return carry

        lax.fori_loop(0, width // 256, outer, 0)
        bias_sum = jnp.zeros((1, width), F32)
        for at in range(0, rank, 256):
            part = slice(at, at + 256)
            mixed = dot(down_ref[:, part], mix_ref[...], TN) * up_ref[part, :].astype(F32) * factor
            scale = jnp.broadcast_to(scale_row[:, part], (LANES, 256)).T[:, :1]
            bias_sum += jnp.sum(mixed * scale, axis=0, keepdims=True)
            weighted = mixed * bias
            folded = weighted[:, :LANES]
            for lane in range(LANES, width, LANES):
                folded = folded + weighted[:, lane : lane + LANES]
            row, column = at // PACK, at % PACK
            s_slots[seq, pl.ds(scale_at[row][0], 1), pl.ds(column, 256)] = jnp.sum(
                folded.T, axis=0, keepdims=True
            )
        for row, start, size in bias_at:
            s_slots[seq, pl.ds(row, 1), pl.ds(0, size)] = bias_sum[:, start : start + size]

    def over_z(k):
        return remote(
            z_slots.at[head_at], z_slots.at[head_at], z_sem.at[2 * k], z_sem.at[2 * k + 1],
            seq, (head_at + k) % n_head,
        )

    def over_seq(k):
        return remote(
            s_slots.at[seq], s_slots.at[seq], s_sem.at[2 * k], s_sem.at[2 * k + 1],
            (seq + k) % n_seq, head_at,
        )

    for k in range(1, n_seq):
        over_seq(k).start()
    for load in loads[13:]:
        load.wait()

    def tokens_part(index, carry):
        part = span(index, 256)
        own_ref[part, :] = (
            gf_ref[part, :]
            + dot(wqe_ref[part, :], dq_ref[...], NN)
            + dot(wk_ref[part, :], dk_ref[:, own], NN)
            + dot(wve_ref[part, :], dv_ref[:, own], NN)
        )
        return carry

    lax.fori_loop(0, width // 256, tokens_part, 0)
    for k in range(1, n_seq):
        over_seq(k).wait_recv()
    total = s_slots[0]
    for k in range(1, n_seq):
        total = total + s_slots[k]
    z_slots[head_at] = total
    for k in range(1, n_head):
        over_z(k).start()

    out = pltpu.make_async_copy(own_ref, own_hbm, load_sem.at[len(pieces)])
    out.start()
    for k in range(1, n_head):
        over_z(k).wait_recv()
    total = z_slots[0]
    for k in range(1, n_head):
        total = total + z_slots[k]
    sum_ref[...] = total
    for absent, back, copy in ((first_z, to_right, to_left), (last_z, to_left, to_right)):

        @pl.when(jnp.logical_not(absent))
        def _():
            for piece in range(width // 256):
                back(piece).wait_recv()
                copy(piece).wait_send()

    out.wait()
    for k in range(1, n_head):
        over_z(k).wait_send()
    for k in range(1, n_seq):
        over_seq(k).wait_send()


def finish_kernel(n_head, own_ref, left_ref, right_ref, sum_ref, out_ref, *vector_refs):
    tile, half = pl.program_id(0), pl.num_programs(0) // 2
    first_z = lax.axis_index("head") == 0
    last_z = lax.axis_index("head") == n_head - 1
    left = jnp.where(first_z, 0.0, left_ref[...].astype(F32))
    right = jnp.where(last_z, 0.0, right_ref[...].astype(F32))
    total = own_ref[...] + jnp.where(tile < half, left, right)
    out_ref[...] = total.T.astype(BF16)

    @pl.when(tile == 0)
    def _():
        places, _ = pack([ref.shape[0] for ref in vector_refs])
        for vector_ref, place in zip(vector_refs, places):
            for row, start, size in place:
                vector_ref[start : start + size] = sum_ref[row, :size]


def call(kernel, outs, count, scratch=(), scalars=0):
    return pl.pallas_call(
        kernel,
        out_shape=outs,
        in_specs=[SMEM] * scalars + [VMEM] * count,
        out_specs=[VMEM] * len(outs),
        scratch_shapes=list(scratch),
        compiler_params=PARAMS,
    )


def front(n_head, n_seq, lengths, tokens, w_query, w_key, w_value, vera, shards):
    rows, width = tokens.shape
    heads = width // HEAD_DIM
    extent = rows + 2 * SEQ_MOST
    tall, wide = sds((width, rows), BF16), sds((width, extent), BF16)
    square, half = sds((width, width), BF16), sds((width, SEQ_MOST), BF16)
    kept = [tall, wide, wide, tall, half, half, square, square]
    outs = [tall, sds((heads, 1, rows), F32)] + kept
    big = (tokens, vera[0], vera[1], w_query, w_value, w_key)
    scratch = [pltpu.VMEM(a.shape, a.dtype) for a in (*big, *kept)] + [
        pltpu.VMEM((SEQ_MOST, width), BF16),
        pltpu.VMEM((SEQ_MOST, width), BF16),
        pltpu.VMEM((width, rows), F32),
        pltpu.VMEM((heads, 1, rows), F32),
        pltpu.VMEM((heads, 1, rows), F32),
        pltpu.VMEM((lengths.shape[1], rows), BF16),
        pltpu.VMEM((lengths.shape[1], extent), BF16),
        pltpu.SemaphoreType.DMA((len(big),)),
        pltpu.SemaphoreType.DMA((len(kept),)),
        pltpu.SemaphoreType.DMA((4,)),
    ]
    gather = len(shards) > 0
    specs = [VMEM] * 2 + [ANY] * len(kept)
    if gather:
        shard = shards[0].shape[0]
        outs.append(sds((2, n_head * n_seq * shard, width), BF16))
        specs.append(ANY)
        scratch += [pltpu.VMEM((2, shard, width), BF16), pltpu.SemaphoreType.DMA((182,))]
    return pl.pallas_call(
        functools.partial(front_kernel, n_head, n_seq, gather),
        out_shape=outs,
        in_specs=[ANY] * len(big) + [SMEM] + [VMEM] * (4 + len(shards)),
        out_specs=specs,
        scratch_shapes=scratch,
        compiler_params=pltpu.CompilerParams(
            vmem_limit_bytes=58 << 20, collective_id=0, has_side_effects=True
        ),
    )(*big, lengths, *vera[2:], *shards)


def feed(xt, ct, cotangent, w_output, weights):
    width, rows = xt.shape
    hidden = weights.shape[1]
    heads = width // HEAD_DIM
    tile, step = 512, 768
    column = pl.BlockSpec((width, tile), lambda i: (0, i))
    row = pl.BlockSpec((tile, width), lambda i: (i, 0))
    return pl.pallas_call(
        feed_kernel,
        grid=(rows // tile,),
        out_shape=[
            sds((rows, width), BF16), sds((width, rows), F32), sds((width, rows), BF16),
            sds((heads, 1, rows), F32),
        ],
        in_specs=[column, column, row, VMEM, VMEM],
        out_specs=[row, column, column, pl.BlockSpec((heads, 1, tile), lambda i: (0, 0, i))],
        scratch_shapes=[
            pltpu.VMEM((width, tile), F32),
            pltpu.VMEM((width, tile), BF16),
            pltpu.VMEM((hidden, tile), F32),
            pltpu.VMEM((width, tile), F32),
            pltpu.VMEM((2, step, tile), BF16),
            pltpu.VMEM((2, step, tile), F32),
        ],
        compiler_params=PARAMS,
    )(xt, ct, cotangent, w_output, weights)


def attend_back(lengths, qt, ke, ve, ls, gc, dl):
    width, rows = qt.shape
    extent = ke.shape[1]
    outs = [sds((width, rows), BF16), sds(ke.shape, BF16), sds(ke.shape, BF16)]
    return pl.pallas_call(
        attend_back_kernel,
        out_shape=outs,
        in_specs=[SMEM, ANY, ANY, ANY, VMEM, ANY, VMEM],
        out_specs=[ANY] * 3,
        scratch_shapes=[pltpu.VMEM(a.shape, BF16) for a in (qt, ke, ve, gc, *outs)]
        + [
            pltpu.VMEM((width, TILE_Q), F32),
            pltpu.VMEM((width, extent), F32),
            pltpu.VMEM((width, extent), F32),
            pltpu.VMEM((TILE_K, TILE_Q), F32),
            pltpu.SemaphoreType.DMA((4,)),
            pltpu.SemaphoreType.DMA((3, extent // TILE_Q)),
        ],
        compiler_params=PARAMS,
    )(lengths, qt, ke, ve, ls, gc, dl)


def tail(n_head, n_seq, big, small):
    dq, up = big[5], big[9]
    width, rows = dq.shape
    rank = up.shape[0]
    sizes = (rank, width, rank, width)
    depth = -(-pack(sizes)[1] // 8) * 8
    half = sds((width, SEQ_MOST), BF16)
    outs = [sds((width, rows), F32), half, half, sds((depth, PACK), F32)]
    own, left, right, total = pl.pallas_call(
        functools.partial(tail_kernel, n_head, n_seq),
        out_shape=outs,
        in_specs=[ANY] * len(big) + [VMEM] * len(small),
        out_specs=[ANY] * 3 + [VMEM],
        scratch_shapes=[pltpu.VMEM(a.shape, a.dtype) for a in big]
        + [
            pltpu.SemaphoreType.DMA((17,)),
            pltpu.VMEM((width, rows), F32),
            pltpu.VMEM((width, width), BF16),
            pltpu.VMEM(half.shape, BF16),
            pltpu.VMEM(half.shape, BF16),
            pltpu.SemaphoreType.DMA((4 * (width // 256),)),
            pltpu.VMEM((n_head, depth, PACK), F32),
            pltpu.VMEM((n_seq, depth, PACK), F32),
            pltpu.SemaphoreType.DMA((2 * n_head,)),
            pltpu.SemaphoreType.DMA((2 * n_seq,)),
        ],
        compiler_params=pltpu.CompilerParams(
            vmem_limit_bytes=58 << 20, collective_id=1, has_side_effects=True
        ),
    )(*big, *small)
    tile = 512
    edge = SEQ_MOST // tile
    away = rows // tile - edge
    return pl.pallas_call(
        functools.partial(finish_kernel, n_head),
        grid=(rows // tile,),
        out_shape=[sds((rows, width), BF16)] + [sds((size,), F32) for size in sizes],
        in_specs=[
            pl.BlockSpec((width, tile), lambda i: (0, i)),
            pl.BlockSpec((width, tile), lambda i: (0, jnp.minimum(i, edge - 1))),
            pl.BlockSpec((width, tile), lambda i: (0, jnp.maximum(i - away, 0))),
            VMEM,
        ],
        out_specs=[pl.BlockSpec((tile, width), lambda i: (i, 0))] + [VMEM] * 4,
        compiler_params=PARAMS,
    )(own, left, right, total)


def body(n_seq, n_head, *arrays):
    (
        tokens, lengths, cotangent, w_query, w_key, w_value, w_output, vera_down, vera_up,
        query_scale, query_bias, value_scale, value_bias, hidden_in, hidden_out,
    ) = arrays
    rows, width = tokens.shape
    vera = (vera_down, vera_up, query_scale, query_bias, value_scale, value_bias)
    fused = (n_seq, n_head) == (8, 4)
    shards = (hidden_in.T, hidden_out.T) if fused else ()
    ct, ls, qt, ke, ve, xt, lt, rt, wqe, wve, *full = front(
        n_head, n_seq, lengths, tokens, w_query, w_key, w_value, vera, shards
    )
    if fused:
        (weights,) = full
    else:
        weights = lax.all_gather(
            jnp.stack([hidden_in.T, hidden_out.T]), ("seq", "head"), axis=1, tiled=True
        )
    layer_out, gf, gc, dl = feed(xt, ct, cotangent, w_output, weights)
    dq, dk, dv = attend_back(lengths, qt, ke, ve, ls, gc, dl)
    token_grad, *totals = tail(
        n_head, n_seq, (dk, dv, w_key, wve, xt, dq, lt, rt, vera_down, vera_up, wqe, gf), vera[2:]
    )
    return (layer_out, token_grad, *totals)


def solution(mesh):
    return jax.shard_map(
        functools.partial(body, mesh.shape["seq"], mesh.shape["head"]),
        mesh=mesh,
        in_specs=(
            P(("seq", "head"), None),
            P("seq", None),
            P(("seq", "head"), None),
            P(), P(), P(), P(), P(), P(), P(), P(), P(), P(),
            P(None, ("seq", "head")),
            P(None, ("seq", "head")),
        ),
        out_specs=(P(("seq", "head"), None), P(("seq", "head"), None), P(), P(), P(), P()),
        check_vma=False,
    )
```

```python
import functools
import math

import jax
import jax.numpy as jnp
from jax import lax
from jax.experimental import pallas as pl
from jax.experimental.pallas import tpu as pltpu
from jax.sharding import PartitionSpec as P

HEAD_DIM = 64
SEQ_MOST = 512
EPSILON = 1e-05
HIDDEN = -(2.0**100)
LN2 = math.log(2.0)
QUERY_FOLD = HEAD_DIM ** (-0.5) / LN2
TILE_Q = 256
TILE_K = 256
LANES = 128
PACK = 512
NN = (((1,), (0,)), ((), ()))
NT = (((1,), (1,)), ((), ()))
TN = (((0,), (0,)), ((), ()))
F32 = jnp.float32
BF16 = jnp.bfloat16
VMEM = pl.BlockSpec(memory_space=pltpu.VMEM)
SMEM = pl.BlockSpec(memory_space=pltpu.SMEM)
MESH = pl.DeviceIdType.MESH
ANY = pl.BlockSpec(memory_space=pl.ANY)
PARAMS = pltpu.CompilerParams(vmem_limit_bytes=58 << 20)


def dot(left, right, form):
    return lax.dot_general(left, right, form, preferred_element_type=F32)


def sds(shape, dtype):
    return jax.ShapeDtypeStruct(shape, dtype)


def span(index, size):
    if isinstance(index, int):
        return pl.ds(index * size, size)
    return pl.ds(pl.multiple_of(index * size, size), size)


def bounds(len_ref, first, count):
    row = first + lax.broadcasted_iota(jnp.int32, (1, count), 1)
    low = jnp.zeros((1, count), jnp.int32)
    high = jnp.full((1, count), 1 << 30, jnp.int32)
    end = 0
    for i in range(len_ref.shape[1]):
        end = end + len_ref[0, i]
        low = jnp.where(row >= end, end, low)
        high = jnp.where(row < end, jnp.minimum(high, end), high)
    return low, high


def fill_masks(len_ref, shift, query_mask, key_mask):
    for ref, first, within, outside in ((query_mask, shift + SEQ_MOST, HIDDEN, 0.0), (key_mask, shift, 0.0, 1.0)):
        row = first + lax.broadcasted_iota(jnp.int32, (1, ref.shape[1]), 1)
        end, pieces = 0, []
        for i in range(ref.shape[0]):
            start, end = end, end + len_ref[0, i]
            pieces.append(jnp.where((row >= start) & (row < end), within, outside))
        ref[...] = jnp.concatenate(pieces, axis=0).astype(BF16)


def reach(len_ref, first, count):
    last = first + count - 1
    end, least, most = 0, 0, 1 << 30
    for i in range(len_ref.shape[1]):
        end = end + len_ref[0, i]
        least = jnp.where(first >= end, end, least)
        most = jnp.where(last < end, jnp.minimum(most, end), most)
    return least, most


def key_range(least, most, shift, extent):
    start = (least - shift) // LANES
    tiles = (most - shift - start * LANES + TILE_K - 1) // TILE_K
    start = jnp.minimum(start, (extent - tiles * TILE_K) // LANES)
    return start, tiles


def other(index, bit):
    return index + bit - 2 * bit * ((index // bit) % 2)


def remote(src, dst, send, recv, seq, head):
    return pltpu.make_async_remote_copy(
        src_ref=src, dst_ref=dst, send_sem=send, recv_sem=recv, device_id=(seq, head), device_id_type=MESH
    )


class Gather:
    def __init__(self, own, full, sems, seq, head, n_head):
        self.own, self.full, self.sems = own, full, sems
        self.seq, self.head, self.n = seq, head, n_head
        self.shard = own.shape[1]
        self.near_x, self.near_y = other(seq, 2), other(seq, 4)
        self.groups = (seq, self.near_x, self.near_y, other(self.near_x, 4))

    def origin(self, way):
        return self.head - way if way < 4 else self.head + way - 3

    def there(self, way):
        return self.head >= way if way < 4 else self.head + way - 3 < self.n

    def rows(self, seq, origin):
        return self.full.at[:, span(seq * self.n + origin, self.shard), :]

    def source(self, way):
        return self.own if way == 0 else self.rows(self.seq, self.origin(way))

    def pair(self, kind, way):
        return self.sems.at[2 * (7 * kind + way)], self.sems.at[2 * (7 * kind + way) + 1]

    def local(self):
        return pltpu.make_async_copy(self.own, self.rows(self.seq, self.head), self.sems.at[0])

    def up(self, far):
        dst = self.rows(self.seq, self.head - far)
        return remote(self.source(far), dst, self.pair(8, far)[0], self.pair(0, far + 1)[1], self.seq, self.head + 1)

    def down(self, far):
        way = far + 3 if far else 0
        dst = self.rows(self.seq, self.head + far)
        return remote(self.source(way), dst, self.pair(8, far)[1], self.pair(0, far + 4)[1], self.seq, self.head - 1)

    def came_z(self, way):
        dst = self.rows(self.seq, self.origin(way))
        return remote(dst, dst, *self.pair(0, way), self.seq, self.head)

    def over_x(self, way):
        dst = self.rows(self.seq, self.origin(way))
        return remote(self.source(way), dst, *self.pair(1, way), self.near_x, self.head)

    def over_y(self, way):
        dst = self.rows(self.seq, self.origin(way))
        return remote(self.source(way), dst, *self.pair(2, way), self.near_y, self.head)

    def onward(self, way, half):
        src, to = ((self.near_x, self.near_y), (self.near_y, self.near_x))[half]
        part = self.rows(src, self.origin(way)).at[half]
        return remote(part, part, *self.pair(3 + half, way), to, self.head)

    def across(self, group, way):
        dst = self.rows(self.groups[group], self.origin(way))
        src = self.own if group == 0 and way == 0 else dst
        sems = self.sems.at[126 + 2 * (7 * group + way)], self.sems.at[127 + 2 * (7 * group + way)]
        return remote(src, dst, *sems, other(self.seq, 1), self.head)

    def slots(self, index):
        z = self.head
        return (
            ((0, None),),
            ((1, z > 0), (4, z == 0)),
            ((4, (z == 1) | (z == 2)), (5, z == 0), (2, z == 3)),
            ((6, z == 0), (5, z == 1), (2, z == 2), (3, z == 3)),
        )[index]

    def each(self, index, action):
        for way, chosen in self.slots(index):
            if chosen is None:
                action(way)
            else:
                pl.when(chosen)(functools.partial(action, way))

    def begin(self):
        pl.when(self.head < self.n - 1)(lambda: self.up(0).start())
        pl.when(self.head > 0)(lambda: self.down(0).start())
        self.local().start()
        self.spread(0)

    def take_z(self, far):
        def below():
            self.came_z(far).wait_recv()
            if far < self.n - 1:
                pl.when(self.head < self.n - 1)(lambda: self.up(far).start())

        def above():
            self.came_z(far + 3).wait_recv()
            if far < self.n - 1:
                pl.when(self.head > 0)(lambda: self.down(far).start())

        pl.when(self.there(far))(below)
        pl.when(self.there(far + 3))(above)

    def spread(self, index):
        def action(way):
            self.over_x(way).start()
            self.over_y(way).start()
            self.across(0, way).start()

        self.each(index, action)

    def take_xy(self, index):
        def action(way):
            self.over_x(way).wait_recv()
            self.onward(way, 0).start()
            self.over_y(way).wait_recv()
            self.onward(way, 1).start()
            self.across(1, way).start()
            self.across(2, way).start()

        self.each(index, action)

    def take_far(self, index):
        def action(way):
            self.onward(way, 0).wait_recv()
            self.onward(way, 1).wait_recv()
            self.across(3, way).start()

        self.each(index, action)

    def end(self):
        self.local().wait()
        for far in range(3):
            pl.when((self.head < self.n - 1) & (self.head >= far))(lambda: self.up(far).wait_send())
            pl.when((self.head > 0) & (self.head + far < self.n))(lambda: self.down(far).wait_send())
        for way in range(7):

            def action():
                self.over_x(way).wait_send()
                self.over_y(way).wait_send()
                self.onward(way, 0).wait_send()
                self.onward(way, 1).wait_send()
                for group in range(4):
                    copy = self.across(group, way)
                    copy.wait_send()
                    copy.wait_recv()

            if way == 0:
                action()
            else:
                pl.when(self.there(way))(action)


def front_kernel(n_head, n_seq, gather, *refs):
    big, refs = refs[:6], refs[6:]
    len_ref, vectors, refs = refs[0], refs[1:5], refs[5:]
    if gather:
        (hi_ref, ho_ref), refs = refs[:2], refs[2:]
    (ct_ref, ls_ref), refs = refs[:2], refs[2:]
    stored, refs = refs[:8], refs[8:]
    if gather:
        full_ref, refs = refs[0], refs[1:]
    held, refs = refs[:6], refs[6:]
    kept, refs = refs[:8], refs[8:]
    (
        xl_ref, xr_ref, acc_ref, high_ref, total_ref, query_mask, key_mask,
        load_sem, store_sem, halo_sem,
    ), refs = refs[:10], refs[10:]
    x_hbm = big[0]
    loads = [pltpu.make_async_copy(src, dst, load_sem.at[n]) for n, (src, dst) in enumerate(zip(big, held))]
    stores = [pltpu.make_async_copy(src, dst, store_sem.at[n]) for n, (src, dst) in enumerate(zip(kept, stored))]
    for n in (1, 2, 3, 4, 0, 5):
        loads[n].start()
    x_ref, down_ref, up_ref, wq_ref, wv_ref, wk_ref = held
    qt_ref, ke_ref, ve_ref, xt_ref, lt_ref, rt_ref, wqe_ref, wve_ref = kept
    rows, width = x_ref.shape
    heads = width // HEAD_DIM
    seq, head_at = lax.axis_index("seq"), lax.axis_index("head")
    shift = head_at * rows - SEQ_MOST
    first_z, last_z = head_at == 0, head_at == n_head - 1

    barrier = pltpu.get_barrier_semaphore()
    partners = [(seq, (head_at + k) % n_head) for k in range(1, n_head)]
    if gather:
        partners += [(other(seq, bit), head_at) for bit in (1, 2, 4)]
        own_ref, gather_sem = refs
        own_ref[0] = hi_ref[...]
        own_ref[1] = ho_ref[...]
    for partner in partners:
        pl.semaphore_signal(barrier, inc=1, device_id=partner, device_id_type=MESH)
    pl.semaphore_wait(barrier, len(partners))

    half = SEQ_MOST // 2

    def to_right(far):
        at = 0 if far else half
        sems = halo_sem.at[4 * far], halo_sem.at[4 * far + 1]
        src = x_hbm.at[pl.ds(rows - SEQ_MOST + at, half)]
        return remote(src, xl_ref.at[pl.ds(at, half)], *sems, seq, (head_at + 1) % n_head)

    def to_left(far):
        at = half if far else 0
        sems = halo_sem.at[4 * far + 2], halo_sem.at[4 * far + 3]
        src = x_hbm.at[pl.ds(at, half)]
        return remote(src, xr_ref.at[pl.ds(at, half)], *sems, seq, (head_at + n_head - 1) % n_head)

    def send_halo(far):
        pl.when(head_at < n_head - 1)(lambda: to_right(far).start())
        pl.when(head_at > 0)(lambda: to_left(far).start())

    if gather:
        g = Gather(own_ref, full_ref, gather_sem, seq, head_at, n_head)
        g.begin()
    else:
        send_halo(0)
        send_halo(1)
    query_scale, query_bias, value_scale, value_bias = [ref[...].reshape(1, -1) for ref in vectors]
    for n in (1, 2, 3, 4):
        loads[n].wait()

    def fold(index, carry):
        part = span(index, 256)
        down = down_ref[part, :].astype(F32)
        side_q = dot((down * query_scale).astype(BF16), up_ref[...], NN) * query_bias
        wqe_ref[part, :] = ((wq_ref[part, :].astype(F32) + side_q) * QUERY_FOLD).astype(BF16)
        side_v = dot((down * value_scale).astype(BF16), up_ref[...], NN) * value_bias
        wve_ref[part, :] = (wv_ref[part, :].astype(F32) + side_v).astype(BF16)
        return carry

    lax.fori_loop(0, width // 256, fold, 0)
    stores[6].start()
    stores[7].start()
    loads[0].wait()

    def flip(index, carry):
        part = span(index, 256)
        xt_ref[:, part] = x_ref[part, :].T
        return carry

    lax.fori_loop(0, rows // 256, flip, 0)
    stores[3].start()
    own = slice(SEQ_MOST, SEQ_MOST + rows)

    def apply(weight_ref, out_ref, at):
        def piece(index, carry):
            part = span(index, 256)
            out_ref[part, at] = dot(weight_ref[:, part], xt_ref[...], TN).astype(BF16)
            return carry

        lax.fori_loop(0, width // 256, piece, 0)

    apply(wqe_ref, qt_ref, slice(0, rows))
    if gather:
        g.take_z(1)
        g.spread(1)
    loads[5].wait()
    stores[0].start()
    apply(wk_ref, ke_ref, own)
    apply(wve_ref, ve_ref, own)

    fill_masks(len_ref, shift, query_mask, key_mask)
    acc_ref[...] = jnp.zeros_like(acc_ref)
    high_ref[...] = jnp.full_like(high_ref, HIDDEN)
    total_ref[...] = jnp.zeros_like(total_ref)

    def block(tile, key_tile):
        q_part, k_part = span(tile, TILE_Q), span(key_tile, TILE_K)
        q_mask, k_mask = query_mask[:, q_part], key_mask[:, k_part]
        parts = [span(head, HEAD_DIM) for head in range(heads)]
        before = [high_ref[head, :, q_part] for head in range(heads)]
        totals = [total_ref[head, :, q_part] for head in range(heads)]
        sums = [acc_ref[part, q_part] for part in parts]
        scores = [
            dot(
                jnp.concatenate([ke_ref[part, k_part], k_mask]),
                jnp.concatenate([qt_ref[part, q_part], q_mask]),
                TN,
            )
            for part in parts
        ]
        best = [jnp.maximum(b, jnp.max(v, axis=0, keepdims=True)) for b, v in zip(before, scores)]
        probs = [jnp.exp2(v - b) for v, b in zip(scores, best)]
        fade = [jnp.exp2(a - b) for a, b in zip(before, best)]
        totals = [t * f + jnp.sum(p, axis=0, keepdims=True) for t, f, p in zip(totals, fade, probs)]
        sums = [
            a * f + dot(ve_ref[part, k_part], p.astype(BF16), NN)
            for a, f, p, part in zip(sums, fade, probs, parts)
        ]
        for head, part, b, t, a in zip(range(heads), parts, best, totals, sums):
            high_ref[head, :, q_part] = b
            total_ref[head, :, q_part] = t
            acc_ref[part, q_part] = a

    steps = {}
    if gather:
        steps = {
            0: lambda: (g.take_xy(0),),
            2: lambda: (g.take_z(2), g.spread(2),),
            3: lambda: (send_halo(0),),
            4: lambda: (g.take_xy(1),),
            7: lambda: (g.take_z(3), g.spread(3), g.take_far(0),),
            8: lambda: (send_halo(1),),
            10: lambda: (g.take_xy(2),),
            12: lambda: (g.take_far(1),),
            15: lambda: (g.take_xy(3),),
            16: lambda: (g.take_far(2),),
            19: lambda: (g.take_far(3),),
        }

    def blocks(first, last, place):
        def one(index, carry):
            for at in steps:
                if first <= at < last:

                    @pl.when(index == at)
                    def _():
                        steps[at]()

            block(*place(index))
            return carry

        lax.fori_loop(first, last, one, 0)

    def own_place(index):
        tile = (index + 1) // 4
        return tile, (index + 1) % 4 + 1 + (tile + 1) // 2

    blocks(0, 14, own_place)

    def take_halo(far):
        for absent, copy, side_ref, flat_ref, base, at in (
            (first_z, to_right(far), xl_ref, lt_ref, 0, 0 if far else half),
            (last_z, to_left(far), xr_ref, rt_ref, SEQ_MOST + rows, half if far else 0),
        ):
            piece, place = slice(at, at + half), slice(base + at, base + at + half)

            @pl.when(absent)
            def _():
                side_ref[piece, :] = jnp.zeros((half, width), BF16)

            pl.when(jnp.logical_not(absent))(copy.wait_recv)
            flat_ref[:, piece] = side_ref[piece, :].T

            def edge(index, carry):
                part = span(index, 256)
                ke_ref[part, place] = dot(wk_ref[:, part], flat_ref[:, piece], TN).astype(BF16)
                ve_ref[part, place] = dot(wve_ref[:, part], flat_ref[:, piece], TN).astype(BF16)
                return carry

            lax.fori_loop(0, width // 256, edge, 0)

    take_halo(0)
    blocks(14, 18, lambda index: (index - 14, 1 + 5 * ((index - 14) // 2)))
    take_halo(1)
    for n in (1, 2, 4, 5):
        stores[n].start()
    blocks(18, 20, lambda index: (3 * (index - 18), 7 * (index - 18)))

    for head in range(heads):
        part = pl.ds(head * HEAD_DIM, HEAD_DIM)
        total = total_ref[head]
        ct_ref[part, :] = (acc_ref[part, :] / total).astype(BF16)
        ls_ref[head] = high_ref[head] + jnp.log2(total)

    for far in range(2):
        pl.when(head_at < n_head - 1)(to_right(far).wait_send)
        pl.when(head_at > 0)(to_left(far).wait_send)
    for store in stores:
        store.wait()
    if gather:
        g.end()


def attend_back_kernel(
    len_ref, qt_hbm, ke_hbm, ve_hbm, ls_ref, gt_hbm, dl_ref,
    dq_hbm, dk_hbm, dv_hbm,
    qt_ref, ke_ref, ve_ref, gt_ref, dq_ref, dk_ref, dv_ref,
    dq_acc, dk_acc, dv_acc, bias_ref, load_sem, store_sem,
):
    width, rows = qt_ref.shape
    extent = ke_ref.shape[1]
    heads = width // HEAD_DIM
    shift = lax.axis_index("head") * rows - SEQ_MOST
    loads = [
        pltpu.make_async_copy(src, dst, load_sem.at[n])
        for n, (src, dst) in enumerate(((ke_hbm, ke_ref), (qt_hbm, qt_ref), (ve_hbm, ve_ref), (gt_hbm, gt_ref)))
    ]
    for load in loads:
        load.start()

    def store(kind, tile):
        src, dst = ((dq_ref, dq_hbm), (dk_ref, dk_hbm), (dv_ref, dv_hbm))[kind]
        part = span(tile, TILE_Q)
        return pltpu.make_async_copy(src.at[:, part], dst.at[:, part], store_sem.at[kind, tile])

    def settle(tile, carry):
        part = span(tile, TILE_Q)
        dk_ref[:, part] = (dk_acc[:, part] * LN2).astype(BF16)
        dv_ref[:, part] = dv_acc[:, part].astype(BF16)
        store(1, tile).start()
        store(2, tile).start()
        return carry

    dk_acc[...] = jnp.zeros_like(dk_acc)
    dv_acc[...] = jnp.zeros_like(dv_acc)
    for load in loads:
        load.wait()

    def query_tile(tile, carry):
        first = shift + SEQ_MOST + tile * TILE_Q
        low, high = bounds(len_ref, first, TILE_Q)
        least, most = reach(len_ref, first, TILE_Q)
        start, tiles = key_range(least, most, shift, extent)
        q_part = span(tile, TILE_Q)
        dq_acc[...] = jnp.zeros_like(dq_acc)

        def key_tile(step, inner):
            base = pl.multiple_of((start + step * (TILE_K // LANES)) * LANES, LANES)
            k_part = pl.ds(base, TILE_K)
            key = shift + base + lax.broadcasted_iota(jnp.int32, (TILE_K, TILE_Q), 0)
            bias_ref[...] = jnp.where((key >= low) & (key < high), 0.0, HIDDEN)

            def group(index):
                heads_of = [index * 6 + sub for sub in range(6)]
                parts = [span(head, HEAD_DIM) for head in heads_of]
                bias = bias_ref[...]
                scores = [dot(ke_ref[part, k_part], qt_ref[part, q_part], TN) + bias for part in parts]
                grad_probs = [dot(ve_ref[part, k_part], gt_ref[part, q_part], TN) for part in parts]
                probs = [jnp.exp2(v - ls_ref[head, :, q_part]) for head, v in zip(heads_of, scores)]
                slopes = [
                    (p * (g - dl_ref[head, :, q_part])).astype(BF16)
                    for head, p, g in zip(heads_of, probs, grad_probs)
                ]
                for part, p, d in zip(parts, probs, slopes):
                    dv_acc[part, k_part] += dot(gt_ref[part, q_part], p.astype(BF16), NT)
                    dk_acc[part, k_part] += dot(qt_ref[part, q_part], d, NT)
                    dq_acc[part, :] += dot(ke_ref[part, k_part], d, NN)

            for index in range(heads // 6):
                group(index)
            return inner

        lax.fori_loop(0, tiles, key_tile, 0)
        dq_ref[:, q_part] = (dq_acc[...] * LN2).astype(BF16)
        store(0, tile).start()
        settle(tile, 0)
        return carry

    def drain(tile, carry):
        store(1, tile).wait()
        store(2, tile).wait()
        return carry

    lax.fori_loop(0, rows // TILE_Q, query_tile, 0)
    lax.fori_loop(rows // TILE_Q, extent // TILE_Q, settle, 0)
    for tile in range(rows // TILE_Q):
        store(0, tile).wait()
    lax.fori_loop(0, extent // TILE_Q, drain, 0)


def norm(values):
    center = values - jnp.mean(values, axis=0, keepdims=True)
    inverse = lax.rsqrt(jnp.mean(center * center, axis=0, keepdims=True) + EPSILON)
    return center * inverse, inverse


def norm_back(gradient, normed, inverse):
    centered = gradient - jnp.mean(gradient, axis=0, keepdims=True)
    return inverse * (centered - normed * jnp.mean(gradient * normed, axis=0, keepdims=True))


def gelu_parts(x):
    bell = jnp.exp2((-0.5 / LN2) * (x * x))
    t = 1.0 / (1.0 + (0.3275911 * math.sqrt(0.5)) * jnp.abs(x))
    poly = t * (0.127414796 + t * (-0.142248368 + t * (0.710706870 + t * (-0.726576013 + t * 0.530702714))))
    tail = poly * bell
    normal = jnp.where(x >= 0, 1.0 - tail, tail)
    return x * normal, normal + x * (bell * (1.0 / math.sqrt(2.0 * math.pi)))


def feed_kernel(
    xt_ref, ct_ref, cot_ref, wo_ref, w_ref,
    out_ref, gf_ref, gc_ref, dl_ref,
    normed_ref, low_ref, slope_ref, sum_ref, act_ref, pre_ref,
):
    width = xt_ref.shape[0]
    hidden = w_ref.shape[1]
    step = act_ref.shape[1]
    heads = width // HEAD_DIM
    pieces = [pl.ds(at, step) for at in range(0, hidden, step)]

    def sweep(first, second, change):
        count = len(pieces)
        pre_ref[0] = dot(w_ref[first, pieces[0], :], low_ref[...], NN)
        for at in range(count):
            if at + 1 < count:
                pre_ref[(at + 1) % 2] = dot(w_ref[first, pieces[at + 1], :], low_ref[...], NN)
            act_ref[at % 2] = change(pieces[at], pre_ref[at % 2]).astype(BF16)
            if at > 0:
                sum_ref[...] += dot(w_ref[second, pieces[at - 1], :], act_ref[(at - 1) % 2], TN)
        sum_ref[...] += dot(w_ref[second, pieces[-1], :], act_ref[(count - 1) % 2], TN)

    def forward(piece, pre):
        act, slope = gelu_parts(pre)
        slope_ref[piece, :] = slope
        return act

    attended = dot(wo_ref[...], ct_ref[...], TN)
    normed, inverse_first = norm(xt_ref[...].astype(F32) + attended)
    normed_ref[...] = normed
    low_ref[...] = normed.astype(BF16)
    sum_ref[...] = normed
    sweep(0, 1, forward)
    layer_out, inverse_second = norm(sum_ref[...])
    out_ref[...] = layer_out.T.astype(BF16)
    grad = norm_back(cot_ref[...].astype(F32).T, layer_out, inverse_second)
    sum_ref[...] = grad
    low_ref[...] = grad.astype(BF16)
    sweep(1, 0, lambda piece, upstream: slope_ref[piece, :] * upstream)
    grad_first = norm_back(sum_ref[...], normed_ref[...], inverse_first)
    gf_ref[...] = grad_first
    grad_context = dot(wo_ref[...], grad_first.astype(BF16), NN).astype(BF16)
    gc_ref[...] = grad_context
    product = grad_context.astype(F32) * ct_ref[...].astype(F32)
    for head in range(heads):
        dl_ref[head] = jnp.sum(
            product[head * HEAD_DIM : (head + 1) * HEAD_DIM], axis=0, keepdims=True
        )


def pack(rows):
    places, at = [], 0
    for size in rows:
        places.append([(at + n, n * PACK, min(PACK, size - n * PACK)) for n in range(-(-size // PACK))])
        at += len(places[-1])
    return places, at


def tail_kernel(n_head, n_seq, *refs):
    big, refs = refs[:12], refs[12:]
    vectors, refs = refs[:4], refs[4:]
    query_scale, query_bias, value_scale, value_bias = [ref[...].reshape(1, -1) for ref in vectors]
    (own_hbm, from_left, from_right, sum_ref), refs = refs[:4], refs[4:]
    held, refs = refs[:12], refs[12:]
    (
        load_sem, own_ref, mix_ref, send_left, send_right, halo_sem, z_slots, s_slots, z_sem, s_sem,
    ) = refs
    dk_ref, dv_ref, wk_ref, wve_ref, xt_ref, dq_ref, lt_ref, rt_ref, down_ref, up_ref, wqe_ref, gf_ref = held
    width, rows = dq_ref.shape
    rank = up_ref.shape[0]
    own = slice(SEQ_MOST, SEQ_MOST + rows)
    sides = (slice(0, SEQ_MOST), slice(SEQ_MOST + rows, 2 * SEQ_MOST + rows))
    pieces = [(wk_ref, big[2]), (wve_ref, big[3])]
    pieces += [(ref.at[:, side], hbm.at[:, side]) for side in sides for ref, hbm in zip(held[:2], big[:2])]
    pieces += [(dq_ref, big[5]), (xt_ref, big[4]), (down_ref, big[8]), (up_ref, big[9])]
    pieces += [(lt_ref, big[6]), (rt_ref, big[7]), (dv_ref.at[:, own], big[1].at[:, own])]
    pieces += [(dk_ref.at[:, own], big[0].at[:, own]), (wqe_ref, big[10]), (gf_ref, big[11])]
    loads = [pltpu.make_async_copy(src, dst, load_sem.at[n]) for n, (dst, src) in enumerate(pieces)]
    for load in loads[:6]:
        load.start()
    seq, head_at = lax.axis_index("seq"), lax.axis_index("head")

    barrier = pltpu.get_barrier_semaphore()
    partners = [(seq, (head_at + k) % n_head) for k in range(1, n_head)]
    partners += [((seq + k) % n_seq, head_at) for k in range(1, n_seq)]
    for partner in partners:
        pl.semaphore_signal(barrier, inc=1, device_id=partner, device_id_type=MESH)
    pl.semaphore_wait(barrier, len(partners))
    first_z, last_z = head_at == 0, head_at == n_head - 1

    def to_left(piece):
        part = span(piece, 256)
        sems = halo_sem.at[2 * piece], halo_sem.at[2 * piece + 1]
        return remote(
            send_left.at[:, part], from_right.at[:, part], *sems, seq, (head_at + n_head - 1) % n_head
        )

    def to_right(piece):
        part = span(piece, 256)
        piece += width // 256
        sems = halo_sem.at[2 * piece], halo_sem.at[2 * piece + 1]
        return remote(send_right.at[:, part], from_left.at[:, part], *sems, seq, (head_at + 1) % n_head)

    for load in loads[:6]:
        load.wait()
    for load in loads[6:]:
        load.start()
    for piece in range(width // 256):
        part = span(piece, 256)
        for side_ref, side, absent, copy in (
            (send_left, sides[0], first_z, to_left(piece)),
            (send_right, sides[1], last_z, to_right(piece)),
        ):
            partial = dot(wk_ref[part, :], dk_ref[:, side], NN) + dot(wve_ref[part, :], dv_ref[:, side], NN)
            side_ref[:, part] = partial.astype(BF16).T
            pl.when(jnp.logical_not(absent))(copy.start)

    places, depth = pack((rank, width, rank, width))
    s_slots[seq] = jnp.zeros_like(s_slots[0])
    for load in loads[6:10]:
        load.wait()

    for value in (False, True):
        scale_row, bias = (value_scale, value_bias) if value else (query_scale, query_bias)
        factor = 1.0 if value else QUERY_FOLD
        scale_at, bias_at = places[2 * value], places[2 * value + 1]

        if value:
            for load in loads[10:13]:
                load.wait()

        def outer(index, carry):
            part = span(index, 256)
            if value:
                total = dot(xt_ref[part, :], dv_ref[:, own], NT)
                total += dot(lt_ref[part, :], dv_ref[:, :SEQ_MOST], NT)
                total += dot(rt_ref[part, :], dv_ref[:, SEQ_MOST + rows :], NT)
            else:
                total = dot(xt_ref[part, :], dq_ref[...], NT)
            mix_ref[part, :] = total.astype(BF16)
            return carry

        lax.fori_loop(0, width // 256, outer, 0)
        bias_sum = jnp.zeros((1, width), F32)
        for at in range(0, rank, 256):
            part = slice(at, at + 256)
            mixed = dot(down_ref[:, part], mix_ref[...], TN) * up_ref[part, :].astype(F32) * factor
            scale = jnp.broadcast_to(scale_row[:, part], (LANES, 256)).T[:, :1]
            bias_sum += jnp.sum(mixed * scale, axis=0, keepdims=True)
            weighted = mixed * bias
            folded = weighted[:, :LANES]
            for lane in range(LANES, width, LANES):
                folded = folded + weighted[:, lane : lane + LANES]
            row, column = at // PACK, at % PACK
            s_slots[seq, pl.ds(scale_at[row][0], 1), pl.ds(column, 256)] = jnp.sum(
                folded.T, axis=0, keepdims=True
            )
        for row, start, size in bias_at:
            s_slots[seq, pl.ds(row, 1), pl.ds(0, size)] = bias_sum[:, start : start + size]

    def over_z(k):
        return remote(
            z_slots.at[head_at], z_slots.at[head_at], z_sem.at[2 * k], z_sem.at[2 * k + 1],
            seq, (head_at + k) % n_head,
        )

    def over_seq(k):
        return remote(
            s_slots.at[seq], s_slots.at[seq], s_sem.at[2 * k], s_sem.at[2 * k + 1],
            (seq + k) % n_seq, head_at,
        )

    for k in range(1, n_seq):
        over_seq(k).start()
    for load in loads[13:]:
        load.wait()

    def tokens_part(index, carry):
        part = span(index, 256)
        total = (
            gf_ref[part, :]
            + dot(wqe_ref[part, :], dq_ref[...], NN)
            + dot(wk_ref[part, :], dk_ref[:, own], NN)
            + dot(wve_ref[part, :], dv_ref[:, own], NN)
        )
        own_ref[:, part] = total.astype(BF16).T
        return carry

    lax.fori_loop(0, width // 256, tokens_part, 0)
    for k in range(1, n_seq):
        over_seq(k).wait_recv()
    total = s_slots[0]
    for k in range(1, n_seq):
        total = total + s_slots[k]
    z_slots[head_at] = total
    for k in range(1, n_head):
        over_z(k).start()

    out = pltpu.make_async_copy(own_ref, own_hbm, load_sem.at[len(pieces)])
    out.start()
    for k in range(1, n_head):
        over_z(k).wait_recv()
    total = z_slots[0]
    for k in range(1, n_head):
        total = total + z_slots[k]
    sum_ref[...] = total
    for absent, back, copy in ((first_z, to_right, to_left), (last_z, to_left, to_right)):

        @pl.when(jnp.logical_not(absent))
        def _():
            for piece in range(width // 256):
                back(piece).wait_recv()
                copy(piece).wait_send()

    out.wait()
    for k in range(1, n_head):
        over_z(k).wait_send()
    for k in range(1, n_seq):
        over_seq(k).wait_send()


def finish_kernel(n_head, own_ref, left_ref, right_ref, sum_ref, out_ref, *vector_refs):
    tile, last = pl.program_id(0), pl.num_programs(0) - 1
    to_first = (tile == 0) & (lax.axis_index("head") > 0)
    to_last = (tile == last) & (lax.axis_index("head") < n_head - 1)
    total = own_ref[...].astype(F32) + jnp.where(to_first, left_ref[...].astype(F32), 0.0)
    out_ref[...] = (total + jnp.where(to_last, right_ref[...].astype(F32), 0.0)).astype(BF16)

    @pl.when(tile == 0)
    def _():
        places, _ = pack([ref.shape[0] for ref in vector_refs])
        for vector_ref, place in zip(vector_refs, places):
            for row, start, size in place:
                vector_ref[start : start + size] = sum_ref[row, :size]


def call(kernel, outs, count, scratch=(), scalars=0):
    return pl.pallas_call(
        kernel,
        out_shape=outs,
        in_specs=[SMEM] * scalars + [VMEM] * count,
        out_specs=[VMEM] * len(outs),
        scratch_shapes=list(scratch),
        compiler_params=PARAMS,
    )


def front(n_head, n_seq, lengths, tokens, w_query, w_key, w_value, vera, shards):
    rows, width = tokens.shape
    heads = width // HEAD_DIM
    extent = rows + 2 * SEQ_MOST
    tall, wide = sds((width, rows), BF16), sds((width, extent), BF16)
    square, half = sds((width, width), BF16), sds((width, SEQ_MOST), BF16)
    kept = [tall, wide, wide, tall, half, half, square, square]
    outs = [tall, sds((heads, 1, rows), F32)] + kept
    big = (tokens, vera[0], vera[1], w_query, w_value, w_key)
    scratch = [pltpu.VMEM(a.shape, a.dtype) for a in (*big, *kept)] + [
        pltpu.VMEM((SEQ_MOST, width), BF16),
        pltpu.VMEM((SEQ_MOST, width), BF16),
        pltpu.VMEM((width, rows), F32),
        pltpu.VMEM((heads, 1, rows), F32),
        pltpu.VMEM((heads, 1, rows), F32),
        pltpu.VMEM((lengths.shape[1], rows), BF16),
        pltpu.VMEM((lengths.shape[1], extent), BF16),
        pltpu.SemaphoreType.DMA((len(big),)),
        pltpu.SemaphoreType.DMA((len(kept),)),
        pltpu.SemaphoreType.DMA((8,)),
    ]
    gather = len(shards) > 0
    specs = [VMEM] * 2 + [ANY] * len(kept)
    if gather:
        shard = shards[0].shape[0]
        outs.append(sds((2, n_head * n_seq * shard, width), BF16))
        specs.append(ANY)
        scratch += [pltpu.VMEM((2, shard, width), BF16), pltpu.SemaphoreType.DMA((182,))]
    return pl.pallas_call(
        functools.partial(front_kernel, n_head, n_seq, gather),
        out_shape=outs,
        in_specs=[ANY] * len(big) + [SMEM] + [VMEM] * (4 + len(shards)),
        out_specs=specs,
        scratch_shapes=scratch,
        compiler_params=pltpu.CompilerParams(
            vmem_limit_bytes=58 << 20, collective_id=0, has_side_effects=True
        ),
    )(*big, lengths, *vera[2:], *shards)


def feed(xt, ct, cotangent, w_output, weights):
    width, rows = xt.shape
    hidden = weights.shape[1]
    heads = width // HEAD_DIM
    tile, step = 512, 768
    column = pl.BlockSpec((width, tile), lambda i: (0, i))
    row = pl.BlockSpec((tile, width), lambda i: (i, 0))
    return pl.pallas_call(
        feed_kernel,
        grid=(rows // tile,),
        out_shape=[
            sds((rows, width), BF16), sds((width, rows), F32), sds((width, rows), BF16),
            sds((heads, 1, rows), F32),
        ],
        in_specs=[column, column, row, VMEM, VMEM],
        out_specs=[row, column, column, pl.BlockSpec((heads, 1, tile), lambda i: (0, 0, i))],
        scratch_shapes=[
            pltpu.VMEM((width, tile), F32),
            pltpu.VMEM((width, tile), BF16),
            pltpu.VMEM((hidden, tile), F32),
            pltpu.VMEM((width, tile), F32),
            pltpu.VMEM((2, step, tile), BF16),
            pltpu.VMEM((2, step, tile), F32),
        ],
        compiler_params=PARAMS,
    )(xt, ct, cotangent, w_output, weights)


def attend_back(lengths, qt, ke, ve, ls, gc, dl):
    width, rows = qt.shape
    extent = ke.shape[1]
    outs = [sds((width, rows), BF16), sds(ke.shape, BF16), sds(ke.shape, BF16)]
    return pl.pallas_call(
        attend_back_kernel,
        out_shape=outs,
        in_specs=[SMEM, ANY, ANY, ANY, VMEM, ANY, VMEM],
        out_specs=[ANY] * 3,
        scratch_shapes=[pltpu.VMEM(a.shape, BF16) for a in (qt, ke, ve, gc, *outs)]
        + [
            pltpu.VMEM((width, TILE_Q), F32),
            pltpu.VMEM((width, extent), F32),
            pltpu.VMEM((width, extent), F32),
            pltpu.VMEM((TILE_K, TILE_Q), F32),
            pltpu.SemaphoreType.DMA((4,)),
            pltpu.SemaphoreType.DMA((3, extent // TILE_Q)),
        ],
        compiler_params=PARAMS,
    )(lengths, qt, ke, ve, ls, gc, dl)


def tail(n_head, n_seq, big, small):
    dq, up = big[5], big[9]
    width, rows = dq.shape
    rank = up.shape[0]
    sizes = (rank, width, rank, width)
    depth = -(-pack(sizes)[1] // 8) * 8
    half = sds((SEQ_MOST, width), BF16)
    outs = [sds((rows, width), BF16), half, half, sds((depth, PACK), F32)]
    own, left, right, total = pl.pallas_call(
        functools.partial(tail_kernel, n_head, n_seq),
        out_shape=outs,
        in_specs=[ANY] * len(big) + [VMEM] * len(small),
        out_specs=[ANY] * 3 + [VMEM],
        scratch_shapes=[pltpu.VMEM(a.shape, a.dtype) for a in big]
        + [
            pltpu.SemaphoreType.DMA((17,)),
            pltpu.VMEM((rows, width), BF16),
            pltpu.VMEM((width, width), BF16),
            pltpu.VMEM(half.shape, BF16),
            pltpu.VMEM(half.shape, BF16),
            pltpu.SemaphoreType.DMA((4 * (width // 256),)),
            pltpu.VMEM((n_head, depth, PACK), F32),
            pltpu.VMEM((n_seq, depth, PACK), F32),
            pltpu.SemaphoreType.DMA((2 * n_head,)),
            pltpu.SemaphoreType.DMA((2 * n_seq,)),
        ],
        compiler_params=pltpu.CompilerParams(
            vmem_limit_bytes=58 << 20, collective_id=1, has_side_effects=True
        ),
    )(*big, *small)
    piece = pl.BlockSpec((SEQ_MOST, width), lambda i: (i, 0))
    return pl.pallas_call(
        functools.partial(finish_kernel, n_head),
        grid=(rows // SEQ_MOST,),
        out_shape=[sds((rows, width), BF16)] + [sds((size,), F32) for size in sizes],
        in_specs=[piece, VMEM, VMEM, VMEM],
        out_specs=[piece] + [VMEM] * 4,
        compiler_params=PARAMS,
    )(own, left, right, total)


def body(n_seq, n_head, *arrays):
    (
        tokens, lengths, cotangent, w_query, w_key, w_value, w_output, vera_down, vera_up,
        query_scale, query_bias, value_scale, value_bias, hidden_in, hidden_out,
    ) = arrays
    rows, width = tokens.shape
    vera = (vera_down, vera_up, query_scale, query_bias, value_scale, value_bias)
    fused = (n_seq, n_head) == (8, 4)
    shards = (hidden_in.T, hidden_out.T) if fused else ()
    ct, ls, qt, ke, ve, xt, lt, rt, wqe, wve, *full = front(
        n_head, n_seq, lengths, tokens, w_query, w_key, w_value, vera, shards
    )
    if fused:
        (weights,) = full
    else:
        weights = lax.all_gather(
            jnp.stack([hidden_in.T, hidden_out.T]), ("seq", "head"), axis=1, tiled=True
        )
    layer_out, gf, gc, dl = feed(xt, ct, cotangent, w_output, weights)
    dq, dk, dv = attend_back(lengths, qt, ke, ve, ls, gc, dl)
    token_grad, *totals = tail(
        n_head, n_seq, (dk, dv, w_key, wve, xt, dq, lt, rt, vera_down, vera_up, wqe, gf), vera[2:]
    )
    return (layer_out, token_grad, *totals)


def solution(mesh):
    return jax.shard_map(
        functools.partial(body, mesh.shape["seq"], mesh.shape["head"]),
        mesh=mesh,
        in_specs=(
            P(("seq", "head"), None),
            P("seq", None),
            P(("seq", "head"), None),
            P(), P(), P(), P(), P(), P(), P(), P(), P(), P(),
            P(None, ("seq", "head")),
            P(None, ("seq", "head")),
        ),
        out_specs=(P(("seq", "head"), None), P(("seq", "head"), None), P(), P(), P(), P()),
        check_vma=False,
    )
```

```python
import functools
import math

import jax
import jax.numpy as jnp
from jax import lax
from jax.experimental import pallas as pl
from jax.experimental.pallas import tpu as pltpu
from jax.sharding import PartitionSpec as P

HEAD_DIM = 64
SEQ_MOST = 512
EPSILON = 1e-05
HIDDEN = -(2.0**100)
LN2 = math.log(2.0)
QUERY_FOLD = HEAD_DIM ** (-0.5) / LN2
TILE_Q = 256
TILE_K = 256
LANES = 128
PACK = 512
NN = (((1,), (0,)), ((), ()))
NT = (((1,), (1,)), ((), ()))
TN = (((0,), (0,)), ((), ()))
F32 = jnp.float32
BF16 = jnp.bfloat16
VMEM = pl.BlockSpec(memory_space=pltpu.VMEM)
SMEM = pl.BlockSpec(memory_space=pltpu.SMEM)
MESH = pl.DeviceIdType.MESH
ANY = pl.BlockSpec(memory_space=pl.ANY)
PARAMS = pltpu.CompilerParams(vmem_limit_bytes=58 << 20)


def dot(left, right, form):
    return lax.dot_general(left, right, form, preferred_element_type=F32)


def sds(shape, dtype):
    return jax.ShapeDtypeStruct(shape, dtype)


def span(index, size):
    if isinstance(index, int):
        return pl.ds(index * size, size)
    return pl.ds(pl.multiple_of(index * size, size), size)


def bounds(len_ref, first, count):
    row = first + lax.broadcasted_iota(jnp.int32, (1, count), 1)
    low = jnp.zeros((1, count), jnp.int32)
    high = jnp.full((1, count), 1 << 30, jnp.int32)
    end = 0
    for i in range(len_ref.shape[1]):
        end = end + len_ref[0, i]
        low = jnp.where(row >= end, end, low)
        high = jnp.where(row < end, jnp.minimum(high, end), high)
    return low, high


def fill_masks(len_ref, shift, query_mask, key_mask):
    for ref, first, within, outside in ((query_mask, shift + SEQ_MOST, HIDDEN, 0.0), (key_mask, shift, 0.0, 1.0)):
        row = first + lax.broadcasted_iota(jnp.int32, (1, ref.shape[1]), 1)
        end, pieces = 0, []
        for i in range(ref.shape[0]):
            start, end = end, end + len_ref[0, i]
            pieces.append(jnp.where((row >= start) & (row < end), within, outside))
        ref[...] = jnp.concatenate(pieces, axis=0).astype(BF16)


def reach(len_ref, first, count):
    last = first + count - 1
    end, least, most = 0, 0, 1 << 30
    for i in range(len_ref.shape[1]):
        end = end + len_ref[0, i]
        least = jnp.where(first >= end, end, least)
        most = jnp.where(last < end, jnp.minimum(most, end), most)
    return least, most


def key_range(least, most, shift):
    start = (least - shift) // LANES
    return start, (most - shift - start * LANES + LANES - 1) // LANES


def other(index, bit):
    return index + bit - 2 * bit * ((index // bit) % 2)


def remote(src, dst, send, recv, seq, head):
    return pltpu.make_async_remote_copy(
        src_ref=src, dst_ref=dst, send_sem=send, recv_sem=recv, device_id=(seq, head), device_id_type=MESH
    )


class Gather:
    def __init__(self, own, full, sems, seq, head, n_head):
        self.own, self.full, self.sems = own, full, sems
        self.seq, self.head, self.n = seq, head, n_head
        self.shard = own.shape[1]
        self.near_x, self.near_y = other(seq, 2), other(seq, 4)
        self.groups = (seq, self.near_x, self.near_y, other(self.near_x, 4))

    def origin(self, way):
        return self.head - way if way < 4 else self.head + way - 3

    def there(self, way):
        return self.head >= way if way < 4 else self.head + way - 3 < self.n

    def rows(self, seq, origin):
        return self.full.at[:, span(seq * self.n + origin, self.shard), :]

    def source(self, way):
        return self.own if way == 0 else self.rows(self.seq, self.origin(way))

    def pair(self, kind, way):
        return self.sems.at[2 * (7 * kind + way)], self.sems.at[2 * (7 * kind + way) + 1]

    def local(self):
        return pltpu.make_async_copy(self.own, self.rows(self.seq, self.head), self.sems.at[0])

    def up(self, far):
        dst = self.rows(self.seq, self.head - far)
        return remote(self.source(far), dst, self.pair(8, far)[0], self.pair(0, far + 1)[1], self.seq, self.head + 1)

    def down(self, far):
        way = far + 3 if far else 0
        dst = self.rows(self.seq, self.head + far)
        return remote(self.source(way), dst, self.pair(8, far)[1], self.pair(0, far + 4)[1], self.seq, self.head - 1)

    def came_z(self, way):
        dst = self.rows(self.seq, self.origin(way))
        return remote(dst, dst, *self.pair(0, way), self.seq, self.head)

    def over_x(self, way):
        dst = self.rows(self.seq, self.origin(way))
        return remote(self.source(way), dst, *self.pair(1, way), self.near_x, self.head)

    def over_y(self, way):
        dst = self.rows(self.seq, self.origin(way))
        return remote(self.source(way), dst, *self.pair(2, way), self.near_y, self.head)

    def onward(self, way, half):
        src, to = ((self.near_x, self.near_y), (self.near_y, self.near_x))[half]
        part = self.rows(src, self.origin(way)).at[half]
        return remote(part, part, *self.pair(3 + half, way), to, self.head)

    def across(self, group, way):
        dst = self.rows(self.groups[group], self.origin(way))
        src = self.own if group == 0 and way == 0 else dst
        sems = self.sems.at[126 + 2 * (7 * group + way)], self.sems.at[127 + 2 * (7 * group + way)]
        return remote(src, dst, *sems, other(self.seq, 1), self.head)

    def slots(self, index):
        z = self.head
        return (
            ((0, None),),
            ((1, z > 0), (4, z == 0)),
            ((4, (z == 1) | (z == 2)), (5, z == 0), (2, z == 3)),
            ((6, z == 0), (5, z == 1), (2, z == 2), (3, z == 3)),
        )[index]

    def each(self, index, action):
        for way, chosen in self.slots(index):
            if chosen is None:
                action(way)
            else:
                pl.when(chosen)(functools.partial(action, way))

    def begin(self):
        pl.when(self.head < self.n - 1)(lambda: self.up(0).start())
        pl.when(self.head > 0)(lambda: self.down(0).start())
        self.local().start()
        self.spread(0)

    def take_z(self, far):
        def below():
            self.came_z(far).wait_recv()
            if far < self.n - 1:
                pl.when(self.head < self.n - 1)(lambda: self.up(far).start())

        def above():
            self.came_z(far + 3).wait_recv()
            if far < self.n - 1:
                pl.when(self.head > 0)(lambda: self.down(far).start())

        pl.when(self.there(far))(below)
        pl.when(self.there(far + 3))(above)

    def spread(self, index):
        def action(way):
            self.over_x(way).start()
            self.over_y(way).start()
            self.across(0, way).start()

        self.each(index, action)

    def take_xy(self, index):
        def action(way):
            self.over_x(way).wait_recv()
            self.onward(way, 0).start()
            self.over_y(way).wait_recv()
            self.onward(way, 1).start()
            self.across(1, way).start()
            self.across(2, way).start()

        self.each(index, action)

    def take_far(self, index):
        def action(way):
            self.onward(way, 0).wait_recv()
            self.onward(way, 1).wait_recv()
            self.across(3, way).start()

        self.each(index, action)

    def end(self):
        self.local().wait()
        for far in range(3):
            pl.when((self.head < self.n - 1) & (self.head >= far))(lambda: self.up(far).wait_send())
            pl.when((self.head > 0) & (self.head + far < self.n))(lambda: self.down(far).wait_send())
        for way in range(7):

            def action():
                self.over_x(way).wait_send()
                self.over_y(way).wait_send()
                self.onward(way, 0).wait_send()
                self.onward(way, 1).wait_send()
                for group in range(4):
                    copy = self.across(group, way)
                    copy.wait_send()
                    copy.wait_recv()

            if way == 0:
                action()
            else:
                pl.when(self.there(way))(action)


def front_kernel(n_head, n_seq, gather, *refs):
    big, refs = refs[:6], refs[6:]
    len_ref, vectors, refs = refs[0], refs[1:5], refs[5:]
    if gather:
        (hi_ref, ho_ref), refs = refs[:2], refs[2:]
    (ct_ref, ls_ref), refs = refs[:2], refs[2:]
    stored, refs = refs[:8], refs[8:]
    if gather:
        full_ref, refs = refs[0], refs[1:]
    held, refs = refs[:6], refs[6:]
    kept, refs = refs[:8], refs[8:]
    (
        xl_ref, xr_ref, acc_ref, high_ref, total_ref, query_mask, key_mask,
        load_sem, store_sem, halo_sem,
    ), refs = refs[:10], refs[10:]
    x_hbm = big[0]
    loads = [pltpu.make_async_copy(src, dst, load_sem.at[n]) for n, (src, dst) in enumerate(zip(big, held))]
    stores = [pltpu.make_async_copy(src, dst, store_sem.at[n]) for n, (src, dst) in enumerate(zip(kept, stored))]
    for n in (1, 2, 3, 4, 0, 5):
        loads[n].start()
    x_ref, down_ref, up_ref, wq_ref, wv_ref, wk_ref = held
    qt_ref, ke_ref, ve_ref, xt_ref, lt_ref, rt_ref, wqe_ref, wve_ref = kept
    rows, width = x_ref.shape
    heads = width // HEAD_DIM
    seq, head_at = lax.axis_index("seq"), lax.axis_index("head")
    shift = head_at * rows - SEQ_MOST
    first_z, last_z = head_at == 0, head_at == n_head - 1

    barrier = pltpu.get_barrier_semaphore()
    partners = [(seq, (head_at + k) % n_head) for k in range(1, n_head)]
    if gather:
        partners += [(other(seq, bit), head_at) for bit in (1, 2, 4)]
        own_ref, gather_sem = refs
        own_ref[0] = hi_ref[...]
        own_ref[1] = ho_ref[...]
    for partner in partners:
        pl.semaphore_signal(barrier, inc=1, device_id=partner, device_id_type=MESH)
    pl.semaphore_wait(barrier, len(partners))

    half = SEQ_MOST // 2

    def to_right(far):
        at = 0 if far else half
        sems = halo_sem.at[4 * far], halo_sem.at[4 * far + 1]
        src = x_hbm.at[pl.ds(rows - SEQ_MOST + at, half)]
        return remote(src, xl_ref.at[pl.ds(at, half)], *sems, seq, (head_at + 1) % n_head)

    def to_left(far):
        at = half if far else 0
        sems = halo_sem.at[4 * far + 2], halo_sem.at[4 * far + 3]
        src = x_hbm.at[pl.ds(at, half)]
        return remote(src, xr_ref.at[pl.ds(at, half)], *sems, seq, (head_at + n_head - 1) % n_head)

    def send_halo(far):
        pl.when(head_at < n_head - 1)(lambda: to_right(far).start())
        pl.when(head_at > 0)(lambda: to_left(far).start())

    if gather:
        g = Gather(own_ref, full_ref, gather_sem, seq, head_at, n_head)
        g.begin()
    else:
        send_halo(0)
        send_halo(1)
    query_scale, query_bias, value_scale, value_bias = [ref[...].reshape(1, -1) for ref in vectors]
    for n in (1, 2, 3, 4):
        loads[n].wait()

    def fold(index, carry):
        part = span(index, 256)
        down = down_ref[part, :].astype(F32)
        side_q = dot((down * query_scale).astype(BF16), up_ref[...], NN) * query_bias
        wqe_ref[part, :] = ((wq_ref[part, :].astype(F32) + side_q) * QUERY_FOLD).astype(BF16)
        side_v = dot((down * value_scale).astype(BF16), up_ref[...], NN) * value_bias
        wve_ref[part, :] = (wv_ref[part, :].astype(F32) + side_v).astype(BF16)
        return carry

    lax.fori_loop(0, width // 256, fold, 0)
    stores[6].start()
    stores[7].start()
    loads[0].wait()

    def flip(index, carry):
        part = span(index, 256)
        xt_ref[:, part] = x_ref[part, :].T
        return carry

    lax.fori_loop(0, rows // 256, flip, 0)
    stores[3].start()
    own = slice(SEQ_MOST, SEQ_MOST + rows)

    def apply(weight_ref, out_ref, at):
        def piece(index, carry):
            part = span(index, 256)
            out_ref[part, at] = dot(weight_ref[:, part], xt_ref[...], TN).astype(BF16)
            return carry

        lax.fori_loop(0, width // 256, piece, 0)

    apply(wqe_ref, qt_ref, slice(0, rows))
    if gather:
        g.take_z(1)
        g.spread(1)
    loads[5].wait()
    stores[0].start()
    apply(wk_ref, ke_ref, own)
    apply(wve_ref, ve_ref, own)

    fill_masks(len_ref, shift, query_mask, key_mask)
    acc_ref[...] = jnp.zeros_like(acc_ref)
    high_ref[...] = jnp.full_like(high_ref, HIDDEN)
    total_ref[...] = jnp.zeros_like(total_ref)

    def block(tile, key_tile):
        q_part, k_part = span(tile, TILE_Q), span(key_tile, TILE_K)
        q_mask, k_mask = query_mask[:, q_part], key_mask[:, k_part]
        parts = [span(head, HEAD_DIM) for head in range(heads)]
        before = [high_ref[head, :, q_part] for head in range(heads)]
        totals = [total_ref[head, :, q_part] for head in range(heads)]
        sums = [acc_ref[part, q_part] for part in parts]
        scores = [
            dot(
                jnp.concatenate([ke_ref[part, k_part], k_mask]),
                jnp.concatenate([qt_ref[part, q_part], q_mask]),
                TN,
            )
            for part in parts
        ]
        best = [jnp.maximum(b, jnp.max(v, axis=0, keepdims=True)) for b, v in zip(before, scores)]
        probs = [jnp.exp2(v - b) for v, b in zip(scores, best)]
        fade = [jnp.exp2(a - b) for a, b in zip(before, best)]
        totals = [t * f + jnp.sum(p, axis=0, keepdims=True) for t, f, p in zip(totals, fade, probs)]
        sums = [
            a * f + dot(ve_ref[part, k_part], p.astype(BF16), NN)
            for a, f, p, part in zip(sums, fade, probs, parts)
        ]
        for head, part, b, t, a in zip(range(heads), parts, best, totals, sums):
            high_ref[head, :, q_part] = b
            total_ref[head, :, q_part] = t
            acc_ref[part, q_part] = a

    steps = {}
    if gather:
        steps = {
            0: lambda: (g.take_xy(0),),
            2: lambda: (g.take_z(2), g.spread(2),),
            3: lambda: (send_halo(0),),
            4: lambda: (g.take_xy(1),),
            7: lambda: (g.take_z(3), g.spread(3), g.take_far(0),),
            8: lambda: (send_halo(1),),
            10: lambda: (g.take_xy(2),),
            12: lambda: (g.take_far(1),),
            15: lambda: (g.take_xy(3),),
            16: lambda: (g.take_far(2),),
            19: lambda: (g.take_far(3),),
        }

    def blocks(first, last, place):
        def one(index, carry):
            for at in steps:
                if first <= at < last:

                    @pl.when(index == at)
                    def _():
                        steps[at]()

            block(*place(index))
            return carry

        lax.fori_loop(first, last, one, 0)

    def own_place(index):
        tile = (index + 1) // 4
        return tile, (index + 1) % 4 + 1 + (tile + 1) // 2

    blocks(0, 14, own_place)

    def take_halo(far):
        for absent, copy, side_ref, flat_ref, base, at in (
            (first_z, to_right(far), xl_ref, lt_ref, 0, 0 if far else half),
            (last_z, to_left(far), xr_ref, rt_ref, SEQ_MOST + rows, half if far else 0),
        ):
            piece, place = slice(at, at + half), slice(base + at, base + at + half)

            @pl.when(absent)
            def _():
                side_ref[piece, :] = jnp.zeros((half, width), BF16)

            pl.when(jnp.logical_not(absent))(copy.wait_recv)
            flat_ref[:, piece] = side_ref[piece, :].T

            def edge(index, carry):
                part = span(index, 256)
                ke_ref[part, place] = dot(wk_ref[:, part], flat_ref[:, piece], TN).astype(BF16)
                ve_ref[part, place] = dot(wve_ref[:, part], flat_ref[:, piece], TN).astype(BF16)
                return carry

            lax.fori_loop(0, width // 256, edge, 0)

    take_halo(0)
    blocks(14, 18, lambda index: (index - 14, 1 + 5 * ((index - 14) // 2)))
    take_halo(1)
    for n in (1, 2, 4, 5):
        stores[n].start()
    blocks(18, 20, lambda index: (3 * (index - 18), 7 * (index - 18)))

    for head in range(heads):
        part = pl.ds(head * HEAD_DIM, HEAD_DIM)
        total = total_ref[head]
        ct_ref[part, :] = (acc_ref[part, :] / total).astype(BF16)
        ls_ref[head] = high_ref[head] + jnp.log2(total)

    for far in range(2):
        pl.when(head_at < n_head - 1)(to_right(far).wait_send)
        pl.when(head_at > 0)(to_left(far).wait_send)
    for store in stores:
        store.wait()
    if gather:
        g.end()


def attend_back_kernel(
    len_ref, qt_hbm, ke_hbm, ve_hbm, ls_ref, gt_hbm, dl_ref,
    dq_hbm, dk_hbm, dv_hbm,
    qt_ref, ke_ref, ve_ref, gt_ref, dq_ref, dk_ref, dv_ref,
    dq_acc, dk_acc, dv_acc, bias_ref, load_sem, store_sem,
):
    width, rows = qt_ref.shape
    extent = ke_ref.shape[1]
    heads = width // HEAD_DIM
    shift = lax.axis_index("head") * rows - SEQ_MOST
    loads = [
        pltpu.make_async_copy(src, dst, load_sem.at[n])
        for n, (src, dst) in enumerate(((ke_hbm, ke_ref), (qt_hbm, qt_ref), (ve_hbm, ve_ref), (gt_hbm, gt_ref)))
    ]
    for load in loads:
        load.start()

    def store(kind, tile):
        src, dst = ((dq_ref, dq_hbm), (dk_ref, dk_hbm), (dv_ref, dv_hbm))[kind]
        part = span(tile, TILE_Q)
        return pltpu.make_async_copy(src.at[:, part], dst.at[:, part], store_sem.at[kind, tile])

    def settle(tile, carry):
        part = span(tile, TILE_Q)
        dk_ref[:, part] = (dk_acc[:, part] * LN2).astype(BF16)
        dv_ref[:, part] = dv_acc[:, part].astype(BF16)
        store(1, tile).start()
        store(2, tile).start()
        return carry

    dk_acc[...] = jnp.zeros_like(dk_acc)
    dv_acc[...] = jnp.zeros_like(dv_acc)
    for load in loads:
        load.wait()

    def query_tile(tile, carry):
        first = shift + SEQ_MOST + tile * TILE_Q
        low, high = bounds(len_ref, first, TILE_Q)
        least, most = reach(len_ref, first, TILE_Q)
        start, count = key_range(least, most, shift)
        q_part = span(tile, TILE_Q)
        dq_acc[...] = jnp.zeros_like(dq_acc)

        def keys(column, size):
            base = pl.multiple_of(column * LANES, LANES)
            k_part = pl.ds(base, size)
            key = shift + base + lax.broadcasted_iota(jnp.int32, (size, TILE_Q), 0)
            bias_ref[:size, :] = jnp.where((key >= low) & (key < high), 0.0, HIDDEN)

            def group(index):
                heads_of = [index * 6 + sub for sub in range(6)]
                parts = [span(head, HEAD_DIM) for head in heads_of]
                bias = bias_ref[:size, :]
                scores = [dot(ke_ref[part, k_part], qt_ref[part, q_part], TN) + bias for part in parts]
                grad_probs = [dot(ve_ref[part, k_part], gt_ref[part, q_part], TN) for part in parts]
                probs = [jnp.exp2(v - ls_ref[head, :, q_part]) for head, v in zip(heads_of, scores)]
                slopes = [
                    (p * (g - dl_ref[head, :, q_part])).astype(BF16)
                    for head, p, g in zip(heads_of, probs, grad_probs)
                ]
                for part, p, d in zip(parts, probs, slopes):
                    dv_acc[part, k_part] += dot(gt_ref[part, q_part], p.astype(BF16), NT)
                    dk_acc[part, k_part] += dot(qt_ref[part, q_part], d, NT)
                    dq_acc[part, :] += dot(ke_ref[part, k_part], d, NN)

            for index in range(heads // 6):
                group(index)

        def key_tile(step, inner):
            keys(start + step * (TILE_K // LANES), TILE_K)
            return inner

        lax.fori_loop(0, count // (TILE_K // LANES), key_tile, 0)
        pl.when(count % (TILE_K // LANES) == 1)(lambda: keys(start + count - 1, LANES))
        dq_ref[:, q_part] = (dq_acc[...] * LN2).astype(BF16)
        store(0, tile).start()
        settle(tile, 0)
        return carry

    def drain(tile, carry):
        store(1, tile).wait()
        store(2, tile).wait()
        return carry

    lax.fori_loop(0, rows // TILE_Q, query_tile, 0)
    lax.fori_loop(rows // TILE_Q, extent // TILE_Q, settle, 0)
    for tile in range(rows // TILE_Q):
        store(0, tile).wait()
    lax.fori_loop(0, extent // TILE_Q, drain, 0)


def norm(values):
    center = values - jnp.mean(values, axis=0, keepdims=True)
    inverse = lax.rsqrt(jnp.mean(center * center, axis=0, keepdims=True) + EPSILON)
    return center * inverse, inverse


def norm_back(gradient, normed, inverse):
    centered = gradient - jnp.mean(gradient, axis=0, keepdims=True)
    return inverse * (centered - normed * jnp.mean(gradient * normed, axis=0, keepdims=True))


def gelu_parts(x):
    bell = jnp.exp2((-0.5 / LN2) * (x * x))
    t = 1.0 / (1.0 + (0.3275911 * math.sqrt(0.5)) * jnp.abs(x))
    poly = t * (0.127414796 + t * (-0.142248368 + t * (0.710706870 + t * (-0.726576013 + t * 0.530702714))))
    tail = poly * bell
    normal = jnp.where(x >= 0, 1.0 - tail, tail)
    return x * normal, normal + x * (bell * (1.0 / math.sqrt(2.0 * math.pi)))


def feed_kernel(
    xt_ref, ct_ref, cot_ref, wo_ref, w_ref,
    out_ref, gf_ref, gc_ref, dl_ref,
    normed_ref, low_ref, slope_ref, sum_ref, act_ref, pre_ref,
):
    width = xt_ref.shape[0]
    hidden = w_ref.shape[1]
    step = act_ref.shape[1]
    heads = width // HEAD_DIM
    pieces = [pl.ds(at, step) for at in range(0, hidden, step)]

    def sweep(first, second, change):
        count = len(pieces)
        pre_ref[0] = dot(w_ref[first, pieces[0], :], low_ref[...], NN)
        for at in range(count):
            if at + 1 < count:
                pre_ref[(at + 1) % 2] = dot(w_ref[first, pieces[at + 1], :], low_ref[...], NN)
            act_ref[at % 2] = change(pieces[at], pre_ref[at % 2]).astype(BF16)
            if at > 0:
                sum_ref[...] += dot(w_ref[second, pieces[at - 1], :], act_ref[(at - 1) % 2], TN)
        sum_ref[...] += dot(w_ref[second, pieces[-1], :], act_ref[(count - 1) % 2], TN)

    def forward(piece, pre):
        act, slope = gelu_parts(pre)
        slope_ref[piece, :] = slope
        return act

    attended = dot(wo_ref[...], ct_ref[...], TN)
    normed, inverse_first = norm(xt_ref[...].astype(F32) + attended)
    normed_ref[...] = normed
    low_ref[...] = normed.astype(BF16)
    sum_ref[...] = normed
    sweep(0, 1, forward)
    layer_out, inverse_second = norm(sum_ref[...])
    out_ref[...] = layer_out.T.astype(BF16)
    grad = norm_back(cot_ref[...].astype(F32).T, layer_out, inverse_second)
    sum_ref[...] = grad
    low_ref[...] = grad.astype(BF16)
    sweep(1, 0, lambda piece, upstream: slope_ref[piece, :] * upstream)
    grad_first = norm_back(sum_ref[...], normed_ref[...], inverse_first)
    gf_ref[...] = grad_first
    grad_context = dot(wo_ref[...], grad_first.astype(BF16), NN).astype(BF16)
    gc_ref[...] = grad_context
    product = grad_context.astype(F32) * ct_ref[...].astype(F32)
    for head in range(heads):
        dl_ref[head] = jnp.sum(
            product[head * HEAD_DIM : (head + 1) * HEAD_DIM], axis=0, keepdims=True
        )


def pack(rows):
    places, at = [], 0
    for size in rows:
        places.append([(at + n, n * PACK, min(PACK, size - n * PACK)) for n in range(-(-size // PACK))])
        at += len(places[-1])
    return places, at


def tail_kernel(n_head, n_seq, *refs):
    big, refs = refs[:12], refs[12:]
    vectors, refs = refs[:4], refs[4:]
    query_scale, query_bias, value_scale, value_bias = [ref[...].reshape(1, -1) for ref in vectors]
    (own_hbm, from_left, from_right, sum_ref), refs = refs[:4], refs[4:]
    held, refs = refs[:12], refs[12:]
    (
        load_sem, own_ref, mix_ref, send_left, send_right, halo_sem, z_slots, s_slots, z_sem, s_sem,
    ) = refs
    dk_ref, dv_ref, wk_ref, wve_ref, xt_ref, dq_ref, lt_ref, rt_ref, down_ref, up_ref, wqe_ref, gf_ref = held
    width, rows = dq_ref.shape
    rank = up_ref.shape[0]
    own = slice(SEQ_MOST, SEQ_MOST + rows)
    sides = (slice(0, SEQ_MOST), slice(SEQ_MOST + rows, 2 * SEQ_MOST + rows))
    pieces = [(wk_ref, big[2]), (wve_ref, big[3])]
    pieces += [(ref.at[:, side], hbm.at[:, side]) for side in sides for ref, hbm in zip(held[:2], big[:2])]
    pieces += [(dq_ref, big[5]), (xt_ref, big[4]), (down_ref, big[8]), (up_ref, big[9])]
    pieces += [(lt_ref, big[6]), (rt_ref, big[7]), (dv_ref.at[:, own], big[1].at[:, own])]
    pieces += [(dk_ref.at[:, own], big[0].at[:, own]), (wqe_ref, big[10]), (gf_ref, big[11])]
    loads = [pltpu.make_async_copy(src, dst, load_sem.at[n]) for n, (dst, src) in enumerate(pieces)]
    for load in loads[:6]:
        load.start()
    seq, head_at = lax.axis_index("seq"), lax.axis_index("head")

    barrier = pltpu.get_barrier_semaphore()
    partners = [(seq, (head_at + k) % n_head) for k in range(1, n_head)]
    partners += [((seq + k) % n_seq, head_at) for k in range(1, n_seq)]
    for partner in partners:
        pl.semaphore_signal(barrier, inc=1, device_id=partner, device_id_type=MESH)
    pl.semaphore_wait(barrier, len(partners))
    first_z, last_z = head_at == 0, head_at == n_head - 1

    def to_left(piece):
        part = span(piece, 256)
        sems = halo_sem.at[2 * piece], halo_sem.at[2 * piece + 1]
        return remote(
            send_left.at[:, part], from_right.at[:, part], *sems, seq, (head_at + n_head - 1) % n_head
        )

    def to_right(piece):
        part = span(piece, 256)
        piece += width // 256
        sems = halo_sem.at[2 * piece], halo_sem.at[2 * piece + 1]
        return remote(send_right.at[:, part], from_left.at[:, part], *sems, seq, (head_at + 1) % n_head)

    for load in loads[:6]:
        load.wait()
    for load in loads[6:]:
        load.start()
    for piece in range(width // 256):
        part = span(piece, 256)
        for side_ref, side, absent, copy in (
            (send_left, sides[0], first_z, to_left(piece)),
            (send_right, sides[1], last_z, to_right(piece)),
        ):
            partial = dot(wk_ref[part, :], dk_ref[:, side], NN) + dot(wve_ref[part, :], dv_ref[:, side], NN)
            side_ref[:, part] = partial.astype(BF16).T
            pl.when(jnp.logical_not(absent))(copy.start)

    places, depth = pack((rank, width, rank, width))
    s_slots[seq] = jnp.zeros_like(s_slots[0])
    for load in loads[6:10]:
        load.wait()

    for value in (False, True):
        scale_row, bias = (value_scale, value_bias) if value else (query_scale, query_bias)
        factor = 1.0 if value else QUERY_FOLD
        scale_at, bias_at = places[2 * value], places[2 * value + 1]

        if value:
            for load in loads[10:13]:
                load.wait()

        def outer(index, carry):
            part = span(index, 256)
            if value:
                total = dot(xt_ref[part, :], dv_ref[:, own], NT)
                total += dot(lt_ref[part, :], dv_ref[:, :SEQ_MOST], NT)
                total += dot(rt_ref[part, :], dv_ref[:, SEQ_MOST + rows :], NT)
            else:
                total = dot(xt_ref[part, :], dq_ref[...], NT)
            mix_ref[part, :] = total.astype(BF16)
            return carry

        lax.fori_loop(0, width // 256, outer, 0)
        bias_sum = jnp.zeros((1, width), F32)
        for at in range(0, rank, 256):
            part = slice(at, at + 256)
            mixed = dot(down_ref[:, part], mix_ref[...], TN) * up_ref[part, :].astype(F32) * factor
            scale = jnp.broadcast_to(scale_row[:, part], (LANES, 256)).T[:, :1]
            bias_sum += jnp.sum(mixed * scale, axis=0, keepdims=True)
            weighted = mixed * bias
            folded = weighted[:, :LANES]
            for lane in range(LANES, width, LANES):
                folded = folded + weighted[:, lane : lane + LANES]
            row, column = at // PACK, at % PACK
            s_slots[seq, pl.ds(scale_at[row][0], 1), pl.ds(column, 256)] = jnp.sum(
                folded.T, axis=0, keepdims=True
            )
        for row, start, size in bias_at:
            s_slots[seq, pl.ds(row, 1), pl.ds(0, size)] = bias_sum[:, start : start + size]

    def over_z(k):
        return remote(
            z_slots.at[head_at], z_slots.at[head_at], z_sem.at[2 * k], z_sem.at[2 * k + 1],
            seq, (head_at + k) % n_head,
        )

    def over_seq(k):
        return remote(
            s_slots.at[seq], s_slots.at[seq], s_sem.at[2 * k], s_sem.at[2 * k + 1],
            (seq + k) % n_seq, head_at,
        )

    for k in range(1, n_seq):
        over_seq(k).start()
    for load in loads[13:]:
        load.wait()

    def tokens_part(index, carry):
        part = span(index, 256)
        total = (
            gf_ref[part, :]
            + dot(wqe_ref[part, :], dq_ref[...], NN)
            + dot(wk_ref[part, :], dk_ref[:, own], NN)
            + dot(wve_ref[part, :], dv_ref[:, own], NN)
        )
        own_ref[:, part] = total.astype(BF16).T
        return carry

    lax.fori_loop(0, width // 256, tokens_part, 0)
    for k in range(1, n_seq):
        over_seq(k).wait_recv()
    total = s_slots[0]
    for k in range(1, n_seq):
        total = total + s_slots[k]
    z_slots[head_at] = total
    for k in range(1, n_head):
        over_z(k).start()

    out = pltpu.make_async_copy(own_ref, own_hbm, load_sem.at[len(pieces)])
    out.start()
    for k in range(1, n_head):
        over_z(k).wait_recv()
    total = z_slots[0]
    for k in range(1, n_head):
        total = total + z_slots[k]
    sum_ref[...] = total
    for absent, back, copy in ((first_z, to_right, to_left), (last_z, to_left, to_right)):

        @pl.when(jnp.logical_not(absent))
        def _():
            for piece in range(width // 256):
                back(piece).wait_recv()
                copy(piece).wait_send()

    out.wait()
    for k in range(1, n_head):
        over_z(k).wait_send()
    for k in range(1, n_seq):
        over_seq(k).wait_send()


def finish_kernel(n_head, own_ref, left_ref, right_ref, sum_ref, out_ref, *vector_refs):
    tile, last = pl.program_id(0), pl.num_programs(0) - 1
    to_first = (tile == 0) & (lax.axis_index("head") > 0)
    to_last = (tile == last) & (lax.axis_index("head") < n_head - 1)
    total = own_ref[...].astype(F32) + jnp.where(to_first, left_ref[...].astype(F32), 0.0)
    out_ref[...] = (total + jnp.where(to_last, right_ref[...].astype(F32), 0.0)).astype(BF16)

    @pl.when(tile == 0)
    def _():
        places, _ = pack([ref.shape[0] for ref in vector_refs])
        for vector_ref, place in zip(vector_refs, places):
            for row, start, size in place:
                vector_ref[start : start + size] = sum_ref[row, :size]


def call(kernel, outs, count, scratch=(), scalars=0):
    return pl.pallas_call(
        kernel,
        out_shape=outs,
        in_specs=[SMEM] * scalars + [VMEM] * count,
        out_specs=[VMEM] * len(outs),
        scratch_shapes=list(scratch),
        compiler_params=PARAMS,
    )


def front(n_head, n_seq, lengths, tokens, w_query, w_key, w_value, vera, shards):
    rows, width = tokens.shape
    heads = width // HEAD_DIM
    extent = rows + 2 * SEQ_MOST
    tall, wide = sds((width, rows), BF16), sds((width, extent), BF16)
    square, half = sds((width, width), BF16), sds((width, SEQ_MOST), BF16)
    kept = [tall, wide, wide, tall, half, half, square, square]
    outs = [tall, sds((heads, 1, rows), F32)] + kept
    big = (tokens, vera[0], vera[1], w_query, w_value, w_key)
    scratch = [pltpu.VMEM(a.shape, a.dtype) for a in (*big, *kept)] + [
        pltpu.VMEM((SEQ_MOST, width), BF16),
        pltpu.VMEM((SEQ_MOST, width), BF16),
        pltpu.VMEM((width, rows), F32),
        pltpu.VMEM((heads, 1, rows), F32),
        pltpu.VMEM((heads, 1, rows), F32),
        pltpu.VMEM((lengths.shape[1], rows), BF16),
        pltpu.VMEM((lengths.shape[1], extent), BF16),
        pltpu.SemaphoreType.DMA((len(big),)),
        pltpu.SemaphoreType.DMA((len(kept),)),
        pltpu.SemaphoreType.DMA((8,)),
    ]
    gather = len(shards) > 0
    specs = [VMEM] * 2 + [ANY] * len(kept)
    if gather:
        shard = shards[0].shape[0]
        outs.append(sds((2, n_head * n_seq * shard, width), BF16))
        specs.append(ANY)
        scratch += [pltpu.VMEM((2, shard, width), BF16), pltpu.SemaphoreType.DMA((182,))]
    return pl.pallas_call(
        functools.partial(front_kernel, n_head, n_seq, gather),
        out_shape=outs,
        in_specs=[ANY] * len(big) + [SMEM] + [VMEM] * (4 + len(shards)),
        out_specs=specs,
        scratch_shapes=scratch,
        compiler_params=pltpu.CompilerParams(
            vmem_limit_bytes=58 << 20, collective_id=0, has_side_effects=True
        ),
    )(*big, lengths, *vera[2:], *shards)


def feed(xt, ct, cotangent, w_output, weights):
    width, rows = xt.shape
    hidden = weights.shape[1]
    heads = width // HEAD_DIM
    tile, step = 512, 768
    column = pl.BlockSpec((width, tile), lambda i: (0, i))
    row = pl.BlockSpec((tile, width), lambda i: (i, 0))
    return pl.pallas_call(
        feed_kernel,
        grid=(rows // tile,),
        out_shape=[
            sds((rows, width), BF16), sds((width, rows), F32), sds((width, rows), BF16),
            sds((heads, 1, rows), F32),
        ],
        in_specs=[column, column, row, VMEM, VMEM],
        out_specs=[row, column, column, pl.BlockSpec((heads, 1, tile), lambda i: (0, 0, i))],
        scratch_shapes=[
            pltpu.VMEM((width, tile), F32),
            pltpu.VMEM((width, tile), BF16),
            pltpu.VMEM((hidden, tile), F32),
            pltpu.VMEM((width, tile), F32),
            pltpu.VMEM((2, step, tile), BF16),
            pltpu.VMEM((2, step, tile), F32),
        ],
        compiler_params=PARAMS,
    )(xt, ct, cotangent, w_output, weights)


def attend_back(lengths, qt, ke, ve, ls, gc, dl):
    width, rows = qt.shape
    extent = ke.shape[1]
    outs = [sds((width, rows), BF16), sds(ke.shape, BF16), sds(ke.shape, BF16)]
    return pl.pallas_call(
        attend_back_kernel,
        out_shape=outs,
        in_specs=[SMEM, ANY, ANY, ANY, VMEM, ANY, VMEM],
        out_specs=[ANY] * 3,
        scratch_shapes=[pltpu.VMEM(a.shape, BF16) for a in (qt, ke, ve, gc, *outs)]
        + [
            pltpu.VMEM((width, TILE_Q), F32),
            pltpu.VMEM((width, extent), F32),
            pltpu.VMEM((width, extent), F32),
            pltpu.VMEM((TILE_K, TILE_Q), F32),
            pltpu.SemaphoreType.DMA((4,)),
            pltpu.SemaphoreType.DMA((3, extent // TILE_Q)),
        ],
        compiler_params=PARAMS,
    )(lengths, qt, ke, ve, ls, gc, dl)


def tail(n_head, n_seq, big, small):
    dq, up = big[5], big[9]
    width, rows = dq.shape
    rank = up.shape[0]
    sizes = (rank, width, rank, width)
    depth = -(-pack(sizes)[1] // 8) * 8
    half = sds((SEQ_MOST, width), BF16)
    outs = [sds((rows, width), BF16), half, half, sds((depth, PACK), F32)]
    own, left, right, total = pl.pallas_call(
        functools.partial(tail_kernel, n_head, n_seq),
        out_shape=outs,
        in_specs=[ANY] * len(big) + [VMEM] * len(small),
        out_specs=[ANY] * 3 + [VMEM],
        scratch_shapes=[pltpu.VMEM(a.shape, a.dtype) for a in big]
        + [
            pltpu.SemaphoreType.DMA((17,)),
            pltpu.VMEM((rows, width), BF16),
            pltpu.VMEM((width, width), BF16),
            pltpu.VMEM(half.shape, BF16),
            pltpu.VMEM(half.shape, BF16),
            pltpu.SemaphoreType.DMA((4 * (width // 256),)),
            pltpu.VMEM((n_head, depth, PACK), F32),
            pltpu.VMEM((n_seq, depth, PACK), F32),
            pltpu.SemaphoreType.DMA((2 * n_head,)),
            pltpu.SemaphoreType.DMA((2 * n_seq,)),
        ],
        compiler_params=pltpu.CompilerParams(
            vmem_limit_bytes=58 << 20, collective_id=1, has_side_effects=True
        ),
    )(*big, *small)
    piece = pl.BlockSpec((SEQ_MOST, width), lambda i: (i, 0))
    return pl.pallas_call(
        functools.partial(finish_kernel, n_head),
        grid=(rows // SEQ_MOST,),
        out_shape=[sds((rows, width), BF16)] + [sds((size,), F32) for size in sizes],
        in_specs=[piece, VMEM, VMEM, VMEM],
        out_specs=[piece] + [VMEM] * 4,
        compiler_params=PARAMS,
    )(own, left, right, total)


def body(n_seq, n_head, *arrays):
    (
        tokens, lengths, cotangent, w_query, w_key, w_value, w_output, vera_down, vera_up,
        query_scale, query_bias, value_scale, value_bias, hidden_in, hidden_out,
    ) = arrays
    rows, width = tokens.shape
    vera = (vera_down, vera_up, query_scale, query_bias, value_scale, value_bias)
    fused = (n_seq, n_head) == (8, 4)
    shards = (hidden_in.T, hidden_out.T) if fused else ()
    ct, ls, qt, ke, ve, xt, lt, rt, wqe, wve, *full = front(
        n_head, n_seq, lengths, tokens, w_query, w_key, w_value, vera, shards
    )
    if fused:
        (weights,) = full
    else:
        weights = lax.all_gather(
            jnp.stack([hidden_in.T, hidden_out.T]), ("seq", "head"), axis=1, tiled=True
        )
    layer_out, gf, gc, dl = feed(xt, ct, cotangent, w_output, weights)
    dq, dk, dv = attend_back(lengths, qt, ke, ve, ls, gc, dl)
    token_grad, *totals = tail(
        n_head, n_seq, (dk, dv, w_key, wve, xt, dq, lt, rt, vera_down, vera_up, wqe, gf), vera[2:]
    )
    return (layer_out, token_grad, *totals)


def solution(mesh):
    return jax.shard_map(
        functools.partial(body, mesh.shape["seq"], mesh.shape["head"]),
        mesh=mesh,
        in_specs=(
            P(("seq", "head"), None),
            P("seq", None),
            P(("seq", "head"), None),
            P(), P(), P(), P(), P(), P(), P(), P(), P(), P(),
            P(None, ("seq", "head")),
            P(None, ("seq", "head")),
        ),
        out_specs=(P(("seq", "head"), None), P(("seq", "head"), None), P(), P(), P(), P()),
        check_vma=False,
    )
```

```python
import functools
import math

import jax
import jax.numpy as jnp
from jax import lax
from jax.experimental import pallas as pl
from jax.experimental.pallas import tpu as pltpu
from jax.sharding import PartitionSpec as P

HEAD_DIM = 64
SEQ_MOST = 512
EPSILON = 1e-05
HIDDEN = -(2.0**100)
LN2 = math.log(2.0)
QUERY_FOLD = HEAD_DIM ** (-0.5) / LN2
TILE_Q = 256
TILE_K = 256
LANES = 128
PACK = 512
NN = (((1,), (0,)), ((), ()))
NT = (((1,), (1,)), ((), ()))
TN = (((0,), (0,)), ((), ()))
F32 = jnp.float32
BF16 = jnp.bfloat16
VMEM = pl.BlockSpec(memory_space=pltpu.VMEM)
SMEM = pl.BlockSpec(memory_space=pltpu.SMEM)
MESH = pl.DeviceIdType.MESH
ANY = pl.BlockSpec(memory_space=pl.ANY)
PARAMS = pltpu.CompilerParams(vmem_limit_bytes=58 << 20)


def dot(left, right, form):
    return lax.dot_general(left, right, form, preferred_element_type=F32)


def sds(shape, dtype):
    return jax.ShapeDtypeStruct(shape, dtype)


def span(index, size):
    if isinstance(index, int):
        return pl.ds(index * size, size)
    return pl.ds(pl.multiple_of(index * size, size), size)


def bounds(len_ref, first, count):
    row = first + lax.broadcasted_iota(jnp.int32, (1, count), 1)
    low = jnp.zeros((1, count), jnp.int32)
    high = jnp.full((1, count), 1 << 30, jnp.int32)
    end = 0
    for i in range(len_ref.shape[1]):
        end = end + len_ref[0, i]
        low = jnp.where(row >= end, end, low)
        high = jnp.where(row < end, jnp.minimum(high, end), high)
    return low, high


def fill_masks(len_ref, shift, query_mask, key_mask):
    for ref, first, within, outside in ((query_mask, shift + SEQ_MOST, HIDDEN, 0.0), (key_mask, shift, 0.0, 1.0)):
        row = first + lax.broadcasted_iota(jnp.int32, (1, ref.shape[1]), 1)
        end, pieces = 0, []
        for i in range(ref.shape[0]):
            start, end = end, end + len_ref[0, i]
            pieces.append(jnp.where((row >= start) & (row < end), within, outside))
        ref[...] = jnp.concatenate(pieces, axis=0).astype(BF16)


def reach(len_ref, first, count):
    last = first + count - 1
    end, least, most = 0, 0, 1 << 30
    for i in range(len_ref.shape[1]):
        end = end + len_ref[0, i]
        least = jnp.where(first >= end, end, least)
        most = jnp.where(last < end, jnp.minimum(most, end), most)
    return least, most


def key_range(least, most, shift):
    start = (least - shift) // LANES
    return start, (most - shift - start * LANES + LANES - 1) // LANES


def other(index, bit):
    return index + bit - 2 * bit * ((index // bit) % 2)


def remote(src, dst, send, recv, seq, head):
    return pltpu.make_async_remote_copy(
        src_ref=src, dst_ref=dst, send_sem=send, recv_sem=recv, device_id=(seq, head), device_id_type=MESH
    )


class Gather:
    def __init__(self, own, full, sems, seq, head, n_head):
        self.own, self.full, self.sems = own, full, sems
        self.seq, self.head, self.n = seq, head, n_head
        self.shard = own.shape[1]
        self.near_x, self.near_y = other(seq, 2), other(seq, 4)
        self.groups = (seq, self.near_x, self.near_y, other(self.near_x, 4))

    def origin(self, way):
        return self.head - way if way < 4 else self.head + way - 3

    def there(self, way):
        return self.head >= way if way < 4 else self.head + way - 3 < self.n

    def rows(self, seq, origin):
        return self.full.at[:, span(seq * self.n + origin, self.shard), :]

    def source(self, way):
        return self.own if way == 0 else self.rows(self.seq, self.origin(way))

    def pair(self, kind, way):
        return self.sems.at[2 * (7 * kind + way)], self.sems.at[2 * (7 * kind + way) + 1]

    def local(self):
        return pltpu.make_async_copy(self.own, self.rows(self.seq, self.head), self.sems.at[0])

    def up(self, far):
        dst = self.rows(self.seq, self.head - far)
        return remote(self.source(far), dst, self.pair(8, far)[0], self.pair(0, far + 1)[1], self.seq, self.head + 1)

    def down(self, far):
        way = far + 3 if far else 0
        dst = self.rows(self.seq, self.head + far)
        return remote(self.source(way), dst, self.pair(8, far)[1], self.pair(0, far + 4)[1], self.seq, self.head - 1)

    def came_z(self, way):
        dst = self.rows(self.seq, self.origin(way))
        return remote(dst, dst, *self.pair(0, way), self.seq, self.head)

    def over_x(self, way):
        dst = self.rows(self.seq, self.origin(way))
        return remote(self.source(way), dst, *self.pair(1, way), self.near_x, self.head)

    def over_y(self, way):
        dst = self.rows(self.seq, self.origin(way))
        return remote(self.source(way), dst, *self.pair(2, way), self.near_y, self.head)

    def onward(self, way, half):
        src, to = ((self.near_x, self.near_y), (self.near_y, self.near_x))[half]
        part = self.rows(src, self.origin(way)).at[half]
        return remote(part, part, *self.pair(3 + half, way), to, self.head)

    def across(self, group, way):
        dst = self.rows(self.groups[group], self.origin(way))
        src = self.own if group == 0 and way == 0 else dst
        sems = self.sems.at[126 + 2 * (7 * group + way)], self.sems.at[127 + 2 * (7 * group + way)]
        return remote(src, dst, *sems, other(self.seq, 1), self.head)

    def slots(self, index):
        z = self.head
        return (
            ((0, None),),
            ((1, z > 0), (4, z == 0)),
            ((4, (z == 1) | (z == 2)), (5, z == 0), (2, z == 3)),
            ((6, z == 0), (5, z == 1), (2, z == 2), (3, z == 3)),
        )[index]

    def each(self, index, action):
        for way, chosen in self.slots(index):
            if chosen is None:
                action(way)
            else:
                pl.when(chosen)(functools.partial(action, way))

    def begin(self):
        pl.when(self.head < self.n - 1)(lambda: self.up(0).start())
        pl.when(self.head > 0)(lambda: self.down(0).start())
        self.local().start()
        self.spread(0)

    def take_z(self, far):
        def below():
            self.came_z(far).wait_recv()
            if far < self.n - 1:
                pl.when(self.head < self.n - 1)(lambda: self.up(far).start())

        def above():
            self.came_z(far + 3).wait_recv()
            if far < self.n - 1:
                pl.when(self.head > 0)(lambda: self.down(far).start())

        pl.when(self.there(far))(below)
        pl.when(self.there(far + 3))(above)

    def spread(self, index):
        def action(way):
            self.over_x(way).start()
            self.over_y(way).start()
            self.across(0, way).start()

        self.each(index, action)

    def take_xy(self, index):
        def action(way):
            self.over_x(way).wait_recv()
            self.onward(way, 0).start()
            self.over_y(way).wait_recv()
            self.onward(way, 1).start()
            self.across(1, way).start()
            self.across(2, way).start()

        self.each(index, action)

    def take_far(self, index):
        def action(way):
            self.onward(way, 0).wait_recv()
            self.onward(way, 1).wait_recv()
            self.across(3, way).start()

        self.each(index, action)

    def end(self):
        self.local().wait()
        for far in range(3):
            pl.when((self.head < self.n - 1) & (self.head >= far))(lambda: self.up(far).wait_send())
            pl.when((self.head > 0) & (self.head + far < self.n))(lambda: self.down(far).wait_send())
        for way in range(7):

            def action():
                self.over_x(way).wait_send()
                self.over_y(way).wait_send()
                self.onward(way, 0).wait_send()
                self.onward(way, 1).wait_send()
                for group in range(4):
                    copy = self.across(group, way)
                    copy.wait_send()
                    copy.wait_recv()

            if way == 0:
                action()
            else:
                pl.when(self.there(way))(action)


def front_kernel(n_head, n_seq, gather, *refs):
    big, refs = refs[:6], refs[6:]
    len_ref, vectors, refs = refs[0], refs[1:5], refs[5:]
    if gather:
        (hi_ref, ho_ref), refs = refs[:2], refs[2:]
    (ct_ref, ls_ref), refs = refs[:2], refs[2:]
    stored, refs = refs[:8], refs[8:]
    if gather:
        full_ref, refs = refs[0], refs[1:]
    held, refs = refs[:6], refs[6:]
    kept, refs = refs[:8], refs[8:]
    (
        xl_ref, xr_ref, acc_ref, high_ref, total_ref, query_mask, key_mask,
        load_sem, store_sem, halo_sem,
    ), refs = refs[:10], refs[10:]
    x_hbm = big[0]
    loads = [pltpu.make_async_copy(src, dst, load_sem.at[n]) for n, (src, dst) in enumerate(zip(big, held))]
    stores = [pltpu.make_async_copy(src, dst, store_sem.at[n]) for n, (src, dst) in enumerate(zip(kept, stored))]
    for n in (1, 2, 3, 4, 0, 5):
        loads[n].start()
    x_ref, down_ref, up_ref, wq_ref, wv_ref, wk_ref = held
    qt_ref, ke_ref, ve_ref, xt_ref, lt_ref, rt_ref, wqe_ref, wve_ref = kept
    rows, width = x_ref.shape
    heads = width // HEAD_DIM
    seq, head_at = lax.axis_index("seq"), lax.axis_index("head")
    shift = head_at * rows - SEQ_MOST
    first_z, last_z = head_at == 0, head_at == n_head - 1

    barrier = pltpu.get_barrier_semaphore()
    partners = [(seq, (head_at + k) % n_head) for k in range(1, n_head)]
    if gather:
        partners += [(other(seq, bit), head_at) for bit in (1, 2, 4)]
        own_ref, gather_sem = refs
        own_ref[0] = hi_ref[...]
        own_ref[1] = ho_ref[...]
    for partner in partners:
        pl.semaphore_signal(barrier, inc=1, device_id=partner, device_id_type=MESH)
    pl.semaphore_wait(barrier, len(partners))

    half = SEQ_MOST // 2

    def to_right(far):
        at = 0 if far else half
        sems = halo_sem.at[4 * far], halo_sem.at[4 * far + 1]
        src = x_hbm.at[pl.ds(rows - SEQ_MOST + at, half)]
        return remote(src, xl_ref.at[pl.ds(at, half)], *sems, seq, (head_at + 1) % n_head)

    def to_left(far):
        at = half if far else 0
        sems = halo_sem.at[4 * far + 2], halo_sem.at[4 * far + 3]
        src = x_hbm.at[pl.ds(at, half)]
        return remote(src, xr_ref.at[pl.ds(at, half)], *sems, seq, (head_at + n_head - 1) % n_head)

    def send_halo(far):
        pl.when(head_at < n_head - 1)(lambda: to_right(far).start())
        pl.when(head_at > 0)(lambda: to_left(far).start())

    if gather:
        g = Gather(own_ref, full_ref, gather_sem, seq, head_at, n_head)
        g.begin()
    else:
        send_halo(0)
        send_halo(1)
    query_scale, query_bias, value_scale, value_bias = [ref[...].reshape(1, -1) for ref in vectors]
    for n in (1, 2, 3, 4):
        loads[n].wait()

    def fold(index, carry):
        part = span(index, 256)
        down = down_ref[part, :].astype(F32)
        side_q = dot((down * query_scale).astype(BF16), up_ref[...], NN) * query_bias
        wqe_ref[part, :] = ((wq_ref[part, :].astype(F32) + side_q) * QUERY_FOLD).astype(BF16)
        side_v = dot((down * value_scale).astype(BF16), up_ref[...], NN) * value_bias
        wve_ref[part, :] = (wv_ref[part, :].astype(F32) + side_v).astype(BF16)
        return carry

    lax.fori_loop(0, width // 256, fold, 0)
    stores[6].start()
    stores[7].start()
    loads[0].wait()

    def flip(index, carry):
        part = span(index, 256)
        xt_ref[:, part] = x_ref[part, :].T
        return carry

    lax.fori_loop(0, rows // 256, flip, 0)
    stores[3].start()
    own = slice(SEQ_MOST, SEQ_MOST + rows)

    def apply(weight_ref, out_ref, at):
        def piece(index, carry):
            part = span(index, 256)
            out_ref[part, at] = dot(weight_ref[:, part], xt_ref[...], TN).astype(BF16)
            return carry

        lax.fori_loop(0, width // 256, piece, 0)

    apply(wqe_ref, qt_ref, slice(0, rows))
    if gather:
        g.take_z(1)
        g.spread(1)
    loads[5].wait()
    stores[0].start()
    apply(wk_ref, ke_ref, own)
    apply(wve_ref, ve_ref, own)

    fill_masks(len_ref, shift, query_mask, key_mask)
    acc_ref[...] = jnp.zeros_like(acc_ref)
    high_ref[...] = jnp.full_like(high_ref, HIDDEN)
    total_ref[...] = jnp.zeros_like(total_ref)

    def block(tile, key_tile):
        q_part, k_part = span(tile, TILE_Q), span(key_tile, TILE_K)
        q_mask, k_mask = query_mask[:, q_part], key_mask[:, k_part]
        parts = [span(head, HEAD_DIM) for head in range(heads)]
        before = [high_ref[head, :, q_part] for head in range(heads)]
        totals = [total_ref[head, :, q_part] for head in range(heads)]
        sums = [acc_ref[part, q_part] for part in parts]
        scores = [
            dot(
                jnp.concatenate([ke_ref[part, k_part], k_mask]),
                jnp.concatenate([qt_ref[part, q_part], q_mask]),
                TN,
            )
            for part in parts
        ]
        best = [jnp.maximum(b, jnp.max(v, axis=0, keepdims=True)) for b, v in zip(before, scores)]
        probs = [jnp.exp2(v - b) for v, b in zip(scores, best)]
        fade = [jnp.exp2(a - b) for a, b in zip(before, best)]
        totals = [t * f + jnp.sum(p, axis=0, keepdims=True) for t, f, p in zip(totals, fade, probs)]
        sums = [
            a * f + dot(ve_ref[part, k_part], p.astype(BF16), NN)
            for a, f, p, part in zip(sums, fade, probs, parts)
        ]
        for head, part, b, t, a in zip(range(heads), parts, best, totals, sums):
            high_ref[head, :, q_part] = b
            total_ref[head, :, q_part] = t
            acc_ref[part, q_part] = a

    steps = {}
    if gather:
        steps = {
            0: lambda: (g.take_xy(0),),
            2: lambda: (g.take_z(2), g.spread(2),),
            3: lambda: (send_halo(0),),
            4: lambda: (g.take_xy(1),),
            7: lambda: (g.take_z(3), g.spread(3), g.take_far(0),),
            8: lambda: (send_halo(1),),
            10: lambda: (g.take_xy(2),),
            12: lambda: (g.take_far(1),),
            15: lambda: (g.take_xy(3),),
            16: lambda: (g.take_far(2),),
            19: lambda: (g.take_far(3),),
        }

    def blocks(first, last, place):
        def one(index, carry):
            for at in steps:
                if first <= at < last:

                    @pl.when(index == at)
                    def _():
                        steps[at]()

            block(*place(index))
            return carry

        lax.fori_loop(first, last, one, 0)

    def own_place(index):
        tile = (index + 1) // 4
        return tile, (index + 1) % 4 + 1 + (tile + 1) // 2

    blocks(0, 14, own_place)

    def take_halo(far):
        for absent, copy, side_ref, flat_ref, base, at in (
            (first_z, to_right(far), xl_ref, lt_ref, 0, 0 if far else half),
            (last_z, to_left(far), xr_ref, rt_ref, SEQ_MOST + rows, half if far else 0),
        ):
            piece, place = slice(at, at + half), slice(base + at, base + at + half)

            @pl.when(absent)
            def _():
                side_ref[piece, :] = jnp.zeros((half, width), BF16)

            pl.when(jnp.logical_not(absent))(copy.wait_recv)
            flat_ref[:, piece] = side_ref[piece, :].T

            def edge(index, carry):
                part = span(index, 256)
                ke_ref[part, place] = dot(wk_ref[:, part], flat_ref[:, piece], TN).astype(BF16)
                ve_ref[part, place] = dot(wve_ref[:, part], flat_ref[:, piece], TN).astype(BF16)
                return carry

            lax.fori_loop(0, width // 256, edge, 0)

    take_halo(0)
    blocks(14, 18, lambda index: (index - 14, 1 + 5 * ((index - 14) // 2)))
    take_halo(1)
    for n in (1, 2, 4, 5):
        stores[n].start()
    blocks(18, 20, lambda index: (3 * (index - 18), 7 * (index - 18)))

    for head in range(heads):
        part = pl.ds(head * HEAD_DIM, HEAD_DIM)
        total = total_ref[head]
        ct_ref[part, :] = (acc_ref[part, :] / total).astype(BF16)
        ls_ref[head] = high_ref[head] + jnp.log2(total)

    for far in range(2):
        pl.when(head_at < n_head - 1)(to_right(far).wait_send)
        pl.when(head_at > 0)(to_left(far).wait_send)
    for store in stores:
        store.wait()
    if gather:
        g.end()


def attend_back_kernel(
    len_ref, qt_hbm, ke_hbm, ve_hbm, ls_ref, gt_hbm, dl_ref,
    dq_hbm, dk_hbm, dv_hbm,
    qt_ref, ke_ref, ve_ref, gt_ref, dq_ref, dk_ref, dv_ref,
    dq_acc, dk_acc, dv_acc, bias_ref, load_sem, store_sem,
):
    width, rows = qt_ref.shape
    extent = ke_ref.shape[1]
    heads = width // HEAD_DIM
    shift = lax.axis_index("head") * rows - SEQ_MOST
    loads = [
        pltpu.make_async_copy(src, dst, load_sem.at[n])
        for n, (src, dst) in enumerate(((ke_hbm, ke_ref), (qt_hbm, qt_ref), (ve_hbm, ve_ref), (gt_hbm, gt_ref)))
    ]
    for load in loads:
        load.start()

    def store(kind, tile):
        src, dst = ((dq_ref, dq_hbm), (dk_ref, dk_hbm), (dv_ref, dv_hbm))[kind]
        part = span(tile, TILE_Q)
        return pltpu.make_async_copy(src.at[:, part], dst.at[:, part], store_sem.at[kind, tile])

    def settle(tile, carry):
        part = span(tile, TILE_Q)
        dk_ref[:, part] = (dk_acc[:, part] * LN2).astype(BF16)
        dv_ref[:, part] = dv_acc[:, part].astype(BF16)
        store(1, tile).start()
        store(2, tile).start()
        return carry

    dk_acc[...] = jnp.zeros_like(dk_acc)
    dv_acc[...] = jnp.zeros_like(dv_acc)
    for load in loads:
        load.wait()

    def query_tile(tile, carry):
        first = shift + SEQ_MOST + tile * TILE_Q
        low, high = bounds(len_ref, first, TILE_Q)
        least, most = reach(len_ref, first, TILE_Q)
        start, count = key_range(least, most, shift)
        q_part = span(tile, TILE_Q)
        dq_acc[...] = jnp.zeros_like(dq_acc)

        def keys(column, size):
            base = pl.multiple_of(column * LANES, LANES)
            k_part = pl.ds(base, size)
            key = shift + base + lax.broadcasted_iota(jnp.int32, (size, TILE_Q), 0)
            bias_ref[:size, :] = jnp.where((key >= low) & (key < high), 0.0, HIDDEN)

            def group(index):
                heads_of = [index * 6 + sub for sub in range(6)]
                parts = [span(head, HEAD_DIM) for head in heads_of]
                bias = bias_ref[:size, :]
                scores = [dot(ke_ref[part, k_part], qt_ref[part, q_part], TN) + bias for part in parts]
                grad_probs = [dot(ve_ref[part, k_part], gt_ref[part, q_part], TN) for part in parts]
                probs = [jnp.exp2(v - ls_ref[head, :, q_part]) for head, v in zip(heads_of, scores)]
                slopes = [
                    (p * (g - dl_ref[head, :, q_part])).astype(BF16)
                    for head, p, g in zip(heads_of, probs, grad_probs)
                ]
                for part, p, d in zip(parts, probs, slopes):
                    dv_acc[part, k_part] += dot(gt_ref[part, q_part], p.astype(BF16), NT)
                    dk_acc[part, k_part] += dot(qt_ref[part, q_part], d, NT)
                    dq_acc[part, :] += dot(ke_ref[part, k_part], d, NN)

            if size == TILE_K:
                for index in range(heads // 6):
                    group(index)
            else:
                lax.fori_loop(0, heads // 6, lambda index, carry: group(index), None)

        def key_tile(step, inner):
            keys(start + step * (TILE_K // LANES), TILE_K)
            return inner

        lax.fori_loop(0, count // (TILE_K // LANES), key_tile, 0)
        pl.when(count % (TILE_K // LANES) == 1)(lambda: keys(start + count - 1, LANES))
        dq_ref[:, q_part] = (dq_acc[...] * LN2).astype(BF16)
        store(0, tile).start()
        settle(tile, 0)
        return carry

    def drain(tile, carry):
        store(1, tile).wait()
        store(2, tile).wait()
        return carry

    lax.fori_loop(0, rows // TILE_Q, query_tile, 0)
    lax.fori_loop(rows // TILE_Q, extent // TILE_Q, settle, 0)
    for tile in range(rows // TILE_Q):
        store(0, tile).wait()
    lax.fori_loop(0, extent // TILE_Q, drain, 0)


def norm(values):
    center = values - jnp.mean(values, axis=0, keepdims=True)
    inverse = lax.rsqrt(jnp.mean(center * center, axis=0, keepdims=True) + EPSILON)
    return center * inverse, inverse


def norm_back(gradient, normed, inverse):
    centered = gradient - jnp.mean(gradient, axis=0, keepdims=True)
    return inverse * (centered - normed * jnp.mean(gradient * normed, axis=0, keepdims=True))


def gelu_parts(x):
    bell = jnp.exp2((-0.5 / LN2) * (x * x))
    t = 1.0 / (1.0 + (0.3275911 * math.sqrt(0.5)) * jnp.abs(x))
    poly = t * (0.127414796 + t * (-0.142248368 + t * (0.710706870 + t * (-0.726576013 + t * 0.530702714))))
    tail = poly * bell
    normal = jnp.where(x >= 0, 1.0 - tail, tail)
    return x * normal, normal + x * (bell * (1.0 / math.sqrt(2.0 * math.pi)))


def feed_kernel(
    xt_ref, ct_ref, cot_ref, wo_ref, w_ref,
    out_ref, gf_ref, gc_ref, dl_ref,
    normed_ref, low_ref, slope_ref, sum_ref, act_ref, pre_ref,
):
    width = xt_ref.shape[0]
    hidden = w_ref.shape[1]
    step = act_ref.shape[1]
    heads = width // HEAD_DIM
    pieces = [pl.ds(at, step) for at in range(0, hidden, step)]

    def sweep(first, second, change):
        count = len(pieces)
        pre_ref[0] = dot(w_ref[first, pieces[0], :], low_ref[...], NN)
        for at in range(count):
            if at + 1 < count:
                pre_ref[(at + 1) % 2] = dot(w_ref[first, pieces[at + 1], :], low_ref[...], NN)
            act_ref[at % 2] = change(pieces[at], pre_ref[at % 2]).astype(BF16)
            if at > 0:
                sum_ref[...] += dot(w_ref[second, pieces[at - 1], :], act_ref[(at - 1) % 2], TN)
        sum_ref[...] += dot(w_ref[second, pieces[-1], :], act_ref[(count - 1) % 2], TN)

    def forward(piece, pre):
        act, slope = gelu_parts(pre)
        slope_ref[piece, :] = slope
        return act

    attended = dot(wo_ref[...], ct_ref[...], TN)
    normed, inverse_first = norm(xt_ref[...].astype(F32) + attended)
    normed_ref[...] = normed
    low_ref[...] = normed.astype(BF16)
    sum_ref[...] = normed
    sweep(0, 1, forward)
    layer_out, inverse_second = norm(sum_ref[...])
    out_ref[...] = layer_out.T.astype(BF16)
    grad = norm_back(cot_ref[...].astype(F32).T, layer_out, inverse_second)
    sum_ref[...] = grad
    low_ref[...] = grad.astype(BF16)
    sweep(1, 0, lambda piece, upstream: slope_ref[piece, :] * upstream)
    grad_first = norm_back(sum_ref[...], normed_ref[...], inverse_first)
    gf_ref[...] = grad_first
    grad_context = dot(wo_ref[...], grad_first.astype(BF16), NN).astype(BF16)
    gc_ref[...] = grad_context
    product = grad_context.astype(F32) * ct_ref[...].astype(F32)
    for head in range(heads):
        dl_ref[head] = jnp.sum(
            product[head * HEAD_DIM : (head + 1) * HEAD_DIM], axis=0, keepdims=True
        )


def pack(rows):
    places, at = [], 0
    for size in rows:
        places.append([(at + n, n * PACK, min(PACK, size - n * PACK)) for n in range(-(-size // PACK))])
        at += len(places[-1])
    return places, at


def tail_kernel(n_head, n_seq, *refs):
    big, refs = refs[:12], refs[12:]
    vectors, refs = refs[:4], refs[4:]
    query_scale, query_bias, value_scale, value_bias = [ref[...].reshape(1, -1) for ref in vectors]
    (own_hbm, from_left, from_right, sum_ref), refs = refs[:4], refs[4:]
    held, refs = refs[:12], refs[12:]
    (
        load_sem, own_ref, mix_ref, send_left, send_right, halo_sem, z_slots, s_slots, z_sem, s_sem,
    ) = refs
    dk_ref, dv_ref, wk_ref, wve_ref, xt_ref, dq_ref, lt_ref, rt_ref, down_ref, up_ref, wqe_ref, gf_ref = held
    width, rows = dq_ref.shape
    rank = up_ref.shape[0]
    own = slice(SEQ_MOST, SEQ_MOST + rows)
    sides = (slice(0, SEQ_MOST), slice(SEQ_MOST + rows, 2 * SEQ_MOST + rows))
    pieces = [(wk_ref, big[2]), (wve_ref, big[3])]
    pieces += [(ref.at[:, side], hbm.at[:, side]) for side in sides for ref, hbm in zip(held[:2], big[:2])]
    pieces += [(dq_ref, big[5]), (xt_ref, big[4]), (down_ref, big[8]), (up_ref, big[9])]
    pieces += [(lt_ref, big[6]), (rt_ref, big[7]), (dv_ref.at[:, own], big[1].at[:, own])]
    pieces += [(dk_ref.at[:, own], big[0].at[:, own]), (wqe_ref, big[10]), (gf_ref, big[11])]
    loads = [pltpu.make_async_copy(src, dst, load_sem.at[n]) for n, (dst, src) in enumerate(pieces)]
    for load in loads[:6]:
        load.start()
    seq, head_at = lax.axis_index("seq"), lax.axis_index("head")

    barrier = pltpu.get_barrier_semaphore()
    partners = [(seq, (head_at + k) % n_head) for k in range(1, n_head)]
    partners += [((seq + k) % n_seq, head_at) for k in range(1, n_seq)]
    for partner in partners:
        pl.semaphore_signal(barrier, inc=1, device_id=partner, device_id_type=MESH)
    pl.semaphore_wait(barrier, len(partners))
    first_z, last_z = head_at == 0, head_at == n_head - 1

    def to_left(piece):
        part = span(piece, 256)
        sems = halo_sem.at[2 * piece], halo_sem.at[2 * piece + 1]
        return remote(
            send_left.at[:, part], from_right.at[:, part], *sems, seq, (head_at + n_head - 1) % n_head
        )

    def to_right(piece):
        part = span(piece, 256)
        piece += width // 256
        sems = halo_sem.at[2 * piece], halo_sem.at[2 * piece + 1]
        return remote(send_right.at[:, part], from_left.at[:, part], *sems, seq, (head_at + 1) % n_head)

    for load in loads[:6]:
        load.wait()
    for load in loads[6:]:
        load.start()
    for piece in range(width // 256):
        part = span(piece, 256)
        for side_ref, side, absent, copy in (
            (send_left, sides[0], first_z, to_left(piece)),
            (send_right, sides[1], last_z, to_right(piece)),
        ):
            partial = dot(wk_ref[part, :], dk_ref[:, side], NN) + dot(wve_ref[part, :], dv_ref[:, side], NN)
            side_ref[:, part] = partial.astype(BF16).T
            pl.when(jnp.logical_not(absent))(copy.start)

    places, depth = pack((rank, width, rank, width))
    s_slots[seq] = jnp.zeros_like(s_slots[0])
    for load in loads[6:10]:
        load.wait()

    for value in (False, True):
        scale_row, bias = (value_scale, value_bias) if value else (query_scale, query_bias)
        factor = 1.0 if value else QUERY_FOLD
        scale_at, bias_at = places[2 * value], places[2 * value + 1]

        if value:
            for load in loads[10:13]:
                load.wait()

        def outer(index, carry):
            part = span(index, 256)
            if value:
                total = dot(xt_ref[part, :], dv_ref[:, own], NT)
                total += dot(lt_ref[part, :], dv_ref[:, :SEQ_MOST], NT)
                total += dot(rt_ref[part, :], dv_ref[:, SEQ_MOST + rows :], NT)
            else:
                total = dot(xt_ref[part, :], dq_ref[...], NT)
            mix_ref[part, :] = total.astype(BF16)
            return carry

        lax.fori_loop(0, width // 256, outer, 0)
        bias_sum = jnp.zeros((1, width), F32)
        for at in range(0, rank, 256):
            part = slice(at, at + 256)
            mixed = dot(down_ref[:, part], mix_ref[...], TN) * up_ref[part, :].astype(F32) * factor
            scale = jnp.broadcast_to(scale_row[:, part], (LANES, 256)).T[:, :1]
            bias_sum += jnp.sum(mixed * scale, axis=0, keepdims=True)
            weighted = mixed * bias
            folded = weighted[:, :LANES]
            for lane in range(LANES, width, LANES):
                folded = folded + weighted[:, lane : lane + LANES]
            row, column = at // PACK, at % PACK
            s_slots[seq, pl.ds(scale_at[row][0], 1), pl.ds(column, 256)] = jnp.sum(
                folded.T, axis=0, keepdims=True
            )
        for row, start, size in bias_at:
            s_slots[seq, pl.ds(row, 1), pl.ds(0, size)] = bias_sum[:, start : start + size]

    def over_z(k):
        return remote(
            z_slots.at[head_at], z_slots.at[head_at], z_sem.at[2 * k], z_sem.at[2 * k + 1],
            seq, (head_at + k) % n_head,
        )

    def over_seq(k):
        return remote(
            s_slots.at[seq], s_slots.at[seq], s_sem.at[2 * k], s_sem.at[2 * k + 1],
            (seq + k) % n_seq, head_at,
        )

    for k in range(1, n_seq):
        over_seq(k).start()
    for load in loads[13:]:
        load.wait()

    def tokens_part(index, carry):
        part = span(index, 256)
        total = (
            gf_ref[part, :]
            + dot(wqe_ref[part, :], dq_ref[...], NN)
            + dot(wk_ref[part, :], dk_ref[:, own], NN)
            + dot(wve_ref[part, :], dv_ref[:, own], NN)
        )
        own_ref[:, part] = total.astype(BF16).T
        return carry

    lax.fori_loop(0, width // 256, tokens_part, 0)
    for k in range(1, n_seq):
        over_seq(k).wait_recv()
    total = s_slots[0]
    for k in range(1, n_seq):
        total = total + s_slots[k]
    z_slots[head_at] = total
    for k in range(1, n_head):
        over_z(k).start()

    out = pltpu.make_async_copy(own_ref, own_hbm, load_sem.at[len(pieces)])
    out.start()
    for k in range(1, n_head):
        over_z(k).wait_recv()
    total = z_slots[0]
    for k in range(1, n_head):
        total = total + z_slots[k]
    sum_ref[...] = total
    for absent, back, copy in ((first_z, to_right, to_left), (last_z, to_left, to_right)):

        @pl.when(jnp.logical_not(absent))
        def _():
            for piece in range(width // 256):
                back(piece).wait_recv()
                copy(piece).wait_send()

    out.wait()
    for k in range(1, n_head):
        over_z(k).wait_send()
    for k in range(1, n_seq):
        over_seq(k).wait_send()


def finish_kernel(n_head, own_ref, left_ref, right_ref, sum_ref, out_ref, *vector_refs):
    tile, last = pl.program_id(0), pl.num_programs(0) - 1
    to_first = (tile == 0) & (lax.axis_index("head") > 0)
    to_last = (tile == last) & (lax.axis_index("head") < n_head - 1)
    total = own_ref[...].astype(F32) + jnp.where(to_first, left_ref[...].astype(F32), 0.0)
    out_ref[...] = (total + jnp.where(to_last, right_ref[...].astype(F32), 0.0)).astype(BF16)

    @pl.when(tile == 0)
    def _():
        places, _ = pack([ref.shape[0] for ref in vector_refs])
        for vector_ref, place in zip(vector_refs, places):
            for row, start, size in place:
                vector_ref[start : start + size] = sum_ref[row, :size]


def call(kernel, outs, count, scratch=(), scalars=0):
    return pl.pallas_call(
        kernel,
        out_shape=outs,
        in_specs=[SMEM] * scalars + [VMEM] * count,
        out_specs=[VMEM] * len(outs),
        scratch_shapes=list(scratch),
        compiler_params=PARAMS,
    )


def front(n_head, n_seq, lengths, tokens, w_query, w_key, w_value, vera, shards):
    rows, width = tokens.shape
    heads = width // HEAD_DIM
    extent = rows + 2 * SEQ_MOST
    tall, wide = sds((width, rows), BF16), sds((width, extent), BF16)
    square, half = sds((width, width), BF16), sds((width, SEQ_MOST), BF16)
    kept = [tall, wide, wide, tall, half, half, square, square]
    outs = [tall, sds((heads, 1, rows), F32)] + kept
    big = (tokens, vera[0], vera[1], w_query, w_value, w_key)
    scratch = [pltpu.VMEM(a.shape, a.dtype) for a in (*big, *kept)] + [
        pltpu.VMEM((SEQ_MOST, width), BF16),
        pltpu.VMEM((SEQ_MOST, width), BF16),
        pltpu.VMEM((width, rows), F32),
        pltpu.VMEM((heads, 1, rows), F32),
        pltpu.VMEM((heads, 1, rows), F32),
        pltpu.VMEM((lengths.shape[1], rows), BF16),
        pltpu.VMEM((lengths.shape[1], extent), BF16),
        pltpu.SemaphoreType.DMA((len(big),)),
        pltpu.SemaphoreType.DMA((len(kept),)),
        pltpu.SemaphoreType.DMA((8,)),
    ]
    gather = len(shards) > 0
    specs = [VMEM] * 2 + [ANY] * len(kept)
    if gather:
        shard = shards[0].shape[0]
        outs.append(sds((2, n_head * n_seq * shard, width), BF16))
        specs.append(ANY)
        scratch += [pltpu.VMEM((2, shard, width), BF16), pltpu.SemaphoreType.DMA((182,))]
    return pl.pallas_call(
        functools.partial(front_kernel, n_head, n_seq, gather),
        out_shape=outs,
        in_specs=[ANY] * len(big) + [SMEM] + [VMEM] * (4 + len(shards)),
        out_specs=specs,
        scratch_shapes=scratch,
        compiler_params=pltpu.CompilerParams(
            vmem_limit_bytes=58 << 20, collective_id=0, has_side_effects=True
        ),
    )(*big, lengths, *vera[2:], *shards)


def feed(xt, ct, cotangent, w_output, weights):
    width, rows = xt.shape
    hidden = weights.shape[1]
    heads = width // HEAD_DIM
    tile, step = 512, 768
    column = pl.BlockSpec((width, tile), lambda i: (0, i))
    row = pl.BlockSpec((tile, width), lambda i: (i, 0))
    return pl.pallas_call(
        feed_kernel,
        grid=(rows // tile,),
        out_shape=[
            sds((rows, width), BF16), sds((width, rows), F32), sds((width, rows), BF16),
            sds((heads, 1, rows), F32),
        ],
        in_specs=[column, column, row, VMEM, VMEM],
        out_specs=[row, column, column, pl.BlockSpec((heads, 1, tile), lambda i: (0, 0, i))],
        scratch_shapes=[
            pltpu.VMEM((width, tile), F32),
            pltpu.VMEM((width, tile), BF16),
            pltpu.VMEM((hidden, tile), F32),
            pltpu.VMEM((width, tile), F32),
            pltpu.VMEM((2, step, tile), BF16),
            pltpu.VMEM((2, step, tile), F32),
        ],
        compiler_params=PARAMS,
    )(xt, ct, cotangent, w_output, weights)


def attend_back(lengths, qt, ke, ve, ls, gc, dl):
    width, rows = qt.shape
    extent = ke.shape[1]
    outs = [sds((width, rows), BF16), sds(ke.shape, BF16), sds(ke.shape, BF16)]
    return pl.pallas_call(
        attend_back_kernel,
        out_shape=outs,
        in_specs=[SMEM, ANY, ANY, ANY, VMEM, ANY, VMEM],
        out_specs=[ANY] * 3,
        scratch_shapes=[pltpu.VMEM(a.shape, BF16) for a in (qt, ke, ve, gc, *outs)]
        + [
            pltpu.VMEM((width, TILE_Q), F32),
            pltpu.VMEM((width, extent), F32),
            pltpu.VMEM((width, extent), F32),
            pltpu.VMEM((TILE_K, TILE_Q), F32),
            pltpu.SemaphoreType.DMA((4,)),
            pltpu.SemaphoreType.DMA((3, extent // TILE_Q)),
        ],
        compiler_params=PARAMS,
    )(lengths, qt, ke, ve, ls, gc, dl)


def tail(n_head, n_seq, big, small):
    dq, up = big[5], big[9]
    width, rows = dq.shape
    rank = up.shape[0]
    sizes = (rank, width, rank, width)
    depth = -(-pack(sizes)[1] // 8) * 8
    half = sds((SEQ_MOST, width), BF16)
    outs = [sds((rows, width), BF16), half, half, sds((depth, PACK), F32)]
    own, left, right, total = pl.pallas_call(
        functools.partial(tail_kernel, n_head, n_seq),
        out_shape=outs,
        in_specs=[ANY] * len(big) + [VMEM] * len(small),
        out_specs=[ANY] * 3 + [VMEM],
        scratch_shapes=[pltpu.VMEM(a.shape, a.dtype) for a in big]
        + [
            pltpu.SemaphoreType.DMA((17,)),
            pltpu.VMEM((rows, width), BF16),
            pltpu.VMEM((width, width), BF16),
            pltpu.VMEM(half.shape, BF16),
            pltpu.VMEM(half.shape, BF16),
            pltpu.SemaphoreType.DMA((4 * (width // 256),)),
            pltpu.VMEM((n_head, depth, PACK), F32),
            pltpu.VMEM((n_seq, depth, PACK), F32),
            pltpu.SemaphoreType.DMA((2 * n_head,)),
            pltpu.SemaphoreType.DMA((2 * n_seq,)),
        ],
        compiler_params=pltpu.CompilerParams(
            vmem_limit_bytes=58 << 20, collective_id=1, has_side_effects=True
        ),
    )(*big, *small)
    piece = pl.BlockSpec((SEQ_MOST, width), lambda i: (i, 0))
    return pl.pallas_call(
        functools.partial(finish_kernel, n_head),
        grid=(rows // SEQ_MOST,),
        out_shape=[sds((rows, width), BF16)] + [sds((size,), F32) for size in sizes],
        in_specs=[piece, VMEM, VMEM, VMEM],
        out_specs=[piece] + [VMEM] * 4,
        compiler_params=PARAMS,
    )(own, left, right, total)


def body(n_seq, n_head, *arrays):
    (
        tokens, lengths, cotangent, w_query, w_key, w_value, w_output, vera_down, vera_up,
        query_scale, query_bias, value_scale, value_bias, hidden_in, hidden_out,
    ) = arrays
    rows, width = tokens.shape
    vera = (vera_down, vera_up, query_scale, query_bias, value_scale, value_bias)
    fused = (n_seq, n_head) == (8, 4)
    shards = (hidden_in.T, hidden_out.T) if fused else ()
    ct, ls, qt, ke, ve, xt, lt, rt, wqe, wve, *full = front(
        n_head, n_seq, lengths, tokens, w_query, w_key, w_value, vera, shards
    )
    if fused:
        (weights,) = full
    else:
        weights = lax.all_gather(
            jnp.stack([hidden_in.T, hidden_out.T]), ("seq", "head"), axis=1, tiled=True
        )
    layer_out, gf, gc, dl = feed(xt, ct, cotangent, w_output, weights)
    dq, dk, dv = attend_back(lengths, qt, ke, ve, ls, gc, dl)
    token_grad, *totals = tail(
        n_head, n_seq, (dk, dv, w_key, wve, xt, dq, lt, rt, vera_down, vera_up, wqe, gf), vera[2:]
    )
    return (layer_out, token_grad, *totals)


def solution(mesh):
    return jax.shard_map(
        functools.partial(body, mesh.shape["seq"], mesh.shape["head"]),
        mesh=mesh,
        in_specs=(
            P(("seq", "head"), None),
            P("seq", None),
            P(("seq", "head"), None),
            P(), P(), P(), P(), P(), P(), P(), P(), P(), P(),
            P(None, ("seq", "head")),
            P(None, ("seq", "head")),
        ),
        out_specs=(P(("seq", "head"), None), P(("seq", "head"), None), P(), P(), P(), P()),
        check_vma=False,
    )
```

```python
import functools
import math

import jax
import jax.numpy as jnp
from jax import lax
from jax.experimental import pallas as pl
from jax.experimental.pallas import tpu as pltpu
from jax.sharding import PartitionSpec as P

HEAD_DIM = 64
SEQ_MOST = 512
EPSILON = 1e-05
HIDDEN = -(2.0**100)
LN2 = math.log(2.0)
QUERY_FOLD = HEAD_DIM ** (-0.5) / LN2
TILE_Q = 256
TILE_K = 256
LANES = 128
PACK = 512
NN = (((1,), (0,)), ((), ()))
NT = (((1,), (1,)), ((), ()))
TN = (((0,), (0,)), ((), ()))
F32 = jnp.float32
BF16 = jnp.bfloat16
VMEM = pl.BlockSpec(memory_space=pltpu.VMEM)
SMEM = pl.BlockSpec(memory_space=pltpu.SMEM)
MESH = pl.DeviceIdType.MESH
ANY = pl.BlockSpec(memory_space=pl.ANY)
PARAMS = pltpu.CompilerParams(vmem_limit_bytes=58 << 20)


def dot(left, right, form):
    return lax.dot_general(left, right, form, preferred_element_type=F32)


def sds(shape, dtype):
    return jax.ShapeDtypeStruct(shape, dtype)


def span(index, size):
    if isinstance(index, int):
        return pl.ds(index * size, size)
    return pl.ds(pl.multiple_of(index * size, size), size)


def bounds(len_ref, first, count):
    row = first + lax.broadcasted_iota(jnp.int32, (1, count), 1)
    low = jnp.zeros((1, count), jnp.int32)
    high = jnp.full((1, count), 1 << 30, jnp.int32)
    end = 0
    for i in range(len_ref.shape[1]):
        end = end + len_ref[0, i]
        low = jnp.where(row >= end, end, low)
        high = jnp.where(row < end, jnp.minimum(high, end), high)
    return low, high


def fill_masks(len_ref, shift, query_mask, key_mask):
    for ref, first, within, outside in ((query_mask, shift + SEQ_MOST, HIDDEN, 0.0), (key_mask, shift, 0.0, 1.0)):
        row = first + lax.broadcasted_iota(jnp.int32, (1, ref.shape[1]), 1)
        end, pieces = 0, []
        for i in range(ref.shape[0]):
            start, end = end, end + len_ref[0, i]
            pieces.append(jnp.where((row >= start) & (row < end), within, outside))
        ref[...] = jnp.concatenate(pieces, axis=0).astype(BF16)


def reach(len_ref, first, count):
    last = first + count - 1
    end, least, most = 0, 0, 1 << 30
    for i in range(len_ref.shape[1]):
        end = end + len_ref[0, i]
        least = jnp.where(first >= end, end, least)
        most = jnp.where(last < end, jnp.minimum(most, end), most)
    return least, most


def key_range(least, most, shift):
    start = (least - shift) // LANES
    return start, (most - shift - start * LANES + LANES - 1) // LANES


def other(index, bit):
    return index + bit - 2 * bit * ((index // bit) % 2)


def remote(src, dst, send, recv, seq, head):
    return pltpu.make_async_remote_copy(
        src_ref=src, dst_ref=dst, send_sem=send, recv_sem=recv, device_id=(seq, head), device_id_type=MESH
    )


class Gather:
    def __init__(self, own, full, sems, seq, head, n_head):
        self.own, self.full, self.sems = own, full, sems
        self.seq, self.head, self.n = seq, head, n_head
        self.shard = own.shape[1]
        self.near_x, self.near_y = other(seq, 2), other(seq, 4)
        self.groups = (seq, self.near_x, self.near_y, other(self.near_x, 4))

    def origin(self, way):
        return self.head - way if way < 4 else self.head + way - 3

    def there(self, way):
        return self.head >= way if way < 4 else self.head + way - 3 < self.n

    def rows(self, seq, origin):
        return self.full.at[:, span(seq * self.n + origin, self.shard), :]

    def source(self, way):
        return self.own if way == 0 else self.rows(self.seq, self.origin(way))

    def pair(self, kind, way):
        return self.sems.at[2 * (7 * kind + way)], self.sems.at[2 * (7 * kind + way) + 1]

    def local(self):
        return pltpu.make_async_copy(self.own, self.rows(self.seq, self.head), self.sems.at[0])

    def up(self, far):
        dst = self.rows(self.seq, self.head - far)
        return remote(self.source(far), dst, self.pair(8, far)[0], self.pair(0, far + 1)[1], self.seq, self.head + 1)

    def down(self, far):
        way = far + 3 if far else 0
        dst = self.rows(self.seq, self.head + far)
        return remote(self.source(way), dst, self.pair(8, far)[1], self.pair(0, far + 4)[1], self.seq, self.head - 1)

    def came_z(self, way):
        dst = self.rows(self.seq, self.origin(way))
        return remote(dst, dst, *self.pair(0, way), self.seq, self.head)

    def over_x(self, way):
        dst = self.rows(self.seq, self.origin(way))
        return remote(self.source(way), dst, *self.pair(1, way), self.near_x, self.head)

    def over_y(self, way):
        dst = self.rows(self.seq, self.origin(way))
        return remote(self.source(way), dst, *self.pair(2, way), self.near_y, self.head)

    def onward(self, way, half):
        src, to = ((self.near_x, self.near_y), (self.near_y, self.near_x))[half]
        part = self.rows(src, self.origin(way)).at[half]
        return remote(part, part, *self.pair(3 + half, way), to, self.head)

    def across(self, group, way):
        dst = self.rows(self.groups[group], self.origin(way))
        src = self.own if group == 0 and way == 0 else dst
        sems = self.sems.at[126 + 2 * (7 * group + way)], self.sems.at[127 + 2 * (7 * group + way)]
        return remote(src, dst, *sems, other(self.seq, 1), self.head)

    def slots(self, index):
        z = self.head
        return (
            ((0, None),),
            ((1, z > 0), (4, z == 0)),
            ((4, (z == 1) | (z == 2)), (5, z == 0), (2, z == 3)),
            ((6, z == 0), (5, z == 1), (2, z == 2), (3, z == 3)),
        )[index]

    def each(self, index, action):
        for way, chosen in self.slots(index):
            if chosen is None:
                action(way)
            else:
                pl.when(chosen)(functools.partial(action, way))

    def begin(self):
        pl.when(self.head < self.n - 1)(lambda: self.up(0).start())
        pl.when(self.head > 0)(lambda: self.down(0).start())
        self.local().start()
        self.spread(0)

    def take_z(self, far):
        def below():
            self.came_z(far).wait_recv()
            if far < self.n - 1:
                pl.when(self.head < self.n - 1)(lambda: self.up(far).start())

        def above():
            self.came_z(far + 3).wait_recv()
            if far < self.n - 1:
                pl.when(self.head > 0)(lambda: self.down(far).start())

        pl.when(self.there(far))(below)
        pl.when(self.there(far + 3))(above)

    def spread(self, index):
        def action(way):
            self.over_x(way).start()
            self.over_y(way).start()
            self.across(0, way).start()

        self.each(index, action)

    def take_xy(self, index):
        def action(way):
            self.over_x(way).wait_recv()
            self.onward(way, 0).start()
            self.over_y(way).wait_recv()
            self.onward(way, 1).start()
            self.across(1, way).start()
            self.across(2, way).start()

        self.each(index, action)

    def take_far(self, index):
        def action(way):
            self.onward(way, 0).wait_recv()
            self.onward(way, 1).wait_recv()
            self.across(3, way).start()

        self.each(index, action)

    def end(self):
        self.local().wait()
        for far in range(3):
            pl.when((self.head < self.n - 1) & (self.head >= far))(lambda: self.up(far).wait_send())
            pl.when((self.head > 0) & (self.head + far < self.n))(lambda: self.down(far).wait_send())
        for way in range(7):

            def action():
                self.over_x(way).wait_send()
                self.over_y(way).wait_send()
                self.onward(way, 0).wait_send()
                self.onward(way, 1).wait_send()
                for group in range(4):
                    copy = self.across(group, way)
                    copy.wait_send()
                    copy.wait_recv()

            if way == 0:
                action()
            else:
                pl.when(self.there(way))(action)


def front_kernel(n_head, n_seq, gather, *refs):
    big, refs = refs[:6], refs[6:]
    len_ref, vectors, refs = refs[0], refs[1:5], refs[5:]
    if gather:
        (hi_ref, ho_ref), refs = refs[:2], refs[2:]
    (ct_ref, ls_ref), refs = refs[:2], refs[2:]
    stored, refs = refs[:8], refs[8:]
    if gather:
        full_ref, refs = refs[0], refs[1:]
    held, refs = refs[:6], refs[6:]
    kept, refs = refs[:8], refs[8:]
    (
        xl_ref, xr_ref, acc_ref, high_ref, total_ref, query_mask, key_mask,
        load_sem, store_sem, halo_sem,
    ), refs = refs[:10], refs[10:]
    x_hbm = big[0]
    loads = [pltpu.make_async_copy(src, dst, load_sem.at[n]) for n, (src, dst) in enumerate(zip(big, held))]
    stores = [pltpu.make_async_copy(src, dst, store_sem.at[n]) for n, (src, dst) in enumerate(zip(kept, stored))]
    for n in (1, 2, 3, 4, 0, 5):
        loads[n].start()
    x_ref, down_ref, up_ref, wq_ref, wv_ref, wk_ref = held
    qt_ref, ke_ref, ve_ref, xt_ref, lt_ref, rt_ref, wqe_ref, wve_ref = kept
    rows, width = x_ref.shape
    heads = width // HEAD_DIM
    seq, head_at = lax.axis_index("seq"), lax.axis_index("head")
    shift = head_at * rows - SEQ_MOST
    first_z, last_z = head_at == 0, head_at == n_head - 1

    barrier = pltpu.get_barrier_semaphore()
    partners = [(seq, (head_at + k) % n_head) for k in range(1, n_head)]
    if gather:
        partners += [(other(seq, bit), head_at) for bit in (1, 2, 4)]
        own_ref, gather_sem = refs
        own_ref[0] = hi_ref[...]
        own_ref[1] = ho_ref[...]
    for partner in partners:
        pl.semaphore_signal(barrier, inc=1, device_id=partner, device_id_type=MESH)
    pl.semaphore_wait(barrier, len(partners))

    half = SEQ_MOST // 2

    def to_right(far):
        at = 0 if far else half
        sems = halo_sem.at[4 * far], halo_sem.at[4 * far + 1]
        src = x_hbm.at[pl.ds(rows - SEQ_MOST + at, half)]
        return remote(src, xl_ref.at[pl.ds(at, half)], *sems, seq, (head_at + 1) % n_head)

    def to_left(far):
        at = half if far else 0
        sems = halo_sem.at[4 * far + 2], halo_sem.at[4 * far + 3]
        src = x_hbm.at[pl.ds(at, half)]
        return remote(src, xr_ref.at[pl.ds(at, half)], *sems, seq, (head_at + n_head - 1) % n_head)

    def send_halo(far):
        pl.when(head_at < n_head - 1)(lambda: to_right(far).start())
        pl.when(head_at > 0)(lambda: to_left(far).start())

    if gather:
        g = Gather(own_ref, full_ref, gather_sem, seq, head_at, n_head)
        g.begin()
    else:
        send_halo(0)
        send_halo(1)
    query_scale, query_bias, value_scale, value_bias = [ref[...].reshape(1, -1) for ref in vectors]
    for n in (1, 2, 3, 4):
        loads[n].wait()

    def fold(index, carry):
        part = span(index, 256)
        down = down_ref[part, :].astype(F32)
        side_q = dot((down * query_scale).astype(BF16), up_ref[...], NN) * query_bias
        wqe_ref[part, :] = ((wq_ref[part, :].astype(F32) + side_q) * QUERY_FOLD).astype(BF16)
        side_v = dot((down * value_scale).astype(BF16), up_ref[...], NN) * value_bias
        wve_ref[part, :] = (wv_ref[part, :].astype(F32) + side_v).astype(BF16)
        return carry

    lax.fori_loop(0, width // 256, fold, 0)
    stores[6].start()
    stores[7].start()
    loads[0].wait()

    def flip(index, carry):
        part = span(index, 256)
        xt_ref[:, part] = x_ref[part, :].T
        return carry

    lax.fori_loop(0, rows // 256, flip, 0)
    stores[3].start()
    own = slice(SEQ_MOST, SEQ_MOST + rows)

    def apply(weight_ref, out_ref, at):
        def piece(index, carry):
            part = span(index, 256)
            out_ref[part, at] = dot(weight_ref[:, part], xt_ref[...], TN).astype(BF16)
            return carry

        lax.fori_loop(0, width // 256, piece, 0)

    apply(wqe_ref, qt_ref, slice(0, rows))
    if gather:
        g.take_z(1)
        g.spread(1)
    loads[5].wait()
    stores[0].start()
    apply(wk_ref, ke_ref, own)
    apply(wve_ref, ve_ref, own)

    fill_masks(len_ref, shift, query_mask, key_mask)
    acc_ref[...] = jnp.zeros_like(acc_ref)
    high_ref[...] = jnp.full_like(high_ref, HIDDEN)
    total_ref[...] = jnp.zeros_like(total_ref)

    def block(tile, key_tile):
        q_part, k_part = span(tile, TILE_Q), span(key_tile, TILE_K)
        q_mask, k_mask = query_mask[:, q_part], key_mask[:, k_part]
        parts = [span(head, HEAD_DIM) for head in range(heads)]
        before = [high_ref[head, :, q_part] for head in range(heads)]
        totals = [total_ref[head, :, q_part] for head in range(heads)]
        sums = [acc_ref[part, q_part] for part in parts]
        scores = [
            dot(
                jnp.concatenate([ke_ref[part, k_part], k_mask]),
                jnp.concatenate([qt_ref[part, q_part], q_mask]),
                TN,
            )
            for part in parts
        ]
        best = [jnp.maximum(b, jnp.max(v, axis=0, keepdims=True)) for b, v in zip(before, scores)]
        probs = [jnp.exp2(v - b) for v, b in zip(scores, best)]
        fade = [jnp.exp2(a - b) for a, b in zip(before, best)]
        totals = [t * f + jnp.sum(p, axis=0, keepdims=True) for t, f, p in zip(totals, fade, probs)]
        sums = [
            a * f + dot(ve_ref[part, k_part], p.astype(BF16), NN)
            for a, f, p, part in zip(sums, fade, probs, parts)
        ]
        for head, part, b, t, a in zip(range(heads), parts, best, totals, sums):
            high_ref[head, :, q_part] = b
            total_ref[head, :, q_part] = t
            acc_ref[part, q_part] = a

    steps = {}
    if gather:
        steps = {
            0: lambda: (g.take_xy(0),),
            2: lambda: (g.take_z(2), g.spread(2),),
            3: lambda: (send_halo(0),),
            4: lambda: (g.take_xy(1),),
            7: lambda: (g.take_z(3), g.spread(3), g.take_far(0),),
            8: lambda: (send_halo(1),),
            10: lambda: (g.take_xy(2),),
            12: lambda: (g.take_far(1),),
            15: lambda: (g.take_xy(3),),
            16: lambda: (g.take_far(2),),
            19: lambda: (g.take_far(3),),
        }

    def blocks(first, last, place):
        def one(index, carry):
            for at in steps:
                if first <= at < last:

                    @pl.when(index == at)
                    def _():
                        steps[at]()

            block(*place(index))
            return carry

        lax.fori_loop(first, last, one, 0)

    def own_place(index):
        tile = (index + 1) // 4
        return tile, (index + 1) % 4 + 1 + (tile + 1) // 2

    blocks(0, 14, own_place)

    def take_halo(far):
        for absent, copy, side_ref, flat_ref, base, at in (
            (first_z, to_right(far), xl_ref, lt_ref, 0, 0 if far else half),
            (last_z, to_left(far), xr_ref, rt_ref, SEQ_MOST + rows, half if far else 0),
        ):
            piece, place = slice(at, at + half), slice(base + at, base + at + half)

            @pl.when(absent)
            def _():
                side_ref[piece, :] = jnp.zeros((half, width), BF16)

            pl.when(jnp.logical_not(absent))(copy.wait_recv)
            flat_ref[:, piece] = side_ref[piece, :].T

            def edge(index, carry):
                part = span(index, 256)
                ke_ref[part, place] = dot(wk_ref[:, part], flat_ref[:, piece], TN).astype(BF16)
                ve_ref[part, place] = dot(wve_ref[:, part], flat_ref[:, piece], TN).astype(BF16)
                return carry

            lax.fori_loop(0, width // 256, edge, 0)

    take_halo(0)
    blocks(14, 18, lambda index: (index - 14, 1 + 5 * ((index - 14) // 2)))
    take_halo(1)
    for n in (1, 2, 4, 5):
        stores[n].start()
    blocks(18, 20, lambda index: (3 * (index - 18), 7 * (index - 18)))

    for head in range(heads):
        part = pl.ds(head * HEAD_DIM, HEAD_DIM)
        total = total_ref[head]
        ct_ref[part, :] = (acc_ref[part, :] / total).astype(BF16)
        ls_ref[head] = high_ref[head] + jnp.log2(total)

    for far in range(2):
        pl.when(head_at < n_head - 1)(to_right(far).wait_send)
        pl.when(head_at > 0)(to_left(far).wait_send)
    for store in stores:
        store.wait()
    if gather:
        g.end()


def attend_back_kernel(
    len_ref, qt_hbm, ke_hbm, ve_hbm, ls_ref, gt_hbm, dl_ref,
    dq_hbm, dk_hbm, dv_hbm,
    qt_ref, ke_ref, ve_ref, gt_ref, dq_ref, dk_ref, dv_ref,
    dq_acc, dk_acc, dv_acc, bias_ref, load_sem, store_sem,
):
    width, rows = qt_ref.shape
    extent = ke_ref.shape[1]
    heads = width // HEAD_DIM
    shift = lax.axis_index("head") * rows - SEQ_MOST
    loads = [
        pltpu.make_async_copy(src, dst, load_sem.at[n])
        for n, (src, dst) in enumerate(((ke_hbm, ke_ref), (qt_hbm, qt_ref), (ve_hbm, ve_ref), (gt_hbm, gt_ref)))
    ]
    for load in loads:
        load.start()

    def store(kind, tile):
        src, dst = ((dq_ref, dq_hbm), (dk_ref, dk_hbm), (dv_ref, dv_hbm))[kind]
        part = span(tile, TILE_Q)
        return pltpu.make_async_copy(src.at[:, part], dst.at[:, part], store_sem.at[kind, tile])

    def settle(tile, carry):
        part = span(tile, TILE_Q)
        dk_ref[:, part] = (dk_acc[:, part] * LN2).astype(BF16)
        dv_ref[:, part] = dv_acc[:, part].astype(BF16)
        store(1, tile).start()
        store(2, tile).start()
        return carry

    dk_acc[...] = jnp.zeros_like(dk_acc)
    dv_acc[...] = jnp.zeros_like(dv_acc)
    for load in loads:
        load.wait()

    def query_tile(tile, carry):
        first = shift + SEQ_MOST + tile * TILE_Q
        low, high = bounds(len_ref, first, TILE_Q)
        least, most = reach(len_ref, first, TILE_Q)
        start, count = key_range(least, most, shift)
        q_part = span(tile, TILE_Q)
        dq_acc[...] = jnp.zeros_like(dq_acc)

        def keys(column, size):
            base = pl.multiple_of(column * LANES, LANES)
            k_part = pl.ds(base, size)
            key = shift + base + lax.broadcasted_iota(jnp.int32, (size, TILE_Q), 0)
            bias_ref[:size, :] = jnp.where((key >= low) & (key < high), 0.0, HIDDEN)

            def group(index):
                heads_of = [index * 6 + sub for sub in range(6)]
                parts = [span(head, HEAD_DIM) for head in heads_of]
                bias = bias_ref[:size, :]
                scores = [dot(ke_ref[part, k_part], qt_ref[part, q_part], TN) + bias for part in parts]
                grad_probs = [dot(ve_ref[part, k_part], gt_ref[part, q_part], TN) for part in parts]
                probs = [jnp.exp2(v - ls_ref[head, :, q_part]) for head, v in zip(heads_of, scores)]
                slopes = [
                    (p * (g - dl_ref[head, :, q_part])).astype(BF16)
                    for head, p, g in zip(heads_of, probs, grad_probs)
                ]
                for part, p, d in zip(parts, probs, slopes):
                    dv_acc[part, k_part] += dot(gt_ref[part, q_part], p.astype(BF16), NT)
                    dk_acc[part, k_part] += dot(qt_ref[part, q_part], d, NT)
                    dq_acc[part, :] += dot(ke_ref[part, k_part], d, NN)

            if size == TILE_K:
                for index in range(heads // 6):
                    group(index)
            else:
                lax.fori_loop(0, heads // 6, lambda index, carry: group(index), None)

        def key_tile(step, inner):
            keys(start + step * (TILE_K // LANES), TILE_K)
            return inner

        lax.fori_loop(0, count // (TILE_K // LANES), key_tile, 0)
        pl.when(count % (TILE_K // LANES) == 1)(lambda: keys(start + count - 1, LANES))
        dq_ref[:, q_part] = (dq_acc[...] * LN2).astype(BF16)
        store(0, tile).start()
        settle(tile, 0)
        return carry

    def drain(tile, carry):
        store(1, tile).wait()
        store(2, tile).wait()
        return carry

    lax.fori_loop(0, rows // TILE_Q, query_tile, 0)
    lax.fori_loop(rows // TILE_Q, extent // TILE_Q, settle, 0)
    for tile in range(rows // TILE_Q):
        store(0, tile).wait()
    lax.fori_loop(0, extent // TILE_Q, drain, 0)


def norm(values):
    center = values - jnp.mean(values, axis=0, keepdims=True)
    inverse = lax.rsqrt(jnp.mean(center * center, axis=0, keepdims=True) + EPSILON)
    return center * inverse, inverse


def norm_back(gradient, normed, inverse):
    centered = gradient - jnp.mean(gradient, axis=0, keepdims=True)
    return inverse * (centered - normed * jnp.mean(gradient * normed, axis=0, keepdims=True))


def gelu_parts(x):
    bell = jnp.exp2((-0.5 / LN2) * (x * x))
    t = 1.0 / (1.0 + (0.3275911 * math.sqrt(0.5)) * jnp.abs(x))
    poly = t * (0.127414796 + t * (-0.142248368 + t * (0.710706870 + t * (-0.726576013 + t * 0.530702714))))
    tail = poly * bell
    normal = jnp.where(x >= 0, 1.0 - tail, tail)
    return x * normal, normal + x * (bell * (1.0 / math.sqrt(2.0 * math.pi)))


def feed_kernel(
    xt_ref, ct_ref, cot_ref, wo_ref, w_ref,
    out_ref, gf_ref, gc_ref, dl_ref,
    normed_ref, low_ref, slope_ref, sum_ref, act_ref, pre_ref,
):
    width = xt_ref.shape[0]
    hidden = w_ref.shape[1]
    step = act_ref.shape[1]
    heads = width // HEAD_DIM
    pieces = [pl.ds(at, step) for at in range(0, hidden, step)]

    def sweep(first, second, change):
        count = len(pieces)
        pre_ref[0] = dot(w_ref[first, pieces[0], :], low_ref[...], NN)
        for at in range(count):
            if at + 1 < count:
                pre_ref[(at + 1) % 2] = dot(w_ref[first, pieces[at + 1], :], low_ref[...], NN)
            act_ref[at % 2] = change(pieces[at], pre_ref[at % 2]).astype(BF16)
            if at > 0:
                sum_ref[...] += dot(w_ref[second, pieces[at - 1], :], act_ref[(at - 1) % 2], TN)
        sum_ref[...] += dot(w_ref[second, pieces[-1], :], act_ref[(count - 1) % 2], TN)

    def forward(piece, pre):
        act, slope = gelu_parts(pre)
        slope_ref[piece, :] = slope
        return act

    attended = dot(wo_ref[...], ct_ref[...], TN)
    normed, inverse_first = norm(xt_ref[...].astype(F32) + attended)
    normed_ref[...] = normed
    low_ref[...] = normed.astype(BF16)
    sum_ref[...] = normed
    sweep(0, 1, forward)
    layer_out, inverse_second = norm(sum_ref[...])
    out_ref[...] = layer_out.astype(BF16).T
    grad = norm_back(cot_ref[...].T.astype(F32), layer_out, inverse_second)
    sum_ref[...] = grad
    low_ref[...] = grad.astype(BF16)
    sweep(1, 0, lambda piece, upstream: slope_ref[piece, :] * upstream)
    grad_first = norm_back(sum_ref[...], normed_ref[...], inverse_first)
    gf_ref[...] = grad_first
    grad_context = dot(wo_ref[...], grad_first.astype(BF16), NN).astype(BF16)
    gc_ref[...] = grad_context
    product = grad_context.astype(F32) * ct_ref[...].astype(F32)
    for head in range(heads):
        dl_ref[head] = jnp.sum(
            product[head * HEAD_DIM : (head + 1) * HEAD_DIM], axis=0, keepdims=True
        )


def pack(rows):
    places, at = [], 0
    for size in rows:
        places.append([(at + n, n * PACK, min(PACK, size - n * PACK)) for n in range(-(-size // PACK))])
        at += len(places[-1])
    return places, at


def tail_kernel(n_head, n_seq, *refs):
    big, refs = refs[:12], refs[12:]
    vectors, refs = refs[:4], refs[4:]
    query_scale, query_bias, value_scale, value_bias = [ref[...].reshape(1, -1) for ref in vectors]
    (own_hbm, from_left, from_right, sum_ref), refs = refs[:4], refs[4:]
    held, refs = refs[:12], refs[12:]
    (
        load_sem, own_ref, mix_ref, send_left, send_right, halo_sem, z_slots, s_slots, z_sem, s_sem,
    ) = refs
    dk_ref, dv_ref, wk_ref, wve_ref, xt_ref, dq_ref, lt_ref, rt_ref, down_ref, up_ref, wqe_ref, gf_ref = held
    width, rows = dq_ref.shape
    rank = up_ref.shape[0]
    own = slice(SEQ_MOST, SEQ_MOST + rows)
    sides = (slice(0, SEQ_MOST), slice(SEQ_MOST + rows, 2 * SEQ_MOST + rows))
    pieces = [(wk_ref, big[2]), (wve_ref, big[3])]
    pieces += [(ref.at[:, side], hbm.at[:, side]) for side in sides for ref, hbm in zip(held[:2], big[:2])]
    pieces += [(dq_ref, big[5]), (xt_ref, big[4]), (down_ref, big[8]), (up_ref, big[9])]
    pieces += [(lt_ref, big[6]), (rt_ref, big[7]), (dv_ref.at[:, own], big[1].at[:, own])]
    pieces += [(dk_ref.at[:, own], big[0].at[:, own]), (wqe_ref, big[10]), (gf_ref, big[11])]
    loads = [pltpu.make_async_copy(src, dst, load_sem.at[n]) for n, (dst, src) in enumerate(pieces)]
    for load in loads[:6]:
        load.start()
    seq, head_at = lax.axis_index("seq"), lax.axis_index("head")

    barrier = pltpu.get_barrier_semaphore()
    partners = [(seq, (head_at + k) % n_head) for k in range(1, n_head)]
    partners += [((seq + k) % n_seq, head_at) for k in range(1, n_seq)]
    for partner in partners:
        pl.semaphore_signal(barrier, inc=1, device_id=partner, device_id_type=MESH)
    pl.semaphore_wait(barrier, len(partners))
    first_z, last_z = head_at == 0, head_at == n_head - 1

    def to_left(piece):
        part = span(piece, 256)
        sems = halo_sem.at[2 * piece], halo_sem.at[2 * piece + 1]
        return remote(
            send_left.at[:, part], from_right.at[:, part], *sems, seq, (head_at + n_head - 1) % n_head
        )

    def to_right(piece):
        part = span(piece, 256)
        piece += width // 256
        sems = halo_sem.at[2 * piece], halo_sem.at[2 * piece + 1]
        return remote(send_right.at[:, part], from_left.at[:, part], *sems, seq, (head_at + 1) % n_head)

    for load in loads[:6]:
        load.wait()
    for load in loads[6:]:
        load.start()
    for piece in range(width // 256):
        part = span(piece, 256)
        for side_ref, side, absent, copy in (
            (send_left, sides[0], first_z, to_left(piece)),
            (send_right, sides[1], last_z, to_right(piece)),
        ):
            partial = dot(wk_ref[part, :], dk_ref[:, side], NN) + dot(wve_ref[part, :], dv_ref[:, side], NN)
            side_ref[:, part] = partial.astype(BF16).T
            pl.when(jnp.logical_not(absent))(copy.start)

    places, depth = pack((rank, width, rank, width))
    s_slots[seq] = jnp.zeros_like(s_slots[0])
    for load in loads[6:10]:
        load.wait()

    for value in (False, True):
        scale_row, bias = (value_scale, value_bias) if value else (query_scale, query_bias)
        factor = 1.0 if value else QUERY_FOLD
        scale_at, bias_at = places[2 * value], places[2 * value + 1]

        if value:
            for load in loads[10:13]:
                load.wait()

        def outer(index, carry):
            part = span(index, 256)
            if value:
                total = dot(xt_ref[part, :], dv_ref[:, own], NT)
                total += dot(lt_ref[part, :], dv_ref[:, :SEQ_MOST], NT)
                total += dot(rt_ref[part, :], dv_ref[:, SEQ_MOST + rows :], NT)
            else:
                total = dot(xt_ref[part, :], dq_ref[...], NT)
            mix_ref[part, :] = total.astype(BF16)
            return carry

        lax.fori_loop(0, width // 256, outer, 0)
        bias_sum = jnp.zeros((1, width), F32)
        for at in range(0, rank, 256):
            part = slice(at, at + 256)
            mixed = dot(down_ref[:, part], mix_ref[...], TN) * up_ref[part, :].astype(F32) * factor
            scale = jnp.broadcast_to(scale_row[:, part], (LANES, 256)).T[:, :1]
            bias_sum += jnp.sum(mixed * scale, axis=0, keepdims=True)
            weighted = mixed * bias
            folded = weighted[:, :LANES]
            for lane in range(LANES, width, LANES):
                folded = folded + weighted[:, lane : lane + LANES]
            row, column = at // PACK, at % PACK
            s_slots[seq, pl.ds(scale_at[row][0], 1), pl.ds(column, 256)] = jnp.sum(
                folded.T, axis=0, keepdims=True
            )
        for row, start, size in bias_at:
            s_slots[seq, pl.ds(row, 1), pl.ds(0, size)] = bias_sum[:, start : start + size]

    def over_z(k):
        return remote(
            z_slots.at[head_at], z_slots.at[head_at], z_sem.at[2 * k], z_sem.at[2 * k + 1],
            seq, (head_at + k) % n_head,
        )

    def over_seq(k):
        return remote(
            s_slots.at[seq], s_slots.at[seq], s_sem.at[2 * k], s_sem.at[2 * k + 1],
            (seq + k) % n_seq, head_at,
        )

    for k in range(1, n_seq):
        over_seq(k).start()
    for load in loads[13:]:
        load.wait()

    def tokens_part(index, carry):
        part = span(index, 256)
        total = (
            gf_ref[part, :]
            + dot(wqe_ref[part, :], dq_ref[...], NN)
            + dot(wk_ref[part, :], dk_ref[:, own], NN)
            + dot(wve_ref[part, :], dv_ref[:, own], NN)
        )
        own_ref[:, part] = total.astype(BF16).T
        return carry

    lax.fori_loop(0, width // 256, tokens_part, 0)
    for k in range(1, n_seq):
        over_seq(k).wait_recv()
    total = s_slots[0]
    for k in range(1, n_seq):
        total = total + s_slots[k]
    z_slots[head_at] = total
    for k in range(1, n_head):
        over_z(k).start()

    out = pltpu.make_async_copy(own_ref, own_hbm, load_sem.at[len(pieces)])
    out.start()
    for k in range(1, n_head):
        over_z(k).wait_recv()
    total = z_slots[0]
    for k in range(1, n_head):
        total = total + z_slots[k]
    sum_ref[...] = total
    for absent, back, copy in ((first_z, to_right, to_left), (last_z, to_left, to_right)):

        @pl.when(jnp.logical_not(absent))
        def _():
            for piece in range(width // 256):
                back(piece).wait_recv()
                copy(piece).wait_send()

    out.wait()
    for k in range(1, n_head):
        over_z(k).wait_send()
    for k in range(1, n_seq):
        over_seq(k).wait_send()


def finish_kernel(n_head, own_ref, left_ref, right_ref, sum_ref, out_ref, *vector_refs):
    tile, last = pl.program_id(0), pl.num_programs(0) - 1
    to_first = (tile == 0) & (lax.axis_index("head") > 0)
    to_last = (tile == last) & (lax.axis_index("head") < n_head - 1)
    total = own_ref[...].astype(F32) + jnp.where(to_first, left_ref[...].astype(F32), 0.0)
    out_ref[...] = (total + jnp.where(to_last, right_ref[...].astype(F32), 0.0)).astype(BF16)

    @pl.when(tile == 0)
    def _():
        places, _ = pack([ref.shape[0] for ref in vector_refs])
        for vector_ref, place in zip(vector_refs, places):
            for row, start, size in place:
                vector_ref[start : start + size] = sum_ref[row, :size]


def call(kernel, outs, count, scratch=(), scalars=0):
    return pl.pallas_call(
        kernel,
        out_shape=outs,
        in_specs=[SMEM] * scalars + [VMEM] * count,
        out_specs=[VMEM] * len(outs),
        scratch_shapes=list(scratch),
        compiler_params=PARAMS,
    )


def front(n_head, n_seq, lengths, tokens, w_query, w_key, w_value, vera, shards):
    rows, width = tokens.shape
    heads = width // HEAD_DIM
    extent = rows + 2 * SEQ_MOST
    tall, wide = sds((width, rows), BF16), sds((width, extent), BF16)
    square, half = sds((width, width), BF16), sds((width, SEQ_MOST), BF16)
    kept = [tall, wide, wide, tall, half, half, square, square]
    outs = [tall, sds((heads, 1, rows), F32)] + kept
    big = (tokens, vera[0], vera[1], w_query, w_value, w_key)
    scratch = [pltpu.VMEM(a.shape, a.dtype) for a in (*big, *kept)] + [
        pltpu.VMEM((SEQ_MOST, width), BF16),
        pltpu.VMEM((SEQ_MOST, width), BF16),
        pltpu.VMEM((width, rows), F32),
        pltpu.VMEM((heads, 1, rows), F32),
        pltpu.VMEM((heads, 1, rows), F32),
        pltpu.VMEM((lengths.shape[1], rows), BF16),
        pltpu.VMEM((lengths.shape[1], extent), BF16),
        pltpu.SemaphoreType.DMA((len(big),)),
        pltpu.SemaphoreType.DMA((len(kept),)),
        pltpu.SemaphoreType.DMA((8,)),
    ]
    gather = len(shards) > 0
    specs = [VMEM] * 2 + [ANY] * len(kept)
    if gather:
        shard = shards[0].shape[0]
        outs.append(sds((2, n_head * n_seq * shard, width), BF16))
        specs.append(ANY)
        scratch += [pltpu.VMEM((2, shard, width), BF16), pltpu.SemaphoreType.DMA((182,))]
    return pl.pallas_call(
        functools.partial(front_kernel, n_head, n_seq, gather),
        out_shape=outs,
        in_specs=[ANY] * len(big) + [SMEM] + [VMEM] * (4 + len(shards)),
        out_specs=specs,
        scratch_shapes=scratch,
        compiler_params=pltpu.CompilerParams(
            vmem_limit_bytes=58 << 20, collective_id=0, has_side_effects=True
        ),
    )(*big, lengths, *vera[2:], *shards)


def feed(xt, ct, cotangent, w_output, weights):
    width, rows = xt.shape
    hidden = weights.shape[1]
    heads = width // HEAD_DIM
    tile, step = 512, 768
    column = pl.BlockSpec((width, tile), lambda i: (0, i))
    row = pl.BlockSpec((tile, width), lambda i: (i, 0))
    return pl.pallas_call(
        feed_kernel,
        grid=(rows // tile,),
        out_shape=[
            sds((rows, width), BF16), sds((width, rows), F32), sds((width, rows), BF16),
            sds((heads, 1, rows), F32),
        ],
        in_specs=[column, column, row, VMEM, VMEM],
        out_specs=[row, column, column, pl.BlockSpec((heads, 1, tile), lambda i: (0, 0, i))],
        scratch_shapes=[
            pltpu.VMEM((width, tile), F32),
            pltpu.VMEM((width, tile), BF16),
            pltpu.VMEM((hidden, tile), F32),
            pltpu.VMEM((width, tile), F32),
            pltpu.VMEM((2, step, tile), BF16),
            pltpu.VMEM((2, step, tile), F32),
        ],
        compiler_params=PARAMS,
    )(xt, ct, cotangent, w_output, weights)


def attend_back(lengths, qt, ke, ve, ls, gc, dl):
    width, rows = qt.shape
    extent = ke.shape[1]
    outs = [sds((width, rows), BF16), sds(ke.shape, BF16), sds(ke.shape, BF16)]
    return pl.pallas_call(
        attend_back_kernel,
        out_shape=outs,
        in_specs=[SMEM, ANY, ANY, ANY, VMEM, ANY, VMEM],
        out_specs=[ANY] * 3,
        scratch_shapes=[pltpu.VMEM(a.shape, BF16) for a in (qt, ke, ve, gc, *outs)]
        + [
            pltpu.VMEM((width, TILE_Q), F32),
            pltpu.VMEM((width, extent), F32),
            pltpu.VMEM((width, extent), F32),
            pltpu.VMEM((TILE_K, TILE_Q), F32),
            pltpu.SemaphoreType.DMA((4,)),
            pltpu.SemaphoreType.DMA((3, extent // TILE_Q)),
        ],
        compiler_params=PARAMS,
    )(lengths, qt, ke, ve, ls, gc, dl)


def tail(n_head, n_seq, big, small):
    dq, up = big[5], big[9]
    width, rows = dq.shape
    rank = up.shape[0]
    sizes = (rank, width, rank, width)
    depth = -(-pack(sizes)[1] // 8) * 8
    half = sds((SEQ_MOST, width), BF16)
    outs = [sds((rows, width), BF16), half, half, sds((depth, PACK), F32)]
    own, left, right, total = pl.pallas_call(
        functools.partial(tail_kernel, n_head, n_seq),
        out_shape=outs,
        in_specs=[ANY] * len(big) + [VMEM] * len(small),
        out_specs=[ANY] * 3 + [VMEM],
        scratch_shapes=[pltpu.VMEM(a.shape, a.dtype) for a in big]
        + [
            pltpu.SemaphoreType.DMA((17,)),
            pltpu.VMEM((rows, width), BF16),
            pltpu.VMEM((width, width), BF16),
            pltpu.VMEM(half.shape, BF16),
            pltpu.VMEM(half.shape, BF16),
            pltpu.SemaphoreType.DMA((4 * (width // 256),)),
            pltpu.VMEM((n_head, depth, PACK), F32),
            pltpu.VMEM((n_seq, depth, PACK), F32),
            pltpu.SemaphoreType.DMA((2 * n_head,)),
            pltpu.SemaphoreType.DMA((2 * n_seq,)),
        ],
        compiler_params=pltpu.CompilerParams(
            vmem_limit_bytes=58 << 20, collective_id=1, has_side_effects=True
        ),
    )(*big, *small)
    piece = pl.BlockSpec((SEQ_MOST, width), lambda i: (i, 0))
    return pl.pallas_call(
        functools.partial(finish_kernel, n_head),
        grid=(rows // SEQ_MOST,),
        out_shape=[sds((rows, width), BF16)] + [sds((size,), F32) for size in sizes],
        in_specs=[piece, VMEM, VMEM, VMEM],
        out_specs=[piece] + [VMEM] * 4,
        compiler_params=PARAMS,
    )(own, left, right, total)


def body(n_seq, n_head, *arrays):
    (
        tokens, lengths, cotangent, w_query, w_key, w_value, w_output, vera_down, vera_up,
        query_scale, query_bias, value_scale, value_bias, hidden_in, hidden_out,
    ) = arrays
    rows, width = tokens.shape
    vera = (vera_down, vera_up, query_scale, query_bias, value_scale, value_bias)
    fused = (n_seq, n_head) == (8, 4)
    shards = (hidden_in.T, hidden_out.T) if fused else ()
    ct, ls, qt, ke, ve, xt, lt, rt, wqe, wve, *full = front(
        n_head, n_seq, lengths, tokens, w_query, w_key, w_value, vera, shards
    )
    if fused:
        (weights,) = full
    else:
        weights = lax.all_gather(
            jnp.stack([hidden_in.T, hidden_out.T]), ("seq", "head"), axis=1, tiled=True
        )
    layer_out, gf, gc, dl = feed(xt, ct, cotangent, w_output, weights)
    dq, dk, dv = attend_back(lengths, qt, ke, ve, ls, gc, dl)
    token_grad, *totals = tail(
        n_head, n_seq, (dk, dv, w_key, wve, xt, dq, lt, rt, vera_down, vera_up, wqe, gf), vera[2:]
    )
    return (layer_out, token_grad, *totals)


def solution(mesh):
    return jax.shard_map(
        functools.partial(body, mesh.shape["seq"], mesh.shape["head"]),
        mesh=mesh,
        in_specs=(
            P(("seq", "head"), None),
            P("seq", None),
            P(("seq", "head"), None),
            P(), P(), P(), P(), P(), P(), P(), P(), P(), P(),
            P(None, ("seq", "head")),
            P(None, ("seq", "head")),
        ),
        out_specs=(P(("seq", "head"), None), P(("seq", "head"), None), P(), P(), P(), P()),
        check_vma=False,
    )
```
